32 devices in a mesh: seq: 4 (over y, x), ctx: 8 (over z, core).
Axes of the slice: x: 2, y: 2, z: 4, core: 2. Of those that a mesh axis runs over, the one named last changes fastest.
Arguments:
- queries: bfloat16 [4096, 2048], P(('seq', 'ctx')), parts along dimension 0, may hold values from -1 to 1
- keys_in: bfloat16 [4096, 2048], P(('seq', 'ctx')), parts along dimension 0, may hold values from -1 to 1
- value_input: bfloat16 [4096, 2048], P(('seq', 'ctx')), parts along dimension 0, may hold values from -1 to 1
- level_gain: float32 [11, 16, 4096], P(None, None, ('seq', 'ctx')), parts along dimension 2, may hold values from 0.2 to 2
- decay_log: float32 [16, 4096], P(None, ('seq', 'ctx')), parts along dimension 1, may hold values from -0.7 to 0, as said below
- out_grad: bfloat16 [4096, 2048], P(('seq', 'ctx')), parts along dimension 0, may hold values from -1 to 1
Outputs:
- mixed_out: bfloat16 [4096, 2048], P(('seq', 'ctx')), parts along dimension 0
- query_gradient: bfloat16 [4096, 2048], P(('seq', 'ctx')), parts along dimension 0
- grad_keys: bfloat16 [4096, 2048], P(('seq', 'ctx')), parts along dimension 0
- grad_values: bfloat16 [4096, 2048], P(('seq', 'ctx')), parts along dimension 0
- grad_gain: float32 [11, 16, 4096], P(None, None, ('seq', 'ctx')), parts along dimension 2
- grad_decay: float32 [16, 4096], P(None, ('seq', 'ctx')), parts along dimension 1
The draws below stay inside these ranges and needn't reach their ends.
There are 4 independent parts, one for each index of `seq`. The reference program is written for one: setup_inputs(seed, part) draws one part's arguments, and reference() takes and returns one part's arrays. A program takes and returns all parts, laid end to end along the dimension named above; each array names one. Nothing has to cross between parts.
Inputs may be any that keep to these rules, and one draw needn't show every extreme that they name: `decay_log`: every entry is negative.
All inputs are finite; a program needn't handle non-finite values.
Results may differ from the reference program's by a relative error of at most 0.001.
Values sent between devices are 32-bit elements; how exact they have to be, the bound alone decides.
No kernel may reach another device: no remote copies, remote signals or barrier semaphores. Data moves between devices by JAX's collectives and lax.ppermute only.
A program may use at most 128 MiB of HBM per device.

```python
import math
import jax
import jax.numpy as jnp
from jax import lax

H = 16
HEAD = 128
TOK_DEV = 128
LEN = 1024
XLEV = 3
LEVELS = 11
N_CTX = 8


def draw_decay_log(key, part):
    pieces = jax.random.split(key, 8)
    log_high = jnp.log(jnp.float32(1.0 / 30.0))
    log_low = jnp.log(jnp.float32(0.01 / LEN))
    order = jax.random.permutation(pieces[0], H).astype(jnp.float32)
    place = (order + jax.random.uniform(pieces[1], (H,), jnp.float32)) / H
    rate = jnp.exp(log_low + place * (log_high - log_low))
    blocks = LEN // TOK_DEV
    block_factor = jnp.repeat(jax.random.uniform(pieces[3], (H, blocks), jnp.float32, 0.5, 1.5), TOK_DEV, axis=1)
    token_factor = jax.random.uniform(pieces[4], (H, LEN), jnp.float32, 0.5, 1.5)
    base = -rate[:, None] * block_factor * token_factor
    first_spot = jax.random.randint(pieces[5], (H,), 0, LEN)
    second_location = (first_spot + 1 + jax.random.randint(pieces[6], (H,), 0, LEN - 1)) % LEN
    loss_share = jax.random.uniform(pieces[7], (H, 2), jnp.float32, 0.2, 0.5)
    places = jnp.arange(LEN)
    first_hit = places[None, :] == first_spot[:, None]
    second_hit = places[None, :] == second_location[:, None]
    with_first = jnp.where(first_hit, jnp.log1p(-loss_share[:, 0])[:, None], base)
    return jnp.where(second_hit, jnp.log1p(-loss_share[:, 1])[:, None], with_first)


def steps_of(rng, shape, cuts, least, top_value):
    def one(position, parts):
        heights = jax.random.uniform(jax.random.fold_in(jax.random.fold_in(rng, 6), position), (parts,), jnp.float32, least / len(cuts), top_value / len(cuts))
        return jnp.repeat(jnp.exp(heights), shape[position] // parts).reshape((-1,) + (1,) * (len(shape) - position - 1))

    factor_of = one(*cuts[0])
    for cut in cuts[1:]:
        factor_of = factor_of * one(*cut)
    return factor_of


def scatter_about(rng, shape, width, most, cuts=(), kind=jnp.bfloat16):
    values = jax.random.normal(rng, shape, jnp.float32) * width
    if len(cuts) > 0:
        values = steps_of(rng, shape, cuts, -0.22, 0.18) * values
    return jnp.clip(values, min=-most, max=most).astype(kind)


def setup_inputs(seed: int = 0, part: int = 0) -> dict:
    arg_keys = jax.random.split(jax.random.key(seed), 7)
    part_splits = jax.random.split(jax.random.fold_in(arg_keys[6], part), 7)
    return {
        "queries": scatter_about(part_splits[0], (LEN, H * HEAD), 0.18, 1.0, ((0, 8),)),
        "keys_in": scatter_about(part_splits[1], (LEN, H * HEAD), 0.18, 1.0, ((0, 8),)),
        "value_input": scatter_about(part_splits[2], (LEN, H * HEAD), 0.18, 1.0, ((0, 8),)),
        "level_gain": jnp.clip(jnp.exp(math.log(2.0) - 2.3025851 * jax.random.uniform(part_splits[3], (LEVELS, H, LEN), jnp.float32) ** steps_of(part_splits[3], (LEVELS, H, LEN), ((2, 8),), -0.2, 0.2)), 0.2, 2.0),
        "decay_log": draw_decay_log(jax.random.fold_in(jax.random.fold_in(arg_keys[6], part), 71), part),
        "out_grad": scatter_about(part_splits[5], (LEN, H * HEAD), 0.18, 1.0, ((0, 8),)),
    }


TOP_ACCURACY = lax.Precision.HIGHEST

def level_table(tok, lvl_in):
    places = jnp.arange(tok, dtype=jnp.int32)
    mixing = jnp.bitwise_xor(places[:, None], places[None, :])
    table = jnp.zeros((tok, tok), jnp.int32)
    for power in range(lvl_in):
        table = table + (mixing >= 2 ** power).astype(jnp.int32)
    return table

def block_front(keys_h, value_rows_head, decay):
    running = jnp.cumsum(decay, axis=1)
    total_sum = running[:, -1]
    scaled_result = keys_h * jnp.exp(total_sum[:, None] - running)[:, :, None]
    return (jnp.einsum('ybu,ybe->yue', scaled_result, value_rows_head, precision=TOP_ACCURACY), total_sum)

def block_output(queries_h, keys_h, value_rows_head, gain, decay, buckets):
    tok = queries_h.shape[1]
    lvl_in = tok.bit_length() - 1
    running = jnp.cumsum(decay, axis=1)
    places = jnp.arange(tok, dtype=jnp.int32)
    causal = places[:, None] >= places[None, :]
    spread_gap = jnp.where(causal[None], running[:, :, None] - running[:, None, :], 0.0)
    fading = jnp.where(causal[None], jnp.exp(spread_gap), 0.0)
    table = level_table(tok, lvl_in)
    picks = (table[None] == jnp.arange(lvl_in + 1, dtype=jnp.int32)[:, None, None]).astype(jnp.float32)
    weighting = jnp.einsum('lij,lhi->hij', picks, gain[:lvl_in + 1], precision=TOP_ACCURACY)
    scores = jnp.einsum('hik,hjk->hij', queries_h, keys_h, precision=TOP_ACCURACY)
    result = jnp.einsum('hij,hjv->hiv', scores * weighting * fading, value_rows_head, precision=TOP_ACCURACY)
    lifted = queries_h * jnp.exp(running)[:, :, None]
    reach = gain[lvl_in + 1:][:, :, :, None] * lifted[None]
    return result + jnp.einsum('jhik,jhkv->hiv', reach, buckets, precision=TOP_ACCURACY)

def membership(count, depth):
    blocks = jnp.arange(count, dtype=jnp.int32)
    powers = jnp.arange(depth, dtype=jnp.int32)
    high_bits = jnp.right_shift(blocks[:, None], powers[None, :] + 1)
    own_bit = jnp.right_shift(blocks[:, None], powers[None, :]) % 2
    return (own_bit[:, :, None] == 1) & (high_bits[:, :, None] == high_bits.T[None]) & (own_bit.T[None] == 0)

def between_mask(count):
    blocks = jnp.arange(count, dtype=jnp.int32)
    inside = (blocks[None, None, :] > blocks[None, :, None]) & (blocks[None, None, :] < blocks[:, None, None])
    return inside.astype(jnp.float32)

def forward(query_full, key_full, value_full, gain, decay):
    count = N_CTX
    heads_q = query_full.reshape(count, TOK_DEV, H, HEAD).transpose(0, 2, 1, 3)
    heads_k = key_full.reshape(count, TOK_DEV, H, HEAD).transpose(0, 2, 1, 3)
    heads_v = value_full.reshape(count, TOK_DEV, H, HEAD).transpose(0, 2, 1, 3)
    decay_blocks = decay.reshape(H, count, TOK_DEV).transpose(1, 0, 2)
    gain_blocks = gain.reshape(LEVELS, H, count, TOK_DEV).transpose(2, 0, 1, 3)
    states, totals = lax.map(lambda items: block_front(items[0], items[1], items[2]), (heads_k, heads_v, decay_blocks))
    gaps = jnp.einsum('cdm,mh->cdh', between_mask(count), totals, precision=TOP_ACCURACY)
    member = membership(count, XLEV).astype(jnp.float32)

    def one_block(items):
        query_b, key_b, value_b, gain_b, decay_b, gap_b, member_b = items
        weights = member_b[:, :, None] * jnp.exp(gap_b)[None]
        buckets = jnp.einsum('jdh,dhkv->jhkv', weights, states, precision=TOP_ACCURACY)
        return block_output(query_b, key_b, value_b, gain_b, decay_b, buckets)
    outputs = lax.map(one_block, (heads_q, heads_k, heads_v, gain_blocks, decay_blocks, gaps, member))
    return outputs.transpose(0, 2, 1, 3).reshape(LEN, H * HEAD)

def reference(queries, keys_in, value_input, level_gain, decay_log, out_grad):
    mixed, back_fn = jax.vjp(forward, queries.astype(jnp.float32), keys_in.astype(jnp.float32), value_input.astype(jnp.float32), level_gain, decay_log)
    grads = back_fn(out_grad.astype(jnp.float32))
    return (mixed.astype(jnp.bfloat16), grads[0].astype(jnp.bfloat16), grads[1].astype(jnp.bfloat16), grads[2].astype(jnp.bfloat16), grads[3], grads[4])
```

```python
import functools

import jax
import jax.numpy as jnp
from jax import lax
from jax.experimental import pallas as pl
from jax.experimental.pallas import tpu as pltpu
from jax.sharding import PartitionSpec as P

TOP_ACCURACY = lax.Precision.HIGHEST


def from_partner(block, axis, distance):
    count = lax.axis_size(axis)
    route = []
    for low in range(count):
        high = low | 1 << distance
        if high != low and high < count:
            route += [(low, high), (high, low)]
    return lax.ppermute(block, axis, route)


def passed_along(value, axis, steps):
    count = lax.axis_size(axis)
    first, last = (max(0, -steps), min(count, count - steps))
    return lax.ppermute(value, axis, [(source, source + steps) for source in range(first, last)])


def level_table(tok, lvl_in):
    places = jnp.arange(tok, dtype=jnp.int32)
    mixing = jnp.bitwise_xor(places[:, None], places[None, :])
    table = jnp.zeros((tok, tok), jnp.int32)
    for power in range(lvl_in):
        table = table + (mixing >= 2**power).astype(jnp.int32)
    return table


def block_front(keys_h, value_rows_head, decay):
    running = jnp.cumsum(decay, axis=1)
    total_sum = running[:, -1]
    scaled_result = keys_h * jnp.exp(total_sum[:, None] - running)[:, :, None]
    return (
        jnp.einsum("ybu,ybe->yue", scaled_result, value_rows_head, precision=TOP_ACCURACY),
        total_sum,
    )


def block_output(queries_h, keys_h, value_rows_head, gain, decay, buckets):
    tok = queries_h.shape[1]
    lvl_in = tok.bit_length() - 1
    running = jnp.cumsum(decay, axis=1)
    places = jnp.arange(tok, dtype=jnp.int32)
    causal = places[:, None] >= places[None, :]
    spread_gap = jnp.where(causal[None], running[:, :, None] - running[:, None, :], 0.0)
    fading = jnp.where(causal[None], jnp.exp(spread_gap), 0.0)
    table = level_table(tok, lvl_in)
    picks = (table[None] == jnp.arange(lvl_in + 1, dtype=jnp.int32)[:, None, None]).astype(
        jnp.float32
    )
    weighting = jnp.einsum("lij,lhi->hij", picks, gain[: lvl_in + 1], precision=TOP_ACCURACY)
    scores = jnp.einsum("hik,hjk->hij", queries_h, keys_h, precision=TOP_ACCURACY)
    result = jnp.einsum(
        "hij,hjv->hiv", scores * weighting * fading, value_rows_head, precision=TOP_ACCURACY
    )
    lifted = queries_h * jnp.exp(running)[:, :, None]
    reach = gain[lvl_in + 1 :][:, :, :, None] * lifted[None]
    return result + jnp.einsum("jhik,jhkv->hiv", reach, buckets, precision=TOP_ACCURACY)


def merge_step(own_total, own_state, offset, other_total, other_state, is_upper):
    bucket = jnp.where(is_upper, jnp.exp(offset)[:, None, None] * other_state, 0.0)
    low_state = jnp.where(is_upper, other_state, own_state)
    high_state = jnp.where(is_upper, own_state, other_state)
    high_total = jnp.where(is_upper, own_total, other_total)
    merged = jnp.exp(high_total)[:, None, None] * low_state + high_state
    new_offset = offset + jnp.where(is_upper, other_total, 0.0)
    return (own_total + other_total, merged, new_offset, bucket)


def partner_grads(
    own_total, own_state, offset, other_total, g_total, g_state, g_offset, g_bucket, is_upper
):
    factor = jnp.exp(jnp.where(is_upper, own_total, other_total))
    d_other_state = jnp.where(
        is_upper,
        factor[:, None, None] * g_state + jnp.exp(offset)[:, None, None] * g_bucket,
        g_state,
    )
    lower_term = factor * jnp.sum(g_state * own_state, axis=(1, 2))
    d_other_total = g_total + jnp.where(is_upper, g_offset, lower_term)
    return (d_other_total, d_other_state)


def own_grads(
    own_total, offset, other_total, other_state, g_total, g_state, g_offset, g_bucket, is_upper
):
    factor = jnp.exp(jnp.where(is_upper, own_total, other_total))
    d_own_state = jnp.where(is_upper, g_state, factor[:, None, None] * g_state)
    upper_total = factor * jnp.sum(g_state * other_state, axis=(1, 2))
    d_own_total = g_total + jnp.where(is_upper, upper_total, 0.0)
    upper_offset = jnp.exp(offset) * jnp.sum(g_bucket * other_state, axis=(1, 2))
    d_offset = g_offset + jnp.where(is_upper, upper_offset, 0.0)
    return (d_own_total, d_own_state, d_offset)


def to_heads(block, heads):
    tokens, width = block.shape
    return block.reshape(tokens, heads, width // heads).transpose(1, 0, 2).astype(jnp.float32)


def from_heads(block):
    heads, tokens, head_dim = block.shape
    return block.transpose(1, 0, 2).reshape(tokens, heads * head_dim)


def per_device(queries, keys_in, value_input, level_gain, decay_log, out_grad):
    heads = decay_log.shape[0]
    query_h = to_heads(queries, heads)
    key_h = to_heads(keys_in, heads)
    value_h = to_heads(value_input, heads)
    cotangent = to_heads(out_grad, heads)
    count = lax.axis_size("ctx")
    depth = count.bit_length() - 1
    position = lax.axis_index("ctx")
    (state, total_sum), front_back = jax.vjp(block_front, key_h, value_h, decay_log)
    own_total = total_sum
    own_state = state
    offset = jnp.zeros_like(total_sum)
    saved = []
    found = []
    top_other = state
    for bit in range(depth):
        other_total, other_state = from_partner((own_total, own_state), "ctx", bit)
        is_upper = jnp.right_shift(position, bit) % 2 == 1
        saved.append((own_total, own_state, offset, other_total))
        if bit == depth - 1:
            top_other = other_state
        own_total, own_state, offset, bucket = merge_step(
            own_total, own_state, offset, other_total, other_state, is_upper
        )
        found.append(bucket)
    buckets = jnp.stack(found)
    mixed, out_back = jax.vjp(block_output, query_h, key_h, value_h, level_gain, decay_log, buckets)
    grad_query, grad_key, grad_value, grad_gain, grad_decay, bucket_gradient = out_back(cotangent)
    grad_total = jnp.zeros_like(total_sum)
    grad_state = jnp.zeros_like(state)
    grad_offset = jnp.zeros_like(total_sum)
    for bit in reversed(range(depth)):
        is_upper = jnp.right_shift(position, bit) % 2 == 1
        level_total, level_state, level_offset, level_other_total = saved[bit]
        d_other_total, d_other_state = partner_grads(
            level_total,
            level_state,
            level_offset,
            level_other_total,
            grad_total,
            grad_state,
            grad_offset,
            bucket_gradient[bit],
            is_upper,
        )
        if bit == depth - 1:
            back_total, back_state = passed_along(
                (d_other_total, d_other_state), "ctx", -(count // 2)
            )
            partner_state = top_other
        else:
            back_total, back_state, partner_state = from_partner(
                (d_other_total, d_other_state, level_state), "ctx", bit
            )
        d_own_total, d_own_state, d_offset = own_grads(
            level_total,
            level_offset,
            level_other_total,
            partner_state,
            grad_total,
            grad_state,
            grad_offset,
            bucket_gradient[bit],
            is_upper,
        )
        grad_total = d_own_total + back_total
        grad_state = d_own_state + back_state
        grad_offset = d_offset
    key_more, value_more, decay_more = front_back((grad_state, grad_total))
    return (
        from_heads(mixed).astype(jnp.bfloat16),
        from_heads(grad_query).astype(jnp.bfloat16),
        from_heads(grad_key + key_more).astype(jnp.bfloat16),
        from_heads(grad_value + value_more).astype(jnp.bfloat16),
        grad_gain,
        grad_decay + decay_more,
    )


F32 = jnp.float32
BF16 = jnp.bfloat16
CHUNKS = 2
NT = (((1,), (1,)), ((), ()))
TN = (((0,), (0,)), ((), ()))
NN = (((1,), (0,)), ((), ()))
NEVER = -1e30


def mxu(left, right, dims):
    return lax.dot_general(left, right, dims, preferred_element_type=F32)


def halves(value):
    high = value.astype(BF16)
    low = (value - high.astype(F32)).astype(BF16)
    return high, low


def split_rows(value):
    return jnp.concatenate(halves(value), axis=0)


def split_lanes(value):
    return jnp.concatenate(halves(value), axis=1)


def twice_rows(value):
    return jnp.concatenate([value, value], axis=0)


def twice_lanes(value):
    return jnp.concatenate([value, value], axis=1)


def running_decay(decay):
    tok = decay.shape[1]
    earlier = lax.broadcasted_iota(jnp.int32, (tok, tok), 0)
    later = lax.broadcasted_iota(jnp.int32, (tok, tok), 1)
    upto = (earlier <= later).astype(F32)
    return jnp.dot(decay, upto, precision=TOP_ACCURACY, preferred_element_type=F32)


def last_lane(running):
    return jnp.broadcast_to(running[:, running.shape[1] - 1 :], running.shape)


def columns(rows):
    count, tok = rows.shape
    if count < tok:
        rows = jnp.concatenate([rows, jnp.zeros((tok - count, tok), rows.dtype)], axis=0)
    return rows.T


def half_first(rows, core):
    half = rows.shape[0] // 2
    swapped = jnp.concatenate([rows[half:], rows[:half]], axis=0)
    return jnp.where(core == 0, rows, swapped)


def lane_block(ref, head, width):
    return ref[:, pl.ds(pl.multiple_of(head * width, width), width)]


def row_sums(value):
    ones = jnp.ones((8, 2 * value.shape[1]), BF16)
    return mxu(ones, split_lanes(value), NT)[:1]


def export_kernel(
    place, query, key, value, cotangent, gain, decay, send1, send2, level0, keep1, keep2
):
    position = place[0]
    core = position % 2
    chip = position // 2
    heads, tok = decay.shape
    dim = query.shape[1] // heads
    half = heads // 2
    first_cross = gain.shape[0] - 3
    running = running_decay(decay[...])
    total = last_lane(running)
    lift = jnp.exp(running)
    fall = jnp.exp(total - running)
    state1 = chip % 2 == 0
    state2 = chip == 1
    state0 = core == 0
    gain1 = gain[first_cross + 1]
    gain2 = gain[first_cross + 2]
    weight1 = jnp.where(state1, fall, jnp.where(chip == 1, gain1, gain2) * lift)
    weight2 = jnp.where(state2, fall, jnp.where(chip == 2, gain2, gain1) * lift)
    weight2 = jnp.where(chip == 0, 0.0, weight2)
    weight0 = jnp.where(state0, fall, gain[first_cross] * lift)
    spread = columns(
        jnp.concatenate([half_first(w, core) for w in (weight1, weight2, weight0)], axis=0)
    )
    for place_in in range(heads):
        mine = place_in < half
        index = place_in % half
        head = (core if mine else 1 - core) * half + index
        q, k, v, o = (lane_block(ref, head, dim) for ref in (query, key, value, cotangent))

        def outer(is_state, column):
            left = jnp.where(is_state, k, q).astype(F32) * spread[:, column : column + 1]
            right = jnp.where(is_state, v, o)
            return mxu(split_rows(left), twice_rows(right), TN)

        rows = pl.ds(index * dim, dim)
        (keep1 if mine else send1)[rows, :] = outer(state1, place_in)
        (keep2 if mine else send2)[rows, :] = outer(state2, heads + place_in)
        level0[pl.ds(pl.multiple_of(head * dim, dim), dim), :] = outer(
            state0, 2 * heads + place_in
        )
    send1[pl.ds(half * dim, heads), :] = total


def pair_factors(position, own_total, other_total, is_state):
    even = position % 2 == 0
    scale_own = is_state == even
    return (
        jnp.where(scale_own, jnp.exp(other_total), 1.0),
        jnp.where(scale_own, 1.0, jnp.exp(own_total)),
    )


def per_head(rows, dim):
    count, lanes = rows.shape
    return jnp.broadcast_to(rows[:, None, :], (count, dim, lanes)).reshape(count * dim, lanes)


def first_merge_kernel(place, decay, keep, got, *outs):
    position = place[0]
    chip = position // 2
    heads, tok = decay.shape
    half = heads // 2
    dim = keep.shape[0] // half
    own_total = last_lane(running_decay(decay[...]))
    other_total = got[pl.ds(half * dim, heads), :]
    own_factor, other_factor = pair_factors(position, own_total, other_total, chip % 2 == 0)
    own_factor = half_first(own_factor, position % 2)[:half]
    other_factor = half_first(other_factor, position % 2)[:half]
    count = half // len(outs)
    for part, out in enumerate(outs):
        for index in range(count):
            head = part * count + index
            rows = pl.ds(head * dim, dim)
            out[pl.ds(index * dim, dim), :] = (
                own_factor[head : head + 1] * keep[rows, :]
                + other_factor[head : head + 1] * got[rows, :]
            )
    outs[0][pl.ds(count * dim, heads), :] = own_total + other_total


def second_merge_kernel(part, place, decay, other_total, keep, got, first, out):
    position = place[0]
    chip = position // 2
    heads, tok = decay.shape
    half = heads // 2
    count = half // CHUNKS
    dim = out.shape[0] // count
    own_total = last_lane(running_decay(decay[...]))
    other_total = other_total[...]
    own_factor, other_factor = pair_factors(position, own_total, other_total, chip == 1)
    inner = (chip == 1) | (chip == 2)
    first_factor = jnp.where(inner, jnp.exp(own_total + other_total), 0.0)
    own_factor, other_factor, first_factor = (
        half_first(factor, position % 2)[part * count : (part + 1) * count]
        for factor in (own_factor, other_factor, first_factor)
    )
    for index in range(count):
        rows = pl.ds(index * dim, dim)
        out[rows, :] = (
            own_factor[index : index + 1] * keep[rows, :]
            + other_factor[index : index + 1] * got[rows, :]
            + first_factor[index : index + 1] * first[rows, :]
        )


def apply_state(left, right, state, weight):
    high, low = halves(state)
    first = mxu(twice_lanes(left), jnp.concatenate([high, low], axis=0), NN)
    second = mxu(twice_lanes(right), jnp.concatenate([high, low], axis=1), NT)
    sums = row_sums(first * right.astype(F32))
    return weight * first, weight * second, sums


def local_kernel(
    place,
    query,
    key,
    value,
    cotangent,
    gain,
    decay,
    level0,
    acc_out,
    acc_query,
    acc_key,
    acc_value,
    gain_rows,
    decay_rows,
    flow_rows,
):
    position = place[0]
    upper = position % 2 == 1
    group = pl.program_id(0)
    heads, tok = decay.shape
    width = query.shape[1]
    per_group = heads // pl.num_programs(0)
    dim = width // per_group
    inner_levels = tok.bit_length()
    running = running_decay(decay[...])
    total = last_lane(running)
    lift = jnp.exp(running)
    fall = jnp.exp(total - running)
    weight0 = jnp.where(upper, gain[inner_levels] * lift, fall)
    spread = columns(jnp.concatenate([running, weight0], axis=0))
    source = lax.broadcasted_iota(jnp.int32, (tok, tok), 0)
    target = lax.broadcasted_iota(jnp.int32, (tok, tok), 1)
    mixing = jnp.bitwise_xor(source, target)
    level = jnp.zeros((tok, tok), jnp.int32)
    for power in range(inner_levels - 1):
        level = level + (mixing >= 2**power).astype(jnp.int32)
    level = jnp.where(source <= target, level, -1)
    causal = source <= target
    ones = jnp.ones((8, 2 * tok), BF16)

    def one_group(start):
        for index in range(per_group):
            head = start + index
            lanes = slice(index * dim, (index + 1) * dim)
            q, k, v, o = (ref[:, lanes] for ref in (query, key, value, cotangent))
            scores = mxu(k, q, NT)
            pulls = mxu(v, o, NT)
            row = running[head : head + 1]
            fading = jnp.exp(jnp.where(causal, row - spread[:, head : head + 1], NEVER))
            weighting = jnp.zeros((tok, tok), F32)
            for place_in in range(inner_levels):
                weighting = jnp.where(
                    level == place_in, gain[place_in, head : head + 1, :], weighting
                )
            weighting = weighting * fading
            mixing_part = scores * weighting
            score_grad = pulls * weighting
            product = scores * pulls * fading
            flow = jnp.zeros((1, tok), F32)
            for place_in in range(inner_levels):
                found = jnp.sum(
                    jnp.where(level == place_in, product, 0.0), axis=0, keepdims=True
                )
                gain_rows[place_in, head : head + 1, :] = found
                if place_in > 0:
                    flow = flow + gain[place_in, head : head + 1, :] * found
            left = jnp.where(level > 0, mixing_part * pulls, 0.0)
            leaving = mxu(ones, split_lanes(left), NT)[:1]
            high, low = halves(mixing_part)
            out = mxu(jnp.concatenate([high, low], axis=0), twice_rows(v), TN)
            d_value = mxu(jnp.concatenate([high, low], axis=1), twice_rows(o), NN)
            high, low = halves(score_grad)
            d_query = mxu(jnp.concatenate([high, low], axis=0), twice_rows(k), TN)
            d_key = mxu(jnp.concatenate([high, low], axis=1), twice_rows(q), NN)
            state = level0[pl.ds(index * dim, dim), :]
            column = spread[:, heads + head : heads + head + 1]
            first, second, sums = apply_state(
                jnp.where(upper, q, k), jnp.where(upper, o, v), state, column
            )
            acc_out[:, lanes] = out + jnp.where(upper, first, 0.0)
            acc_query[:, lanes] = d_query + jnp.where(upper, second, 0.0)
            acc_key[:, lanes] = d_key + jnp.where(upper, 0.0, second)
            acc_value[:, lanes] = d_value + jnp.where(upper, 0.0, first)
            weighted = weight0[head : head + 1] * sums
            gain_rows[inner_levels, head : head + 1, :] = jnp.where(
                upper, lift[head : head + 1] * sums, 0.0
            )
            decay_rows[head : head + 1, :] = flow - leaving + jnp.where(upper, weighted, -weighted)
            flow_rows[head : head + 1, :] = jnp.where(upper, 0.0, weighted)

    for number in range(heads // per_group):
        pl.when(group == number)(lambda start=number * per_group: one_group(start))


def final_kernel(
    part,
    place,
    query,
    key,
    value,
    cotangent,
    gain,
    decay,
    other_total,
    chip_total,
    first_mine,
    first_other,
    second_mine,
    second_other,
    third_mine,
    third_other,
    pair1_mine,
    pair1_other,
    pair2_mine,
    pair2_other,
    level0,
    part_out,
    part_query,
    part_key,
    part_value,
    *rest,
):
    out_mixed, out_query, out_key, out_value, rows_out = rest[-5:]
    position = place[0]
    core = position % 2
    chip = position // 2
    group = pl.program_id(0)
    heads, tok = decay.shape
    half = heads // 2
    count = half // CHUNKS
    dim = query.shape[1] // count
    cross = gain.shape[0] - 3
    running = running_decay(decay[...])
    total = last_lane(running)
    other = other_total[...]
    odd = core == 1
    forward1 = chip != 0
    forward2 = chip == 3
    outer_chip = (chip == 0) | (chip == 3)
    offset1 = jnp.where(forward1 == odd, other, 0.0)
    offset2 = jnp.where(forward2 == odd, other, 0.0)
    offset2 = offset2 + jnp.where(outer_chip, chip_total[...], 0.0)
    chip_offset2 = jnp.where(outer_chip, chip_total[...], 0.0)
    gain1 = jnp.where(chip == 2, gain[cross + 2], gain[cross + 1])
    gain2 = gain[cross + 2]
    lift1 = jnp.exp(running + offset1)
    lift2 = jnp.exp(running + offset2)
    weight1 = jnp.where(forward1, gain1 * lift1, jnp.exp(total - running + offset1))
    weight2 = jnp.where(forward2, gain2 * lift2, jnp.exp(total - running + offset2))
    pair_flow1 = jnp.where(forward1 != odd, jnp.exp(total), 0.0)
    pair_flow2 = jnp.where(forward2 != odd, jnp.exp(total + chip_offset2), 0.0)
    chip_flow = jnp.where((chip == 1) | (chip == 2), jnp.exp(total + other), 0.0)
    picked = []
    for rows in (lift1, lift2, weight1, weight2, pair_flow1, pair_flow2, chip_flow):
        low = part * count
        picked.append(
            jnp.where(group == 0, rows[low : low + count], rows[half + low : half + low + count])
        )
    lift1, lift2, weight1, weight2, pair_flow1, pair_flow2, chip_flow = picked
    spread = columns(jnp.concatenate([weight1, weight2], axis=0))
    mine = group == core
    for index in range(count):
        lanes = slice(index * dim, (index + 1) * dim)
        rows = pl.ds(index * dim, dim)
        one = slice(index, index + 1)
        q, k, v, o = (ref[:, lanes] for ref in (query, key, value, cotangent))
        first = jnp.where(mine, first_mine[rows, :], first_other[rows, :])
        second = jnp.where(mine, second_mine[rows, :], second_other[rows, :])
        third = jnp.where(mine, third_mine[rows, :], third_other[rows, :])
        pair1 = jnp.where(mine, pair1_mine[rows, :], pair1_other[rows, :])
        pair2 = jnp.where(mine, pair2_mine[rows, :], pair2_other[rows, :])
        front = level0[rows, :]
        state1 = jnp.where(chip == 2, second, first)
        state2 = jnp.where(chip == 1, second, third)
        part1 = jnp.where(odd, front, jnp.where(chip == 1, pair1, pair2))
        part2 = jnp.where(odd, front, pair1)
        mixed = part_out[:, lanes]
        d_query = part_query[:, lanes]
        d_key = part_key[:, lanes]
        d_value = part_value[:, lanes]
        decay_row = jnp.zeros((1, tok), F32)
        flow_row = (
            pair_flow1[one] * jnp.sum(state1 * part1, axis=0, keepdims=True)
            + pair_flow2[one] * jnp.sum(state2 * part2, axis=0, keepdims=True)
            + chip_flow[one] * jnp.sum(first * second, axis=0, keepdims=True)
        )
        uses = (
            (forward1, state1, weight1, lift1, 0),
            (forward2, state2, weight2, lift2, count),
        )
        for number, (forward, state, weight, lift, column) in enumerate(uses):
            column = column + index
            left, right, sums = apply_state(
                jnp.where(forward, q, k),
                jnp.where(forward, o, v),
                state,
                spread[:, column : column + 1],
            )
            mixed = mixed + jnp.where(forward, left, 0.0)
            d_query = d_query + jnp.where(forward, right, 0.0)
            d_key = d_key + jnp.where(forward, 0.0, right)
            d_value = d_value + jnp.where(forward, 0.0, left)
            weighted = weight[one] * sums
            decay_row = decay_row + jnp.where(forward, weighted, -weighted)
            flow_row = flow_row + jnp.where(forward, 0.0, weighted)
            rows_out[number * count + index : number * count + index + 1, :] = lift[one] * sums
        rows_out[2 * count + index : 2 * count + index + 1, :] = decay_row
        rows_out[3 * count + index : 3 * count + index + 1, :] = flow_row
        out_mixed[:, lanes] = mixed.astype(BF16)
        out_query[:, lanes] = d_query.astype(BF16)
        out_key[:, lanes] = d_key.astype(BF16)
        out_value[:, lanes] = d_value.astype(BF16)


def gather_kernel(place, gain_rows, decay_rows, flow_rows, *rest):
    parts, (grad_gain, grad_decay) = rest[:-2], rest[-2:]
    position = place[0]
    chip = position // 2
    levels, heads, tok = grad_gain.shape
    half = heads // 2
    count = half // len(parts)

    def natural(kind):
        rows = []
        for group in range(2):
            for ref in parts:
                start = group * 4 * count + kind * count
                rows.append(ref[start : start + count, :])
        return jnp.concatenate(rows, axis=0)

    for place_in in range(levels - 2):
        grad_gain[place_in] = gain_rows[place_in]
    first, second = natural(0), natural(1)
    grad_gain[levels - 2] = jnp.where(chip % 2 == 1, first, 0.0)
    grad_gain[levels - 1] = jnp.where(chip == 2, first, jnp.where(chip == 3, second, 0.0))
    own = decay_rows[...] + natural(2)
    later = flow_rows[...] + natural(3)
    upper = lax.broadcasted_iota(jnp.int32, (tok, tok), 0)
    lower = lax.broadcasted_iota(jnp.int32, (tok, tok), 1)
    after = (upper >= lower).astype(F32)
    every = jnp.ones((tok, tok), F32)
    grad_decay[...] = jnp.dot(
        own, after, precision=TOP_ACCURACY, preferred_element_type=F32
    ) + jnp.dot(later, every, precision=TOP_ACCURACY, preferred_element_type=F32)


def sds(*shape, dtype=F32):
    return jax.ShapeDtypeStruct(shape, dtype)


def params():
    return pltpu.CompilerParams(vmem_limit_bytes=48 * 1024 * 1024)


SCALAR = pl.BlockSpec(memory_space=pltpu.SMEM)


def whole(shape):
    return pl.BlockSpec(shape, lambda g: (0,) * len(shape))


def line_device(queries, keys_in, value_input, level_gain, decay_log, out_grad):
    heads, tok = decay_log.shape
    dim = queries.shape[1] // heads
    half = heads // 2
    count = half // CHUNKS
    part_rows = count * dim
    half_rows = half * dim
    place = lax.axis_index("ctx").astype(jnp.int32).reshape(1)
    tokens = (queries, keys_in, value_input, out_grad)
    core_swap = [(at, at ^ 1) for at in range(8)]
    side_swap = [(at, at ^ 2) for at in range(8)]
    middle_swap = [(2, 4), (4, 2), (3, 5), (5, 3), (6, 6), (7, 7)]

    def swap(block, route):
        return lax.ppermute(block, "ctx", route)

    send1, send2, level0, keep1, keep2 = pl.pallas_call(
        export_kernel,
        out_shape=(
            sds(half_rows + heads, dim),
            sds(half_rows, dim),
            sds(2 * half_rows, dim),
            sds(half_rows, dim),
            sds(half_rows, dim),
        ),
        in_specs=[SCALAR] + [pl.BlockSpec()] * 6,
        compiler_params=params(),
        name="exports",
    )(place, *tokens, level_gain, decay_log)
    got1 = swap(send1, core_swap)
    got2 = swap(send2, core_swap)
    front = swap(level0, core_swap)
    got_keep1 = swap(keep1, core_swap)
    got_keep2 = swap(keep2, core_swap)
    first_sent = pl.pallas_call(
        first_merge_kernel,
        out_shape=tuple(
            sds(part_rows + (heads if part == 0 else 0), dim) for part in range(CHUNKS)
        ),
        in_specs=[SCALAR] + [pl.BlockSpec()] * 3,
        compiler_params=params(),
        name="first_merge",
    )(place, decay_log, keep1, got1)
    first = [swap(block, side_swap) for block in first_sent]

    groups = 4
    wide = pl.BlockSpec((tok, heads // groups * dim), lambda g: (0, g))
    acc_out, acc_query, acc_key, acc_value, gain_rows, decay_rows, flow_rows = pl.pallas_call(
        local_kernel,
        grid=(groups,),
        out_shape=(sds(tok, heads * dim),) * 4
        + (sds(tok.bit_length() + 1, heads, tok), sds(heads, tok), sds(heads, tok)),
        in_specs=[SCALAR]
        + [wide] * 4
        + [
            whole(level_gain.shape),
            whole(decay_log.shape),
            pl.BlockSpec((heads // groups * dim, dim), lambda g: (g, 0)),
        ],
        out_specs=(wide,) * 4
        + (whole((tok.bit_length() + 1, heads, tok)), whole((heads, tok)), whole((heads, tok))),
        compiler_params=params(),
        name="local",
    )(place, *tokens, level_gain, decay_log, front)

    second = []
    for part in range(CHUNKS):
        chunk = pl.BlockSpec((part_rows, dim), lambda g, part=part: (part, 0))
        sent = pl.pallas_call(
            functools.partial(second_merge_kernel, part),
            grid=(1,),
            out_shape=sds(part_rows, dim),
            in_specs=[
                SCALAR,
                whole(decay_log.shape),
                pl.BlockSpec((heads, dim), lambda g: (half_rows // heads, 0)),
                chunk,
                chunk,
                pl.BlockSpec((part_rows, dim), lambda g: (0, 0)),
            ],
            out_specs=pl.BlockSpec((part_rows, dim), lambda g: (0, 0)),
            compiler_params=params(),
            name="second_merge",
        )(place, decay_log, got1, keep2, got2, first[part])
        second.append(swap(sent, middle_swap))
    third = [swap(block, side_swap) for block in second]
    first_over = [swap(block, core_swap) for block in first]
    second_over = [swap(block, core_swap) for block in second]
    third_over = [swap(block, core_swap) for block in third]

    results = ()
    rows = []
    for part in range(CHUNKS):
        lanes = pl.BlockSpec((tok, part_rows), lambda g, part=part: (0, g * CHUNKS + part))
        own = pl.BlockSpec((part_rows, dim), lambda g: (0, 0))
        chunk = pl.BlockSpec((part_rows, dim), lambda g, part=part: (part, 0))
        before = len(results)
        *results, found = pl.pallas_call(
            functools.partial(final_kernel, part),
            grid=(2,),
            out_shape=(sds(tok, heads * dim, dtype=BF16),) * 4 + (sds(8 * count, tok),),
            in_specs=[SCALAR]
            + [lanes] * 4
            + [
                whole(level_gain.shape),
                whole(decay_log.shape),
                pl.BlockSpec((heads, dim), lambda g: (half_rows // heads, 0)),
                pl.BlockSpec((heads, dim), lambda g: (part_rows // heads, 0)),
            ]
            + [own] * 6
            + [chunk] * 4
            + [pl.BlockSpec((part_rows, dim), lambda g, part=part: (g * CHUNKS + part, 0))]
            + [lanes] * 4
            + [pl.BlockSpec(memory_space=pl.ANY)] * before,
            out_specs=(lanes,) * 4 + (pl.BlockSpec((4 * count, tok), lambda g: (g, 0)),),
            input_output_aliases={24 + at: at for at in range(before)},
            compiler_params=params(),
            name="final",
        )(
            place,
            *tokens,
            level_gain,
            decay_log,
            got1,
            first[0],
            first[part],
            first_over[part],
            second[part],
            second_over[part],
            third[part],
            third_over[part],
            got1,
            got_keep1,
            got2,
            got_keep2,
            front,
            acc_out,
            acc_query,
            acc_key,
            acc_value,
            *results,
        )
        rows.append(found)
    grad_gain, grad_decay = pl.pallas_call(
        gather_kernel,
        out_shape=(sds(*level_gain.shape), sds(heads, tok)),
        in_specs=[SCALAR] + [pl.BlockSpec()] * (3 + CHUNKS),
        compiler_params=params(),
        name="gather",
    )(place, gain_rows, decay_rows, flow_rows, *rows)
    return (*results, grad_gain, grad_decay)


def solution(mesh):
    placed = (
        P(("seq", "ctx"), None),
        P(("seq", "ctx"), None),
        P(("seq", "ctx"), None),
        P(None, None, ("seq", "ctx")),
        P(None, ("seq", "ctx")),
        P(("seq", "ctx"), None),
    )
    return jax.shard_map(
        line_device if mesh.shape["ctx"] == 8 else per_device,
        mesh=mesh,
        in_specs=placed,
        out_specs=(
            P(("seq", "ctx"), None),
            P(("seq", "ctx"), None),
            P(("seq", "ctx"), None),
            P(("seq", "ctx"), None),
            P(None, None, ("seq", "ctx")),
            P(None, ("seq", "ctx")),
        ),
        check_vma=False,
    )
```

```python
import functools

import jax
import jax.numpy as jnp
from jax import lax
from jax.experimental import pallas as pl
from jax.experimental.pallas import tpu as pltpu
from jax.sharding import PartitionSpec as P

TOP_ACCURACY = lax.Precision.HIGHEST


def from_partner(block, axis, distance):
    count = lax.axis_size(axis)
    route = []
    for low in range(count):
        high = low | 1 << distance
        if high != low and high < count:
            route += [(low, high), (high, low)]
    return lax.ppermute(block, axis, route)


def passed_along(value, axis, steps):
    count = lax.axis_size(axis)
    first, last = (max(0, -steps), min(count, count - steps))
    return lax.ppermute(value, axis, [(source, source + steps) for source in range(first, last)])


def level_table(tok, lvl_in):
    places = jnp.arange(tok, dtype=jnp.int32)
    mixing = jnp.bitwise_xor(places[:, None], places[None, :])
    table = jnp.zeros((tok, tok), jnp.int32)
    for power in range(lvl_in):
        table = table + (mixing >= 2**power).astype(jnp.int32)
    return table


def block_front(keys_h, value_rows_head, decay):
    running = jnp.cumsum(decay, axis=1)
    total_sum = running[:, -1]
    scaled_result = keys_h * jnp.exp(total_sum[:, None] - running)[:, :, None]
    return (
        jnp.einsum("ybu,ybe->yue", scaled_result, value_rows_head, precision=TOP_ACCURACY),
        total_sum,
    )


def block_output(queries_h, keys_h, value_rows_head, gain, decay, buckets):
    tok = queries_h.shape[1]
    lvl_in = tok.bit_length() - 1
    running = jnp.cumsum(decay, axis=1)
    places = jnp.arange(tok, dtype=jnp.int32)
    causal = places[:, None] >= places[None, :]
    spread_gap = jnp.where(causal[None], running[:, :, None] - running[:, None, :], 0.0)
    fading = jnp.where(causal[None], jnp.exp(spread_gap), 0.0)
    table = level_table(tok, lvl_in)
    picks = (table[None] == jnp.arange(lvl_in + 1, dtype=jnp.int32)[:, None, None]).astype(
        jnp.float32
    )
    weighting = jnp.einsum("lij,lhi->hij", picks, gain[: lvl_in + 1], precision=TOP_ACCURACY)
    scores = jnp.einsum("hik,hjk->hij", queries_h, keys_h, precision=TOP_ACCURACY)
    result = jnp.einsum(
        "hij,hjv->hiv", scores * weighting * fading, value_rows_head, precision=TOP_ACCURACY
    )
    lifted = queries_h * jnp.exp(running)[:, :, None]
    reach = gain[lvl_in + 1 :][:, :, :, None] * lifted[None]
    return result + jnp.einsum("jhik,jhkv->hiv", reach, buckets, precision=TOP_ACCURACY)


def merge_step(own_total, own_state, offset, other_total, other_state, is_upper):
    bucket = jnp.where(is_upper, jnp.exp(offset)[:, None, None] * other_state, 0.0)
    low_state = jnp.where(is_upper, other_state, own_state)
    high_state = jnp.where(is_upper, own_state, other_state)
    high_total = jnp.where(is_upper, own_total, other_total)
    merged = jnp.exp(high_total)[:, None, None] * low_state + high_state
    new_offset = offset + jnp.where(is_upper, other_total, 0.0)
    return (own_total + other_total, merged, new_offset, bucket)


def partner_grads(
    own_total, own_state, offset, other_total, g_total, g_state, g_offset, g_bucket, is_upper
):
    factor = jnp.exp(jnp.where(is_upper, own_total, other_total))
    d_other_state = jnp.where(
        is_upper,
        factor[:, None, None] * g_state + jnp.exp(offset)[:, None, None] * g_bucket,
        g_state,
    )
    lower_term = factor * jnp.sum(g_state * own_state, axis=(1, 2))
    d_other_total = g_total + jnp.where(is_upper, g_offset, lower_term)
    return (d_other_total, d_other_state)


def own_grads(
    own_total, offset, other_total, other_state, g_total, g_state, g_offset, g_bucket, is_upper
):
    factor = jnp.exp(jnp.where(is_upper, own_total, other_total))
    d_own_state = jnp.where(is_upper, g_state, factor[:, None, None] * g_state)
    upper_total = factor * jnp.sum(g_state * other_state, axis=(1, 2))
    d_own_total = g_total + jnp.where(is_upper, upper_total, 0.0)
    upper_offset = jnp.exp(offset) * jnp.sum(g_bucket * other_state, axis=(1, 2))
    d_offset = g_offset + jnp.where(is_upper, upper_offset, 0.0)
    return (d_own_total, d_own_state, d_offset)


def to_heads(block, heads):
    tokens, width = block.shape
    return block.reshape(tokens, heads, width // heads).transpose(1, 0, 2).astype(jnp.float32)


def from_heads(block):
    heads, tokens, head_dim = block.shape
    return block.transpose(1, 0, 2).reshape(tokens, heads * head_dim)


def per_device(queries, keys_in, value_input, level_gain, decay_log, out_grad):
    heads = decay_log.shape[0]
    query_h = to_heads(queries, heads)
    key_h = to_heads(keys_in, heads)
    value_h = to_heads(value_input, heads)
    cotangent = to_heads(out_grad, heads)
    count = lax.axis_size("ctx")
    depth = count.bit_length() - 1
    position = lax.axis_index("ctx")
    (state, total_sum), front_back = jax.vjp(block_front, key_h, value_h, decay_log)
    own_total = total_sum
    own_state = state
    offset = jnp.zeros_like(total_sum)
    saved = []
    found = []
    top_other = state
    for bit in range(depth):
        other_total, other_state = from_partner((own_total, own_state), "ctx", bit)
        is_upper = jnp.right_shift(position, bit) % 2 == 1
        saved.append((own_total, own_state, offset, other_total))
        if bit == depth - 1:
            top_other = other_state
        own_total, own_state, offset, bucket = merge_step(
            own_total, own_state, offset, other_total, other_state, is_upper
        )
        found.append(bucket)
    buckets = jnp.stack(found)
    mixed, out_back = jax.vjp(block_output, query_h, key_h, value_h, level_gain, decay_log, buckets)
    grad_query, grad_key, grad_value, grad_gain, grad_decay, bucket_gradient = out_back(cotangent)
    grad_total = jnp.zeros_like(total_sum)
    grad_state = jnp.zeros_like(state)
    grad_offset = jnp.zeros_like(total_sum)
    for bit in reversed(range(depth)):
        is_upper = jnp.right_shift(position, bit) % 2 == 1
        level_total, level_state, level_offset, level_other_total = saved[bit]
        d_other_total, d_other_state = partner_grads(
            level_total,
            level_state,
            level_offset,
            level_other_total,
            grad_total,
            grad_state,
            grad_offset,
            bucket_gradient[bit],
            is_upper,
        )
        if bit == depth - 1:
            back_total, back_state = passed_along(
                (d_other_total, d_other_state), "ctx", -(count // 2)
            )
            partner_state = top_other
        else:
            back_total, back_state, partner_state = from_partner(
                (d_other_total, d_other_state, level_state), "ctx", bit
            )
        d_own_total, d_own_state, d_offset = own_grads(
            level_total,
            level_offset,
            level_other_total,
            partner_state,
            grad_total,
            grad_state,
            grad_offset,
            bucket_gradient[bit],
            is_upper,
        )
        grad_total = d_own_total + back_total
        grad_state = d_own_state + back_state
        grad_offset = d_offset
    key_more, value_more, decay_more = front_back((grad_state, grad_total))
    return (
        from_heads(mixed).astype(jnp.bfloat16),
        from_heads(grad_query).astype(jnp.bfloat16),
        from_heads(grad_key + key_more).astype(jnp.bfloat16),
        from_heads(grad_value + value_more).astype(jnp.bfloat16),
        grad_gain,
        grad_decay + decay_more,
    )


F32 = jnp.float32
BF16 = jnp.bfloat16
CHUNKS = 2
NT = (((1,), (1,)), ((), ()))
TN = (((0,), (0,)), ((), ()))
NN = (((1,), (0,)), ((), ()))
NEVER = -1e30


def mxu(left, right, dims):
    return lax.dot_general(left, right, dims, preferred_element_type=F32)


def halves(value):
    high = value.astype(BF16)
    low = (value - high.astype(F32)).astype(BF16)
    return high, low


def split_rows(value):
    return jnp.concatenate(halves(value), axis=0)


def split_lanes(value):
    return jnp.concatenate(halves(value), axis=1)


def twice_rows(value):
    return jnp.concatenate([value, value], axis=0)


def twice_lanes(value):
    return jnp.concatenate([value, value], axis=1)


def running_decay(decay):
    tok = decay.shape[1]
    earlier = lax.broadcasted_iota(jnp.int32, (tok, tok), 0)
    later = lax.broadcasted_iota(jnp.int32, (tok, tok), 1)
    upto = (earlier <= later).astype(F32)
    return jnp.dot(decay, upto, precision=TOP_ACCURACY, preferred_element_type=F32)


def last_lane(running):
    return jnp.broadcast_to(running[:, running.shape[1] - 1 :], running.shape)


def columns(rows):
    count, tok = rows.shape
    if count < tok:
        rows = jnp.concatenate([rows, jnp.zeros((tok - count, tok), rows.dtype)], axis=0)
    return rows.T


def half_first(rows, core):
    half = rows.shape[0] // 2
    swapped = jnp.concatenate([rows[half:], rows[:half]], axis=0)
    return jnp.where(core == 0, rows, swapped)


def lane_block(ref, head, width):
    return ref[:, pl.ds(pl.multiple_of(head * width, width), width)]


def take_half(rows, core, part, count):
    half = rows.shape[0] // 2
    low = part * count
    return jnp.where(core == 0, rows[low : low + count], rows[half + low : half + low + count])


def outer_products(left, right, weight_column):
    turned = left.T
    return mxu(twice_lanes(turned), split_rows(right.astype(F32) * weight_column), NN)


def first_export_kernel(
    place, query, key, value, cotangent, gain, decay, send, keep, lefts, rights, gains, decays, sems
):
    position = place[0]
    core = position % 2
    chip = position // 2
    heads, tok = decay.shape
    width = query.shape[1]
    dim = width // heads
    half = heads // 2
    cross = gain.shape[0] - 3
    wide = half * dim
    state = chip % 2 == 0
    copies = []
    for side in range(2):
        lanes = pl.ds(pl.multiple_of((1 - core if side == 0 else core) * wide, wide), wide)
        for slot, (chosen, plain, into) in enumerate(((key, query, lefts), (value, cotangent, rights))):
            sem = sems.at[2 * side + slot]
            target = into.at[:, pl.ds(side * wide, wide)]

            @pl.when(state)
            def _(chosen=chosen, target=target, sem=sem, lanes=lanes):
                pltpu.make_async_copy(chosen.at[:, lanes], target, sem).start()

            @pl.when(jnp.logical_not(state))
            def _(plain=plain, target=target, sem=sem, lanes=lanes):
                pltpu.make_async_copy(plain.at[:, lanes], target, sem).start()

            copies.append(pltpu.make_async_copy(plain.at[:, lanes], target, sem))
    small = [
        pltpu.make_async_copy(decay, decays, sems.at[4]),
        pltpu.make_async_copy(gain.at[pl.ds(cross + 1, 2)], gains, sems.at[5]),
    ]
    for copy in small:
        copy.start()
    for copy in small:
        copy.wait()
    running = running_decay(decays[...])
    total = last_lane(running)
    lift = jnp.exp(running)
    weight = jnp.where(
        state, jnp.exp(total - running), jnp.where(chip == 1, gains[0], gains[1]) * lift
    )
    spread = columns(half_first(weight, 1 - core))
    send[pl.ds(half * dim, heads), :] = total
    for index in range(heads):
        if index % half == 0:
            for copy in copies[2 * (index // half) : 2 * (index // half) + 2]:
                copy.wait()
        lanes = slice(index * dim, (index + 1) * dim)
        rows = pl.ds(index % half * dim, dim)
        (send if index < half else keep)[rows, :] = outer_products(
            lefts[:, lanes], rights[:, lanes], spread[:, index : index + 1]
        )


def second_export_kernel(
    place, query, key, value, cotangent, gain, decay, keep1, send, keep, bundle
):
    position = place[0]
    core = position % 2
    chip = position // 2
    heads, tok = decay.shape
    dim = query.shape[1] // heads
    half = heads // 2
    cross = gain.shape[0] - 3
    running = running_decay(decay[...])
    lift = jnp.exp(running)
    fall = jnp.exp(last_lane(running) - running)
    state2 = chip == 1
    state0 = core == 0
    weight2 = jnp.where(state2, fall, jnp.where(chip == 2, gain[cross + 2], gain[cross + 1]) * lift)
    weight2 = jnp.where(chip == 0, 0.0, weight2)
    weight0 = jnp.where(state0, fall, gain[cross] * lift)
    spread = columns(
        jnp.concatenate([half_first(w, 1 - core) for w in (weight2, weight0)], axis=0)
    )
    bundle[pl.ds(heads * dim, half * dim), :] = keep1[...]
    for index in range(heads):
        mine = index >= half
        head = (core if mine else 1 - core) * half + index % half
        q, k, v, o = (lane_block(ref, head, dim) for ref in (query, key, value, cotangent))
        second = outer_products(
            jnp.where(state2, k, q), jnp.where(state2, v, o), spread[:, index : index + 1]
        )
        rows = pl.ds(index % half * dim, dim)
        (keep if mine else send)[rows, :] = second
        if mine:
            bundle[pl.ds((heads + index) * dim, dim), :] = second
        bundle[pl.ds(pl.multiple_of(head * dim, dim), dim), :] = outer_products(
            jnp.where(state0, k, q),
            jnp.where(state0, v, o),
            spread[:, heads + index : heads + index + 1],
        )


def pair_factors(position, own_total, other_total, is_state):
    even = position % 2 == 0
    scale_own = is_state == even
    return (
        jnp.where(scale_own, jnp.exp(other_total), 1.0),
        jnp.where(scale_own, 1.0, jnp.exp(own_total)),
    )


def first_merge_kernel(place, decay, keep, got, after, *outs):
    position = place[0]
    chip = position // 2
    heads, tok = decay.shape
    half = heads // 2
    dim = keep.shape[0] // half
    own_total = last_lane(running_decay(decay[...]))
    other_total = got[pl.ds(half * dim, heads), :]
    own_factor, other_factor = pair_factors(position, own_total, other_total, chip % 2 == 0)
    own_factor = half_first(own_factor, position % 2)[:half]
    other_factor = half_first(other_factor, position % 2)[:half]
    count = half // len(outs)
    for part, out in enumerate(outs):
        for index in range(count):
            head = part * count + index
            rows = pl.ds(head * dim, dim)
            out[pl.ds(index * dim, dim), :] = (
                own_factor[head : head + 1] * keep[rows, :]
                + other_factor[head : head + 1] * got[rows, :]
            )
    outs[0][pl.ds(count * dim, heads), :] = own_total + other_total


def second_merge_kernel(part, place, decay, other_total, keep, got, first, after, out):
    position = place[0]
    chip = position // 2
    heads, tok = decay.shape
    half = heads // 2
    count = half // CHUNKS
    dim = out.shape[0] // count
    own_total = last_lane(running_decay(decay[...]))
    other_total = other_total[...]
    own_factor, other_factor = pair_factors(position, own_total, other_total, chip == 1)
    inner = (chip == 1) | (chip == 2)
    first_factor = jnp.where(inner, jnp.exp(own_total + other_total), 0.0)
    own_factor, other_factor, first_factor = (
        half_first(factor, position % 2)[part * count : (part + 1) * count]
        for factor in (own_factor, other_factor, first_factor)
    )
    for index in range(count):
        rows = pl.ds(index * dim, dim)
        out[rows, :] = (
            own_factor[index : index + 1] * keep[rows, :]
            + other_factor[index : index + 1] * got[rows, :]
            + first_factor[index : index + 1] * first[rows, :]
        )


def lane_sums(value):
    ones = jnp.ones((2 * value.shape[1], value.shape[1]), BF16)
    return mxu(split_lanes(value), ones, NN)


def apply_state(left, right, state, weight):
    high, low = halves(state)
    first = mxu(twice_lanes(left), jnp.concatenate([high, low], axis=0), NN)
    second = mxu(twice_lanes(right), jnp.concatenate([high, low], axis=1), NT)
    sums = lane_sums(first * right.astype(F32))
    return weight * first, weight * second, sums


def local_kernel(start, query, key, value, cotangent, gain, decay, *rest):
    acc_out, acc_query, acc_key, acc_value, gain_rows, decay_rows = rest[-6:]
    tok = decay.shape[1]
    count = decay_rows.shape[0]
    dim = query.shape[1] // count
    inner_levels = tok.bit_length()
    running = running_decay(decay[...])
    spread = columns(running)
    source = lax.broadcasted_iota(jnp.int32, (tok, tok), 0)
    target = lax.broadcasted_iota(jnp.int32, (tok, tok), 1)
    mixing = jnp.bitwise_xor(source, target)
    level = jnp.zeros((tok, tok), jnp.int32)
    for power in range(inner_levels - 1):
        level = level + (mixing >= 2**power).astype(jnp.int32)
    level = jnp.where(source <= target, level, -1)
    causal = source <= target
    lane = lax.broadcasted_iota(jnp.int32, (tok, tok), 1)
    gathered = jnp.zeros((tok, tok), F32)
    for index in range(count):
        head = start + index
        lanes = slice(index * dim, (index + 1) * dim)
        q, k, v, o = (ref[:, lanes] for ref in (query, key, value, cotangent))
        scores = mxu(k, q, NT)
        pulls = mxu(v, o, NT)
        row = running[head : head + 1]
        fading = jnp.exp(jnp.where(causal, row - spread[:, head : head + 1], NEVER))
        weighting = jnp.zeros((tok, tok), F32)
        for place_in in range(inner_levels):
            weighting = jnp.where(
                level == place_in, gain[place_in, head : head + 1, :], weighting
            )
        weighting = weighting * fading
        mixing_part = scores * weighting
        score_grad = pulls * weighting
        product = scores * pulls * fading
        flow = jnp.zeros((1, tok), F32)
        for place_in in range(inner_levels):
            found = jnp.sum(jnp.where(level == place_in, product, 0.0), axis=0, keepdims=True)
            gain_rows[place_in, index : index + 1, :] = found
            if place_in > 0:
                flow = flow + gain[place_in, head : head + 1, :] * found
        decay_rows[index : index + 1, :] = flow
        left = jnp.where(level > 0, mixing_part * pulls, 0.0)
        gathered = jnp.where(lane == index, lane_sums(left), gathered)
        high, low = halves(mixing_part)
        acc_out[:, lanes] = mxu(jnp.concatenate([high, low], axis=0), twice_rows(v), TN)
        acc_value[:, lanes] = mxu(jnp.concatenate([high, low], axis=1), twice_rows(o), NN)
        high, low = halves(score_grad)
        acc_query[:, lanes] = mxu(jnp.concatenate([high, low], axis=0), twice_rows(k), TN)
        acc_key[:, lanes] = mxu(jnp.concatenate([high, low], axis=1), twice_rows(q), NN)
    decay_rows[...] = decay_rows[...] - gathered.T[:count]


def use_rows(rows_out, uses, gathered, extra):
    turned = gathered.T
    count = rows_out.shape[0] // 4
    decay_row = jnp.zeros((count, turned.shape[1]), F32)
    flow_row = extra
    for number, (forward, weight, lift) in enumerate(uses):
        sums = turned[number * count : (number + 1) * count]
        weighted = weight * sums
        decay_row = decay_row + jnp.where(forward, weighted, -weighted)
        flow_row = flow_row + jnp.where(forward, 0.0, weighted)
        rows_out[number * count : (number + 1) * count, :] = lift * sums
    rows_out[2 * count : 3 * count, :] = decay_row
    rows_out[3 * count : 4 * count, :] = flow_row


def pair_kernel(
    place, query, key, value, cotangent, gain, decay, level0, after, out_left, out_right, rows_out
):
    position = place[0]
    odd = position % 2 == 1
    heads, tok = decay.shape
    dim = query.shape[1] // heads
    running = running_decay(decay[...])
    lift = jnp.exp(running)
    cross = gain.shape[0] - 3
    weight = jnp.where(odd, gain[cross] * lift, jnp.exp(last_lane(running) - running))
    spread = columns(weight)
    lane = lax.broadcasted_iota(jnp.int32, (tok, tok), 1)
    gathered = jnp.zeros((tok, tok), F32)
    for head in range(heads):
        lanes = slice(head * dim, (head + 1) * dim)
        q, k, v, o = (ref[:, lanes] for ref in (query, key, value, cotangent))
        left, right, sums = apply_state(
            jnp.where(odd, q, k),
            jnp.where(odd, o, v),
            level0[pl.ds(head * dim, dim), :],
            spread[:, head : head + 1],
        )
        out_left[:, lanes] = left
        out_right[:, lanes] = right
        gathered = jnp.where(lane == head, sums, gathered)
    use_rows(rows_out, ((odd, weight, jnp.where(odd, lift, 0.0)),), gathered, jnp.zeros((heads, tok), F32))


def first_use_kernel(
    part,
    mine,
    place,
    query,
    key,
    value,
    cotangent,
    gain,
    decay,
    other_total,
    first,
    second,
    pair1,
    pair2,
    level0,
    out_left,
    out_right,
    rows_out,
):
    position = place[0]
    core = position % 2
    side = core if mine else 1 - core
    chip = position // 2
    heads, tok = decay.shape
    count = heads // 2 // CHUNKS
    dim = query.shape[1] // count
    cross = gain.shape[0] - 3
    running = running_decay(decay[...])
    total = last_lane(running)
    other = other_total[...]
    odd = core == 1
    forward = chip != 0
    offset = jnp.where(forward == odd, other, 0.0)
    lift = jnp.exp(running + offset)
    weight = jnp.where(
        forward,
        jnp.where(chip == 2, gain[cross + 2], gain[cross + 1]) * lift,
        jnp.exp(total - running + offset),
    )
    pair_flow = jnp.where(forward != odd, jnp.exp(total), 0.0)
    chip_flow = jnp.where((chip == 1) | (chip == 2), jnp.exp(total + other), 0.0)
    lift, weight, pair_flow, chip_flow = (
        take_half(rows, side, part, count) for rows in (lift, weight, pair_flow, chip_flow)
    )
    spread = columns(weight)
    lane = lax.broadcasted_iota(jnp.int32, (tok, tok), 1)
    gathered = jnp.zeros((tok, tok), F32)
    flows = []
    for index in range(count):
        lanes = slice(index * dim, (index + 1) * dim)
        rows = pl.ds(index * dim, dim)
        one = slice(index, index + 1)
        q, k, v, o = (ref[:, lanes] for ref in (query, key, value, cotangent))
        state = jnp.where(chip == 2, second[rows, :], first[rows, :])
        partner = jnp.where(odd, level0[rows, :], jnp.where(chip == 1, pair1[rows, :], pair2[rows, :]))
        flows.append(
            pair_flow[one] * jnp.sum(state * partner, axis=0, keepdims=True)
            + chip_flow[one] * jnp.sum(first[rows, :] * second[rows, :], axis=0, keepdims=True)
        )
        left, right, sums = apply_state(
            jnp.where(forward, q, k), jnp.where(forward, o, v), state, spread[:, one]
        )
        out_left[:, lanes] = left
        out_right[:, lanes] = right
        gathered = jnp.where(lane == index, sums, gathered)
    use_rows(rows_out, ((forward, weight, lift),), gathered, jnp.concatenate(flows, axis=0))


def last_use_kernel(
    part,
    mine,
    place,
    query,
    key,
    value,
    cotangent,
    gain,
    decay,
    other_total,
    chip_total,
    second,
    third,
    pair1,
    level0,
    left0,
    right0,
    left1,
    right1,
    part_out,
    part_query,
    part_key,
    part_value,
    *rest,
):
    out_mixed, out_query, out_key, out_value, rows_out = rest[-5:]
    position = place[0]
    core = position % 2
    side = core if mine else 1 - core
    chip = position // 2
    heads, tok = decay.shape
    count = heads // 2 // CHUNKS
    dim = query.shape[1] // count
    cross = gain.shape[0] - 3
    running = running_decay(decay[...])
    total = last_lane(running)
    odd = core == 1
    forward1 = chip != 0
    forward = chip == 3
    chip_offset = jnp.where((chip == 0) | (chip == 3), chip_total[...], 0.0)
    offset = jnp.where(forward == odd, other_total[...], 0.0) + chip_offset
    lift = jnp.exp(running + offset)
    weight = jnp.where(forward, gain[cross + 2] * lift, jnp.exp(total - running + offset))
    pair_flow = jnp.where(forward != odd, jnp.exp(total + chip_offset), 0.0)
    lift, weight, pair_flow = (
        take_half(rows, side, part, count) for rows in (lift, weight, pair_flow)
    )
    spread = columns(weight)
    lane = lax.broadcasted_iota(jnp.int32, (tok, tok), 1)
    gathered = jnp.zeros((tok, tok), F32)
    flows = []
    for index in range(count):
        lanes = slice(index * dim, (index + 1) * dim)
        rows = pl.ds(index * dim, dim)
        one = slice(index, index + 1)
        q, k, v, o = (ref[:, lanes] for ref in (query, key, value, cotangent))
        state = jnp.where(chip == 1, second[rows, :], third[rows, :])
        partner = jnp.where(odd, level0[rows, :], pair1[rows, :])
        flows.append(pair_flow[one] * jnp.sum(state * partner, axis=0, keepdims=True))
        left, right, sums = apply_state(
            jnp.where(forward, q, k), jnp.where(forward, o, v), state, spread[:, one]
        )
        gathered = jnp.where(lane == index, sums, gathered)
        forward_left = jnp.where(odd, left0[:, lanes], 0.0)
        forward_right = jnp.where(odd, right0[:, lanes], 0.0)
        back_left = jnp.where(odd, 0.0, left0[:, lanes])
        back_right = jnp.where(odd, 0.0, right0[:, lanes])
        for is_forward, a_left, a_right in (
            (forward1, left1[:, lanes], right1[:, lanes]),
            (forward, left, right),
        ):
            forward_left = forward_left + jnp.where(is_forward, a_left, 0.0)
            forward_right = forward_right + jnp.where(is_forward, a_right, 0.0)
            back_left = back_left + jnp.where(is_forward, 0.0, a_left)
            back_right = back_right + jnp.where(is_forward, 0.0, a_right)
        out_mixed[:, lanes] = (part_out[:, lanes] + forward_left).astype(BF16)
        out_query[:, lanes] = (part_query[:, lanes] + forward_right).astype(BF16)
        out_value[:, lanes] = (part_value[:, lanes] + back_left).astype(BF16)
        out_key[:, lanes] = (part_key[:, lanes] + back_right).astype(BF16)
    use_rows(rows_out, ((forward, weight, lift),), gathered, jnp.concatenate(flows, axis=0))


def gather_kernel(place, pair_rows, *rest):
    groups = 2 * CHUNKS
    gain_rows, decay_rows = rest[:groups], rest[groups : 2 * groups]
    parts, (grad_gain, grad_decay) = rest[2 * groups : -2], rest[-2:]
    position = place[0]
    core = position % 2
    chip = position // 2
    levels, heads, tok = grad_gain.shape
    count = heads // 2 // CHUNKS

    def natural(refs, kind):
        rows = [ref[kind * count : (kind + 1) * count, :] for ref in refs]
        return half_first(jnp.concatenate(rows, axis=0), core)

    def of_pair(kind):
        return pair_rows[kind * heads : (kind + 1) * heads, :]

    for place_in in range(levels - 3):
        grad_gain[place_in] = jnp.concatenate([ref[place_in] for ref in gain_rows], axis=0)
    first, second = natural(parts[:groups], 0), natural(parts[groups:], 0)
    grad_gain[levels - 3] = of_pair(0)
    grad_gain[levels - 2] = jnp.where(chip % 2 == 1, first, 0.0)
    grad_gain[levels - 1] = jnp.where(chip == 2, first, jnp.where(chip == 3, second, 0.0))
    own = jnp.concatenate([ref[...] for ref in decay_rows], axis=0)
    own = own + of_pair(2) + natural(parts[:groups], 2) + natural(parts[groups:], 2)
    later = of_pair(3) + natural(parts[:groups], 3) + natural(parts[groups:], 3)
    upper = lax.broadcasted_iota(jnp.int32, (tok, tok), 0)
    lower = lax.broadcasted_iota(jnp.int32, (tok, tok), 1)
    after = (upper >= lower).astype(F32)
    every = jnp.ones((tok, tok), F32)
    grad_decay[...] = jnp.dot(
        own, after, precision=TOP_ACCURACY, preferred_element_type=F32
    ) + jnp.dot(later, every, precision=TOP_ACCURACY, preferred_element_type=F32)


def after(value, *others):
    return lax.optimization_barrier((value, *others))[0]


def sds(*shape, dtype=F32):
    return jax.ShapeDtypeStruct(shape, dtype)


def params(mebibytes=24):
    return pltpu.CompilerParams(vmem_limit_bytes=mebibytes * 1024 * 1024)


SCALAR = pl.BlockSpec(memory_space=pltpu.SMEM)
ANYWHERE = pl.BlockSpec(memory_space=pl.ANY)
IN_HBM = pl.BlockSpec(memory_space=pltpu.HBM)


def whole(shape):
    return pl.BlockSpec(shape, lambda g, place: (0,) * len(shape))


FIRST_EXPORTS_COST = 1
FIRST_MERGE_COST = 1
SECOND_EXPORTS_COST = 1
LOCAL_COST = 1
SECOND_MERGE_COST = 1
PAIR_USE_COST = 1
FIRST_USE_COST = 1
LAST_USE_COST = 1
GATHER_COST = 1


def cost(flops):
    return pl.CostEstimate(flops=flops, bytes_accessed=1, transcendentals=0)


def line_device(queries, keys_in, value_input, level_gain, decay_log, out_grad):
    heads, tok = decay_log.shape
    dim = queries.shape[1] // heads
    half = heads // 2
    count = half // CHUNKS
    part_rows = count * dim
    half_rows = half * dim
    place = lax.axis_index("ctx").astype(jnp.int32).reshape(1)
    tokens = (queries, keys_in, value_input, out_grad)
    core_swap = [(at, at ^ 1) for at in range(8)]
    side_swap = [(at, at ^ 2) for at in range(8)]
    middle_swap = [(2, 4), (4, 2), (3, 5), (5, 3), (6, 6), (7, 7)]

    def swap(block, route):
        return lax.ppermute(block, "ctx", route)

    send1, keep1 = pl.pallas_call(
        first_export_kernel,
        out_shape=(sds(half_rows + heads, dim), sds(half_rows, dim)),
        in_specs=[SCALAR] + [IN_HBM] * 6,
        scratch_shapes=[
            pltpu.VMEM((tok, heads * dim), BF16),
            pltpu.VMEM((tok, heads * dim), BF16),
            pltpu.VMEM((2, heads, tok), F32),
            pltpu.VMEM((heads, tok), F32),
            pltpu.SemaphoreType.DMA((6,)),
        ],
        compiler_params=params(62),

        cost_estimate=cost(FIRST_EXPORTS_COST),
        name="first_exports",
    )(place, *tokens, level_gain, decay_log)
    got1 = swap(send1, core_swap)
    send2, keep2, bundle = pl.pallas_call(
        second_export_kernel,
        out_shape=(sds(half_rows, dim), sds(half_rows, dim), sds(4 * half_rows, dim)),
        in_specs=[SCALAR] + [pl.BlockSpec()] * 7,
        compiler_params=params(),

        cost_estimate=cost(SECOND_EXPORTS_COST),
        name="second_exports",
    )(place, *tokens, level_gain, decay_log, keep1)
    first_sent = pl.pallas_call(
        first_merge_kernel,
        out_shape=tuple(
            sds(part_rows + (heads if part == 0 else 0), dim) for part in range(CHUNKS)
        ),
        in_specs=[SCALAR] + [pl.BlockSpec()] * 3 + [ANYWHERE],
        compiler_params=params(),
        cost_estimate=cost(FIRST_MERGE_COST),
        name="first_merge",
    )(place, decay_log, keep1, got1, keep2)
    first = [swap(block, side_swap) for block in first_sent]

    got2 = swap(after(send2, got1), core_swap)
    front = swap(after(bundle, got1), core_swap)


    inner = tok.bit_length()
    groups = 2 * CHUNKS

    def local(number, before, after):
        lanes = pl.BlockSpec((tok, part_rows), lambda g: (0, number))
        return pl.pallas_call(
            functools.partial(local_kernel, number * count),
            grid=(1,),
            out_shape=(sds(tok, heads * dim),) * 4 + (sds(inner, count, tok), sds(count, tok)),
            in_specs=[lanes] * 4
            + [
                pl.BlockSpec(level_gain.shape, lambda g: (0, 0, 0)),
                pl.BlockSpec(decay_log.shape, lambda g: (0, 0)),
            ]
            + [ANYWHERE] * (len(before) + len(after)),
            out_specs=(lanes,) * 4
            + (
                pl.BlockSpec((inner, count, tok), lambda g: (0, 0, 0)),
                pl.BlockSpec((count, tok), lambda g: (0, 0)),
            ),
            input_output_aliases={6 + at: at for at in range(len(before))},
            compiler_params=params(),

            cost_estimate=cost(LOCAL_COST),
            name="local",
        )(*tokens, level_gain, decay_log, *before, *after)

    def second_merge(part, after):
        chunk = pl.BlockSpec((part_rows, dim), lambda g: (part, 0))
        start = pl.BlockSpec((part_rows, dim), lambda g: (0, 0))
        return pl.pallas_call(
            functools.partial(second_merge_kernel, part),
            grid=(1,),
            out_shape=sds(part_rows, dim),
            in_specs=[
                SCALAR,
                pl.BlockSpec(decay_log.shape, lambda g: (0, 0)),
                pl.BlockSpec((heads, dim), lambda g: (half_rows // heads, 0)),
                chunk,
                chunk,
                start,
                ANYWHERE,
            ],
            out_specs=start,
            compiler_params=params(),
            cost_estimate=cost(SECOND_MERGE_COST),
            name="second_merge",
        )(place, decay_log, got1, keep2, got2, first[part], after)

    gain_rows, decay_rows = [], []
    acc = ()

    def more_local(number, *others):
        *done, gains, decays = local(number, acc, others)
        gain_rows.append(gains)
        decay_rows.append(decays)
        return done

    acc = more_local(0, first_sent[-1])
    acc = more_local(1)
    sent = [second_merge(0, decay_rows[-1])]
    sent.append(second_merge(1, sent[0]))
    second = [swap(block, middle_swap) for block in sent]
    left0, right0, pair_rows = pl.pallas_call(
        pair_kernel,
        grid=(1,),
        out_shape=(sds(tok, heads * dim),) * 2 + (sds(4 * heads, tok),),
        in_specs=[SCALAR]
        + [pl.BlockSpec()] * 6
        + [pl.BlockSpec((heads * dim, dim), lambda g: (0, 0)), ANYWHERE],
        compiler_params=params(),

        cost_estimate=cost(PAIR_USE_COST),
        name="pair_use",
    )(place, *tokens, level_gain, decay_log, front, sent[1])

    third = [swap(second[0], side_swap)]
    acc = more_local(2, pair_rows)
    first_over = [swap(after(block, decay_rows[2]), core_swap) for block in first]
    second_over = [swap(after(second[0], decay_rows[2]), core_swap)]
    second[1] = after(second[1], decay_rows[2])
    third.append(swap(second[1], side_swap))
    acc = more_local(3, second[1])
    second_over.append(swap(after(second[1], decay_rows[3]), core_swap))
    third_over = [swap(after(third[0], decay_rows[3]), core_swap)]

    def side_specs(part, mine):
        def block(place):
            core = lax.rem(place[0], 2)
            return (core if mine else 1 - core) * CHUNKS + part

        lanes = pl.BlockSpec((tok, part_rows), lambda g, place: (0, block(place)))
        level0 = pl.BlockSpec((part_rows, dim), lambda g, place: (block(place), 0))
        half_lanes = pl.BlockSpec((tok, part_rows), lambda g, place: (0, 0))
        start = pl.BlockSpec((part_rows, dim), lambda g, place: (0, 0))
        if mine:
            pair1 = pair2 = pl.BlockSpec((part_rows, dim), lambda g, place: (part, 0))
        else:
            pair2 = pl.BlockSpec((part_rows, dim), lambda g, place: (2 * groups - groups // 2 + part, 0))
            pair1 = pl.BlockSpec((part_rows, dim), lambda g, place: (groups + part, 0))
        return lanes, level0, half_lanes, start, pair1, pair2

    small = [
        whole(level_gain.shape),
        whole(decay_log.shape),
        pl.BlockSpec((heads, dim), lambda g, place: (half_rows // heads, 0)),
    ]
    used = {}
    for part in range(CHUNKS):
        for mine in (True, False):
            lanes, level0, half_lanes, start, pair1, pair2 = side_specs(part, mine)
            used[part, mine] = pl.pallas_call(
                functools.partial(first_use_kernel, part, mine),
                grid_spec=pltpu.PrefetchScalarGridSpec(
                    num_scalar_prefetch=1,
                    grid=(1,),
                    in_specs=[lanes] * 4 + small + [start] * 2 + [pair1, pair2, level0],
                    out_specs=(half_lanes,) * 2 + (whole((4 * count, tok)),),
                ),
                out_shape=(sds(tok, part_rows),) * 2 + (sds(4 * count, tok),),
                compiler_params=params(),

                cost_estimate=cost(FIRST_USE_COST),
                name="first_use",
            )(
                place,
                *tokens,
                level_gain,
                decay_log,
                got1,
                (first if mine else first_over)[part],
                (second if mine else second_over)[part],
                got1 if mine else front,
                got2 if mine else front,
                front,
            )

    results = ()
    last_rows = {}
    for part in range(CHUNKS):
        if part == 1:
            ready = [last_rows[0, False], used[1, True][2], used[1, False][2]]
            third_over.append(swap(after(third[1], *ready), core_swap))
        for mine in (True, False):
            lanes, level0, half_lanes, start, pair1, pair2 = side_specs(part, mine)
            left1, right1, _ = used[part, mine]
            before = len(results)
            *results, last_rows[part, mine] = pl.pallas_call(
                functools.partial(last_use_kernel, part, mine),
                grid_spec=pltpu.PrefetchScalarGridSpec(
                    num_scalar_prefetch=1,
                    grid=(1,),
                    in_specs=[lanes] * 4
                    + small
                    + [pl.BlockSpec((heads, dim), lambda g, place: (part_rows // heads, 0))]
                    + [start] * 2
                    + [pair1, level0]
                    + [lanes] * 2
                    + [half_lanes] * 2
                    + [lanes] * 4
                    + [ANYWHERE] * before,
                    out_specs=(lanes,) * 4 + (whole((4 * count, tok)),),
                ),
                out_shape=(sds(tok, heads * dim, dtype=BF16),) * 4 + (sds(4 * count, tok),),
                input_output_aliases={21 + at: at for at in range(before)},
                compiler_params=params(),

                cost_estimate=cost(LAST_USE_COST),
                name="last_use",
            )(
                place,
                *tokens,
                level_gain,
                decay_log,
                got1,
                first[0],
                (second if mine else second_over)[part],
                (third if mine else third_over)[part],
                got1 if mine else front,
                front,
                left0,
                right0,
                left1,
                right1,
                *acc,
                *results,
            )
    order = [(part, mine) for mine in (True, False) for part in range(CHUNKS)]
    rows = [used[key][2] for key in order] + [last_rows[key] for key in order]
    grad_gain, grad_decay = pl.pallas_call(
        gather_kernel,
        out_shape=(sds(*level_gain.shape), sds(heads, tok)),
        in_specs=[SCALAR] + [pl.BlockSpec()] * (1 + 2 * groups + len(rows)),
        compiler_params=params(),
        cost_estimate=cost(GATHER_COST),
        name="gather",
    )(place, pair_rows, *gain_rows, *decay_rows, *rows)
    return (*results, grad_gain, grad_decay)


def solution(mesh):
    placed = (
        P(("seq", "ctx"), None),
        P(("seq", "ctx"), None),
        P(("seq", "ctx"), None),
        P(None, None, ("seq", "ctx")),
        P(None, ("seq", "ctx")),
        P(("seq", "ctx"), None),
    )
    return jax.shard_map(
        line_device if mesh.shape["ctx"] == 8 else per_device,
        mesh=mesh,
        in_specs=placed,
        out_specs=(
            P(("seq", "ctx"), None),
            P(("seq", "ctx"), None),
            P(("seq", "ctx"), None),
            P(("seq", "ctx"), None),
            P(None, None, ("seq", "ctx")),
            P(None, ("seq", "ctx")),
        ),
        check_vma=False,
    )
```

```python
import functools

import jax
import jax.numpy as jnp
from jax import lax
from jax.experimental import pallas as pl
from jax.experimental.pallas import tpu as pltpu
from jax.sharding import PartitionSpec as P

TOP_ACCURACY = lax.Precision.HIGHEST


def from_partner(block, axis, distance):
    count = lax.axis_size(axis)
    route = []
    for low in range(count):
        high = low | 1 << distance
        if high != low and high < count:
            route += [(low, high), (high, low)]
    return lax.ppermute(block, axis, route)


def passed_along(value, axis, steps):
    count = lax.axis_size(axis)
    first, last = (max(0, -steps), min(count, count - steps))
    return lax.ppermute(value, axis, [(source, source + steps) for source in range(first, last)])


def level_table(tok, lvl_in):
    places = jnp.arange(tok, dtype=jnp.int32)
    mixing = jnp.bitwise_xor(places[:, None], places[None, :])
    table = jnp.zeros((tok, tok), jnp.int32)
    for power in range(lvl_in):
        table = table + (mixing >= 2**power).astype(jnp.int32)
    return table


def block_front(keys_h, value_rows_head, decay):
    running = jnp.cumsum(decay, axis=1)
    total_sum = running[:, -1]
    scaled_result = keys_h * jnp.exp(total_sum[:, None] - running)[:, :, None]
    return (
        jnp.einsum("ybu,ybe->yue", scaled_result, value_rows_head, precision=TOP_ACCURACY),
        total_sum,
    )


def block_output(queries_h, keys_h, value_rows_head, gain, decay, buckets):
    tok = queries_h.shape[1]
    lvl_in = tok.bit_length() - 1
    running = jnp.cumsum(decay, axis=1)
    places = jnp.arange(tok, dtype=jnp.int32)
    causal = places[:, None] >= places[None, :]
    spread_gap = jnp.where(causal[None], running[:, :, None] - running[:, None, :], 0.0)
    fading = jnp.where(causal[None], jnp.exp(spread_gap), 0.0)
    table = level_table(tok, lvl_in)
    picks = (table[None] == jnp.arange(lvl_in + 1, dtype=jnp.int32)[:, None, None]).astype(
        jnp.float32
    )
    weighting = jnp.einsum("lij,lhi->hij", picks, gain[: lvl_in + 1], precision=TOP_ACCURACY)
    scores = jnp.einsum("hik,hjk->hij", queries_h, keys_h, precision=TOP_ACCURACY)
    result = jnp.einsum(
        "hij,hjv->hiv", scores * weighting * fading, value_rows_head, precision=TOP_ACCURACY
    )
    lifted = queries_h * jnp.exp(running)[:, :, None]
    reach = gain[lvl_in + 1 :][:, :, :, None] * lifted[None]
    return result + jnp.einsum("jhik,jhkv->hiv", reach, buckets, precision=TOP_ACCURACY)


def merge_step(own_total, own_state, offset, other_total, other_state, is_upper):
    bucket = jnp.where(is_upper, jnp.exp(offset)[:, None, None] * other_state, 0.0)
    low_state = jnp.where(is_upper, other_state, own_state)
    high_state = jnp.where(is_upper, own_state, other_state)
    high_total = jnp.where(is_upper, own_total, other_total)
    merged = jnp.exp(high_total)[:, None, None] * low_state + high_state
    new_offset = offset + jnp.where(is_upper, other_total, 0.0)
    return (own_total + other_total, merged, new_offset, bucket)


def partner_grads(
    own_total, own_state, offset, other_total, g_total, g_state, g_offset, g_bucket, is_upper
):
    factor = jnp.exp(jnp.where(is_upper, own_total, other_total))
    d_other_state = jnp.where(
        is_upper,
        factor[:, None, None] * g_state + jnp.exp(offset)[:, None, None] * g_bucket,
        g_state,
    )
    lower_term = factor * jnp.sum(g_state * own_state, axis=(1, 2))
    d_other_total = g_total + jnp.where(is_upper, g_offset, lower_term)
    return (d_other_total, d_other_state)


def own_grads(
    own_total, offset, other_total, other_state, g_total, g_state, g_offset, g_bucket, is_upper
):
    factor = jnp.exp(jnp.where(is_upper, own_total, other_total))
    d_own_state = jnp.where(is_upper, g_state, factor[:, None, None] * g_state)
    upper_total = factor * jnp.sum(g_state * other_state, axis=(1, 2))
    d_own_total = g_total + jnp.where(is_upper, upper_total, 0.0)
    upper_offset = jnp.exp(offset) * jnp.sum(g_bucket * other_state, axis=(1, 2))
    d_offset = g_offset + jnp.where(is_upper, upper_offset, 0.0)
    return (d_own_total, d_own_state, d_offset)


def to_heads(block, heads):
    tokens, width = block.shape
    return block.reshape(tokens, heads, width // heads).transpose(1, 0, 2).astype(jnp.float32)


def from_heads(block):
    heads, tokens, head_dim = block.shape
    return block.transpose(1, 0, 2).reshape(tokens, heads * head_dim)


def per_device(queries, keys_in, value_input, level_gain, decay_log, out_grad):
    heads = decay_log.shape[0]
    query_h = to_heads(queries, heads)
    key_h = to_heads(keys_in, heads)
    value_h = to_heads(value_input, heads)
    cotangent = to_heads(out_grad, heads)
    count = lax.axis_size("ctx")
    depth = count.bit_length() - 1
    position = lax.axis_index("ctx")
    (state, total_sum), front_back = jax.vjp(block_front, key_h, value_h, decay_log)
    own_total = total_sum
    own_state = state
    offset = jnp.zeros_like(total_sum)
    saved = []
    found = []
    top_other = state
    for bit in range(depth):
        other_total, other_state = from_partner((own_total, own_state), "ctx", bit)
        is_upper = jnp.right_shift(position, bit) % 2 == 1
        saved.append((own_total, own_state, offset, other_total))
        if bit == depth - 1:
            top_other = other_state
        own_total, own_state, offset, bucket = merge_step(
            own_total, own_state, offset, other_total, other_state, is_upper
        )
        found.append(bucket)
    buckets = jnp.stack(found)
    mixed, out_back = jax.vjp(block_output, query_h, key_h, value_h, level_gain, decay_log, buckets)
    grad_query, grad_key, grad_value, grad_gain, grad_decay, bucket_gradient = out_back(cotangent)
    grad_total = jnp.zeros_like(total_sum)
    grad_state = jnp.zeros_like(state)
    grad_offset = jnp.zeros_like(total_sum)
    for bit in reversed(range(depth)):
        is_upper = jnp.right_shift(position, bit) % 2 == 1
        level_total, level_state, level_offset, level_other_total = saved[bit]
        d_other_total, d_other_state = partner_grads(
            level_total,
            level_state,
            level_offset,
            level_other_total,
            grad_total,
            grad_state,
            grad_offset,
            bucket_gradient[bit],
            is_upper,
        )
        if bit == depth - 1:
            back_total, back_state = passed_along(
                (d_other_total, d_other_state), "ctx", -(count // 2)
            )
            partner_state = top_other
        else:
            back_total, back_state, partner_state = from_partner(
                (d_other_total, d_other_state, level_state), "ctx", bit
            )
        d_own_total, d_own_state, d_offset = own_grads(
            level_total,
            level_offset,
            level_other_total,
            partner_state,
            grad_total,
            grad_state,
            grad_offset,
            bucket_gradient[bit],
            is_upper,
        )
        grad_total = d_own_total + back_total
        grad_state = d_own_state + back_state
        grad_offset = d_offset
    key_more, value_more, decay_more = front_back((grad_state, grad_total))
    return (
        from_heads(mixed).astype(jnp.bfloat16),
        from_heads(grad_query).astype(jnp.bfloat16),
        from_heads(grad_key + key_more).astype(jnp.bfloat16),
        from_heads(grad_value + value_more).astype(jnp.bfloat16),
        grad_gain,
        grad_decay + decay_more,
    )


F32 = jnp.float32
BF16 = jnp.bfloat16
CHUNKS = 2
NT = (((1,), (1,)), ((), ()))
TN = (((0,), (0,)), ((), ()))
NN = (((1,), (0,)), ((), ()))
NEVER = -1e30


def mxu(left, right, dims):
    return lax.dot_general(left, right, dims, preferred_element_type=F32)


def halves(value):
    high = value.astype(BF16)
    low = (value - high.astype(F32)).astype(BF16)
    return high, low


def split_rows(value):
    return jnp.concatenate(halves(value), axis=0)


def split_lanes(value):
    return jnp.concatenate(halves(value), axis=1)


def twice_rows(value):
    return jnp.concatenate([value, value], axis=0)


def twice_lanes(value):
    return jnp.concatenate([value, value], axis=1)


def running_decay(decay):
    tok = decay.shape[1]
    earlier = lax.broadcasted_iota(jnp.int32, (tok, tok), 0)
    later = lax.broadcasted_iota(jnp.int32, (tok, tok), 1)
    upto = (earlier <= later).astype(F32)
    return jnp.dot(decay, upto, precision=TOP_ACCURACY, preferred_element_type=F32)


def last_lane(running):
    return jnp.broadcast_to(running[:, running.shape[1] - 1 :], running.shape)


def columns(rows):
    count, tok = rows.shape
    if count < tok:
        rows = jnp.concatenate([rows, jnp.zeros((tok - count, tok), rows.dtype)], axis=0)
    return rows.T


def half_first(rows, core):
    half = rows.shape[0] // 2
    swapped = jnp.concatenate([rows[half:], rows[:half]], axis=0)
    return jnp.where(core == 0, rows, swapped)


def lane_block(ref, head, width):
    return ref[:, pl.ds(pl.multiple_of(head * width, width), width)]


def take_half(rows, core, part, count):
    half = rows.shape[0] // 2
    low = part * count
    return jnp.where(core == 0, rows[low : low + count], rows[half + low : half + low + count])


def outer_products(left, right, weight_column):
    turned = left.T
    return mxu(twice_lanes(turned), split_rows(right.astype(F32) * weight_column), NN)


def first_export_kernel(
    place, query, key, value, cotangent, gain, decay, send, keep, lefts, rights, gains, decays, sems
):
    position = place[0]
    core = position % 2
    chip = position // 2
    heads, tok = decay.shape
    width = query.shape[1]
    dim = width // heads
    half = heads // 2
    cross = gain.shape[0] - 3
    wide = half * dim
    state = chip % 2 == 0
    copies = []
    for side in range(2):
        lanes = pl.ds(pl.multiple_of((1 - core if side == 0 else core) * wide, wide), wide)
        for slot, (chosen, plain, into) in enumerate(((key, query, lefts), (value, cotangent, rights))):
            sem = sems.at[2 * side + slot]
            target = into.at[:, pl.ds(side * wide, wide)]

            @pl.when(state)
            def _(chosen=chosen, target=target, sem=sem, lanes=lanes):
                pltpu.make_async_copy(chosen.at[:, lanes], target, sem).start()

            @pl.when(jnp.logical_not(state))
            def _(plain=plain, target=target, sem=sem, lanes=lanes):
                pltpu.make_async_copy(plain.at[:, lanes], target, sem).start()

            copies.append(pltpu.make_async_copy(plain.at[:, lanes], target, sem))
    small = [
        pltpu.make_async_copy(decay, decays, sems.at[4]),
        pltpu.make_async_copy(gain.at[pl.ds(cross + 1, 2)], gains, sems.at[5]),
    ]
    for copy in small:
        copy.start()
    for copy in small:
        copy.wait()
    running = running_decay(decays[...])
    total = last_lane(running)
    lift = jnp.exp(running)
    weight = jnp.where(
        state, jnp.exp(total - running), jnp.where(chip == 1, gains[0], gains[1]) * lift
    )
    spread = columns(half_first(weight, 1 - core))
    send[pl.ds(half * dim, heads), :] = total
    for index in range(heads):
        if index % half == 0:
            for copy in copies[2 * (index // half) : 2 * (index // half) + 2]:
                copy.wait()
        lanes = slice(index * dim, (index + 1) * dim)
        rows = pl.ds(index % half * dim, dim)
        (send if index < half else keep)[rows, :] = outer_products(
            lefts[:, lanes], rights[:, lanes], spread[:, index : index + 1]
        )


def second_core(position):
    return jnp.bitwise_xor(position % 2, (position // 2 == 3).astype(jnp.int32))


def second_export_kernel(
    place, query, key, value, cotangent, gain, decay, keep1, after, *outs
):
    *sends, keep, bundle = outs
    position = place[0]
    core = second_core(position)
    chip = position // 2
    heads, tok = decay.shape
    dim = query.shape[1] // heads
    half = heads // 2
    cross = gain.shape[0] - 3
    running = running_decay(decay[...])
    lift = jnp.exp(running)
    fall = jnp.exp(last_lane(running) - running)
    state2 = chip == 1
    state0 = position % 2 == 0
    weight2 = jnp.where(state2, fall, jnp.where(chip == 2, gain[cross + 2], gain[cross + 1]) * lift)
    weight2 = jnp.where(chip == 0, 0.0, weight2)
    weight0 = jnp.where(state0, fall, gain[cross] * lift)
    spread = columns(jnp.concatenate([half_first(weight2, 1 - core), weight0], axis=0))
    bundle[pl.ds(heads * dim, half * dim), :] = keep1[...]
    count = half // len(sends)
    for index in range(heads):
        mine = index >= half
        head = (core if mine else 1 - core) * half + index % half
        q, k, v, o = (lane_block(ref, head, dim) for ref in (query, key, value, cotangent))
        second = outer_products(
            jnp.where(state2, k, q), jnp.where(state2, v, o), spread[:, index : index + 1]
        )
        if mine:
            keep[pl.ds(index % half * dim, dim), :] = second
            bundle[pl.ds((heads + index) * dim, dim), :] = second
        else:
            sends[index // count][pl.ds(index % count * dim, dim), :] = second
    for head in range(heads):
        lanes = slice(head * dim, (head + 1) * dim)
        q, k, v, o = (ref[:, lanes] for ref in (query, key, value, cotangent))
        bundle[pl.ds(head * dim, dim), :] = outer_products(
            jnp.where(state0, k, q),
            jnp.where(state0, v, o),
            spread[:, heads + head : heads + head + 1],
        )


def pair_factors(position, own_total, other_total, is_state):
    even = position % 2 == 0
    scale_own = is_state == even
    return (
        jnp.where(scale_own, jnp.exp(other_total), 1.0),
        jnp.where(scale_own, 1.0, jnp.exp(own_total)),
    )


def first_merge_kernel(place, decay, keep, got, *outs):
    position = place[0]
    chip = position // 2
    heads, tok = decay.shape
    half = heads // 2
    dim = keep.shape[0] // half
    own_total = last_lane(running_decay(decay[...]))
    other_total = got[pl.ds(half * dim, heads), :]
    own_factor, other_factor = pair_factors(position, own_total, other_total, chip % 2 == 0)
    own_factor = half_first(own_factor, position % 2)[:half]
    other_factor = half_first(other_factor, position % 2)[:half]
    count = half // len(outs)
    for part, out in enumerate(outs):
        for index in range(count):
            head = part * count + index
            rows = pl.ds(head * dim, dim)
            out[pl.ds(index * dim, dim), :] = (
                own_factor[head : head + 1] * keep[rows, :]
                + other_factor[head : head + 1] * got[rows, :]
            )
    outs[0][pl.ds(count * dim, heads), :] = own_total + other_total


def second_merge_kernel(part, place, decay, other_total, keep, got, first, *rest):
    out = rest[-1]
    position = place[0]
    chip = position // 2
    heads, tok = decay.shape
    half = heads // 2
    count = half // CHUNKS
    dim = out.shape[0] // count
    own_total = last_lane(running_decay(decay[...]))
    other_total = other_total[...]
    own_factor, other_factor = pair_factors(position, own_total, other_total, chip == 1)
    inner = (chip == 1) | (chip == 2)
    first_factor = jnp.where(inner, jnp.exp(own_total + other_total), 0.0)
    own_factor, other_factor, first_factor = (
        half_first(factor, second_core(position))[part * count : (part + 1) * count]
        for factor in (own_factor, other_factor, first_factor)
    )
    for index in range(count):
        rows = pl.ds(index * dim, dim)
        out[rows, :] = (
            own_factor[index : index + 1] * keep[rows, :]
            + other_factor[index : index + 1] * got[rows, :]
            + first_factor[index : index + 1] * first[rows, :]
        )


def lane_sums(value):
    ones = jnp.ones((2 * value.shape[1], value.shape[1]), BF16)
    return mxu(split_lanes(value), ones, NN)


def apply_state(left, right, state, weight):
    high, low = halves(state)
    first = mxu(twice_lanes(left), jnp.concatenate([high, low], axis=0), NN)
    second = mxu(twice_lanes(right), jnp.concatenate([high, low], axis=1), NT)
    sums = lane_sums(first * right.astype(F32))
    return weight * first, weight * second, sums


def local_kernel(start, query, key, value, cotangent, gain, decay, *rest):
    acc_out, acc_query, acc_key, acc_value, gain_rows, decay_rows = rest[-6:]
    tok = decay.shape[1]
    count = decay_rows.shape[0]
    dim = query.shape[1] // count
    inner_levels = tok.bit_length()
    running = running_decay(decay[...])
    spread = columns(running)
    source = lax.broadcasted_iota(jnp.int32, (tok, tok), 0)
    target = lax.broadcasted_iota(jnp.int32, (tok, tok), 1)
    mixing = jnp.bitwise_xor(source, target)
    level = jnp.zeros((tok, tok), jnp.int32)
    for power in range(inner_levels - 1):
        level = level + (mixing >= 2**power).astype(jnp.int32)
    level = jnp.where(source <= target, level, -1)
    causal = source <= target
    lane = lax.broadcasted_iota(jnp.int32, (tok, tok), 1)
    gathered = jnp.zeros((tok, tok), F32)
    for index in range(count):
        head = start + index
        lanes = slice(index * dim, (index + 1) * dim)
        q, k, v, o = (ref[:, lanes] for ref in (query, key, value, cotangent))
        scores = mxu(k, q, NT)
        pulls = mxu(v, o, NT)
        row = running[head : head + 1]
        fading = jnp.exp(jnp.where(causal, row - spread[:, head : head + 1], NEVER))
        weighting = jnp.zeros((tok, tok), F32)
        for place_in in range(inner_levels):
            weighting = jnp.where(
                level == place_in, gain[place_in, head : head + 1, :], weighting
            )
        weighting = weighting * fading
        mixing_part = scores * weighting
        score_grad = pulls * weighting
        product = scores * pulls * fading
        flow = jnp.zeros((1, tok), F32)
        for place_in in range(inner_levels):
            found = jnp.sum(jnp.where(level == place_in, product, 0.0), axis=0, keepdims=True)
            gain_rows[place_in, index : index + 1, :] = found
            if place_in > 0:
                flow = flow + gain[place_in, head : head + 1, :] * found
        decay_rows[index : index + 1, :] = flow
        left = jnp.where(level > 0, mixing_part * pulls, 0.0)
        gathered = jnp.where(lane == index, lane_sums(left), gathered)
        high, low = halves(mixing_part)
        acc_out[:, lanes] = mxu(jnp.concatenate([high, low], axis=0), twice_rows(v), TN)
        acc_value[:, lanes] = mxu(jnp.concatenate([high, low], axis=1), twice_rows(o), NN)
        high, low = halves(score_grad)
        acc_query[:, lanes] = mxu(jnp.concatenate([high, low], axis=0), twice_rows(k), TN)
        acc_key[:, lanes] = mxu(jnp.concatenate([high, low], axis=1), twice_rows(q), NN)
    decay_rows[...] = decay_rows[...] - gathered.T[:count]


def use_rows(rows_out, uses, gathered, extra):
    turned = gathered.T
    count = rows_out.shape[0] // 4
    decay_row = jnp.zeros((count, turned.shape[1]), F32)
    flow_row = extra
    for number, (forward, weight, lift) in enumerate(uses):
        sums = turned[number * count : (number + 1) * count]
        weighted = weight * sums
        decay_row = decay_row + jnp.where(forward, weighted, -weighted)
        flow_row = flow_row + jnp.where(forward, 0.0, weighted)
        rows_out[number * count : (number + 1) * count, :] = lift * sums
    rows_out[2 * count : 3 * count, :] = decay_row
    rows_out[3 * count : 4 * count, :] = flow_row


def pair_kernel(
    place, query, key, value, cotangent, gain, decay, level0, after, out_left, out_right, rows_out
):
    position = place[0]
    odd = position % 2 == 1
    heads, tok = decay.shape
    dim = query.shape[1] // heads
    running = running_decay(decay[...])
    lift = jnp.exp(running)
    cross = gain.shape[0] - 3
    weight = jnp.where(odd, gain[cross] * lift, jnp.exp(last_lane(running) - running))
    spread = columns(weight)
    lane = lax.broadcasted_iota(jnp.int32, (tok, tok), 1)
    gathered = jnp.zeros((tok, tok), F32)
    for head in range(heads):
        lanes = slice(head * dim, (head + 1) * dim)
        q, k, v, o = (ref[:, lanes] for ref in (query, key, value, cotangent))
        left, right, sums = apply_state(
            jnp.where(odd, q, k),
            jnp.where(odd, o, v),
            level0[pl.ds(head * dim, dim), :],
            spread[:, head : head + 1],
        )
        out_left[:, lanes] = left
        out_right[:, lanes] = right
        gathered = jnp.where(lane == head, sums, gathered)
    use_rows(rows_out, ((odd, weight, jnp.where(odd, lift, 0.0)),), gathered, jnp.zeros((heads, tok), F32))


def first_use_kernel(
    part,
    mine,
    place,
    query,
    key,
    value,
    cotangent,
    gain,
    decay,
    other_total,
    first,
    second,
    pair1,
    pair2_got,
    pair2_kept,
    level0,
    out_left,
    out_right,
    rows_out,
):
    position = place[0]
    core = position % 2
    side = core if mine else 1 - core
    chip = position // 2
    heads, tok = decay.shape
    count = heads // 2 // CHUNKS
    dim = query.shape[1] // count
    cross = gain.shape[0] - 3
    running = running_decay(decay[...])
    total = last_lane(running)
    other = other_total[...]
    odd = core == 1
    forward = chip != 0
    offset = jnp.where(forward == odd, other, 0.0)
    lift = jnp.exp(running + offset)
    weight = jnp.where(
        forward,
        jnp.where(chip == 2, gain[cross + 2], gain[cross + 1]) * lift,
        jnp.exp(total - running + offset),
    )
    pair_flow = jnp.where(forward != odd, jnp.exp(total), 0.0)
    chip_flow = jnp.where((chip == 1) | (chip == 2), jnp.exp(total + other), 0.0)
    lift, weight, pair_flow, chip_flow = (
        take_half(rows, side, part, count) for rows in (lift, weight, pair_flow, chip_flow)
    )
    spread = columns(weight)
    lane = lax.broadcasted_iota(jnp.int32, (tok, tok), 1)
    gathered = jnp.zeros((tok, tok), F32)
    flows = []
    for index in range(count):
        lanes = slice(index * dim, (index + 1) * dim)
        rows = pl.ds(index * dim, dim)
        one = slice(index, index + 1)
        q, k, v, o = (ref[:, lanes] for ref in (query, key, value, cotangent))
        state = jnp.where(chip == 2, second[rows, :], first[rows, :])
        pair2 = jnp.where((chip == 3) == mine, pair2_kept[rows, :], pair2_got[rows, :])
        partner = jnp.where(odd, level0[rows, :], jnp.where(chip == 1, pair1[rows, :], pair2))
        flows.append(
            pair_flow[one] * jnp.sum(state * partner, axis=0, keepdims=True)
            + chip_flow[one] * jnp.sum(first[rows, :] * second[rows, :], axis=0, keepdims=True)
        )
        left, right, sums = apply_state(
            jnp.where(forward, q, k), jnp.where(forward, o, v), state, spread[:, one]
        )
        out_left[:, lanes] = left
        out_right[:, lanes] = right
        gathered = jnp.where(lane == index, sums, gathered)
    use_rows(rows_out, ((forward, weight, lift),), gathered, jnp.concatenate(flows, axis=0))


def last_use_kernel(
    part,
    mine,
    place,
    query,
    key,
    value,
    cotangent,
    gain,
    decay,
    other_total,
    chip_total,
    second,
    third,
    pair1,
    level0,
    left0,
    right0,
    left1,
    right1,
    part_out,
    part_query,
    part_key,
    part_value,
    *rest,
):
    out_mixed, out_query, out_key, out_value, rows_out = rest[-5:]
    position = place[0]
    core = position % 2
    side = core if mine else 1 - core
    chip = position // 2
    heads, tok = decay.shape
    count = heads // 2 // CHUNKS
    dim = query.shape[1] // count
    cross = gain.shape[0] - 3
    running = running_decay(decay[...])
    total = last_lane(running)
    odd = core == 1
    forward1 = chip != 0
    forward = chip == 3
    chip_offset = jnp.where((chip == 0) | (chip == 3), chip_total[...], 0.0)
    offset = jnp.where(forward == odd, other_total[...], 0.0) + chip_offset
    lift = jnp.exp(running + offset)
    weight = jnp.where(forward, gain[cross + 2] * lift, jnp.exp(total - running + offset))
    pair_flow = jnp.where(forward != odd, jnp.exp(total + chip_offset), 0.0)
    lift, weight, pair_flow = (
        take_half(rows, side, part, count) for rows in (lift, weight, pair_flow)
    )
    spread = columns(weight)
    lane = lax.broadcasted_iota(jnp.int32, (tok, tok), 1)
    gathered = jnp.zeros((tok, tok), F32)
    flows = []
    for index in range(count):
        lanes = slice(index * dim, (index + 1) * dim)
        rows = pl.ds(index * dim, dim)
        one = slice(index, index + 1)
        q, k, v, o = (ref[:, lanes] for ref in (query, key, value, cotangent))
        state = jnp.where(chip == 1, second[rows, :], third[rows, :])
        partner = jnp.where(odd, level0[rows, :], pair1[rows, :])
        flows.append(pair_flow[one] * jnp.sum(state * partner, axis=0, keepdims=True))
        left, right, sums = apply_state(
            jnp.where(forward, q, k), jnp.where(forward, o, v), state, spread[:, one]
        )
        gathered = jnp.where(lane == index, sums, gathered)
        forward_left = jnp.where(odd, left0[:, lanes], 0.0)
        forward_right = jnp.where(odd, right0[:, lanes], 0.0)
        back_left = jnp.where(odd, 0.0, left0[:, lanes])
        back_right = jnp.where(odd, 0.0, right0[:, lanes])
        for is_forward, a_left, a_right in (
            (forward1, left1[:, lanes], right1[:, lanes]),
            (forward, left, right),
        ):
            forward_left = forward_left + jnp.where(is_forward, a_left, 0.0)
            forward_right = forward_right + jnp.where(is_forward, a_right, 0.0)
            back_left = back_left + jnp.where(is_forward, 0.0, a_left)
            back_right = back_right + jnp.where(is_forward, 0.0, a_right)
        out_mixed[:, lanes] = (part_out[:, lanes] + forward_left).astype(BF16)
        out_query[:, lanes] = (part_query[:, lanes] + forward_right).astype(BF16)
        out_value[:, lanes] = (part_value[:, lanes] + back_left).astype(BF16)
        out_key[:, lanes] = (part_key[:, lanes] + back_right).astype(BF16)
    use_rows(rows_out, ((forward, weight, lift),), gathered, jnp.concatenate(flows, axis=0))


def gather_kernel(place, pair_rows, *rest):
    groups = 2 * CHUNKS
    gain_rows, decay_rows = rest[:groups], rest[groups : 2 * groups]
    parts, (grad_gain, grad_decay) = rest[2 * groups : -2], rest[-2:]
    position = place[0]
    core = position % 2
    chip = position // 2
    levels, heads, tok = grad_gain.shape
    count = heads // 2 // CHUNKS

    def natural(refs, kind):
        rows = [ref[kind * count : (kind + 1) * count, :] for ref in refs]
        return half_first(jnp.concatenate(rows, axis=0), core)

    def of_pair(kind):
        return pair_rows[kind * heads : (kind + 1) * heads, :]

    for place_in in range(levels - 3):
        grad_gain[place_in] = jnp.concatenate([ref[place_in] for ref in gain_rows], axis=0)
    first, second = natural(parts[:groups], 0), natural(parts[groups:], 0)
    grad_gain[levels - 3] = of_pair(0)
    grad_gain[levels - 2] = jnp.where(chip % 2 == 1, first, 0.0)
    grad_gain[levels - 1] = jnp.where(chip == 2, first, jnp.where(chip == 3, second, 0.0))
    own = jnp.concatenate([ref[...] for ref in decay_rows], axis=0)
    own = own + of_pair(2) + natural(parts[:groups], 2) + natural(parts[groups:], 2)
    later = of_pair(3) + natural(parts[:groups], 3) + natural(parts[groups:], 3)
    upper = lax.broadcasted_iota(jnp.int32, (tok, tok), 0)
    lower = lax.broadcasted_iota(jnp.int32, (tok, tok), 1)
    after = (upper >= lower).astype(F32)
    every = jnp.ones((tok, tok), F32)
    grad_decay[...] = jnp.dot(
        own, after, precision=TOP_ACCURACY, preferred_element_type=F32
    ) + jnp.dot(later, every, precision=TOP_ACCURACY, preferred_element_type=F32)


def after(value, *others):
    return lax.optimization_barrier((value, *others))[0]


def sds(*shape, dtype=F32):
    return jax.ShapeDtypeStruct(shape, dtype)


def params(mebibytes=24):
    return pltpu.CompilerParams(vmem_limit_bytes=mebibytes * 1024 * 1024)


SCALAR = pl.BlockSpec(memory_space=pltpu.SMEM)
ANYWHERE = pl.BlockSpec(memory_space=pl.ANY)
IN_HBM = pl.BlockSpec(memory_space=pltpu.HBM)


def whole(shape):
    return pl.BlockSpec(shape, lambda g, place: (0,) * len(shape))


FIRST_EXPORTS_COST = 52800000000
FIRST_MERGE_COST = 4800000000
SECOND_EXPORTS_COST = 1500000000
LOCAL_COST = (1570000000, 1570000000, 25120000000, 25120000000)
SECOND_MERGE_COST = 4800000000
PAIR_USE_COST = 28800000000
FIRST_USE_COST = 10720000000
LAST_USE_COST = 24000000000
GATHER_COST = 12800000000


def cost(flops):
    return pl.CostEstimate(flops=flops, bytes_accessed=1, transcendentals=0)


def line_device(queries, keys_in, value_input, level_gain, decay_log, out_grad):
    heads, tok = decay_log.shape
    dim = queries.shape[1] // heads
    half = heads // 2
    count = half // CHUNKS
    part_rows = count * dim
    half_rows = half * dim
    place = lax.axis_index("ctx").astype(jnp.int32).reshape(1)
    tokens = (queries, keys_in, value_input, out_grad)
    core_swap = [(at, at ^ 1) for at in range(8)]
    side_swap = [(at, at ^ 2) for at in range(8)]
    middle_swap = [(0, 1), (1, 0), (2, 4), (4, 2), (3, 5), (5, 3), (6, 7), (7, 6)]

    def swap(block, route):
        return lax.ppermute(block, "ctx", route)

    send1, keep1 = pl.pallas_call(
        first_export_kernel,
        out_shape=(sds(half_rows + heads, dim), sds(half_rows, dim)),
        in_specs=[SCALAR] + [IN_HBM] * 6,
        scratch_shapes=[
            pltpu.VMEM((tok, heads * dim), BF16),
            pltpu.VMEM((tok, heads * dim), BF16),
            pltpu.VMEM((2, heads, tok), F32),
            pltpu.VMEM((heads, tok), F32),
            pltpu.SemaphoreType.DMA((6,)),
        ],
        compiler_params=params(62),

        cost_estimate=cost(FIRST_EXPORTS_COST),
        name="first_exports",
    )(place, *tokens, level_gain, decay_log)
    got1 = swap(send1, core_swap)
    first_sent = pl.pallas_call(
        first_merge_kernel,
        out_shape=tuple(
            sds(part_rows + (heads if part == 0 else 0), dim) for part in range(CHUNKS)
        ),
        in_specs=[SCALAR] + [pl.BlockSpec()] * 3,
        compiler_params=params(),
        cost_estimate=cost(FIRST_MERGE_COST),
        name="first_merge",
    )(place, decay_log, keep1, got1)
    first = [swap(block, side_swap) for block in first_sent]

    inner = tok.bit_length()
    groups = 2 * CHUNKS

    def local(number, before, after):
        lanes = pl.BlockSpec((tok, part_rows), lambda g: (0, number))
        return pl.pallas_call(
            functools.partial(local_kernel, number * count),
            grid=(1,),
            out_shape=(sds(tok, heads * dim),) * 4 + (sds(inner, count, tok), sds(count, tok)),
            in_specs=[lanes] * 4
            + [
                pl.BlockSpec(level_gain.shape, lambda g: (0, 0, 0)),
                pl.BlockSpec(decay_log.shape, lambda g: (0, 0)),
            ]
            + [ANYWHERE] * (len(before) + len(after)),
            out_specs=(lanes,) * 4
            + (
                pl.BlockSpec((inner, count, tok), lambda g: (0, 0, 0)),
                pl.BlockSpec((count, tok), lambda g: (0, 0)),
            ),
            input_output_aliases={6 + at: at for at in range(len(before))},
            compiler_params=params(),

            cost_estimate=cost(LOCAL_COST[number]),
            name="local",
        )(*tokens, level_gain, decay_log, *before, *after)

    gain_rows, decay_rows = [], []
    acc = ()

    def more_local(number, *others):
        *done, gains, decays = local(number, acc, others)
        gain_rows.append(gains)
        decay_rows.append(decays)
        return done

    acc = more_local(0, first_sent[-1])
    *send2, keep2, bundle = pl.pallas_call(
        second_export_kernel,
        out_shape=(sds(part_rows, dim),) * CHUNKS + (sds(half_rows, dim), sds(4 * half_rows, dim)),
        in_specs=[SCALAR] + [pl.BlockSpec()] * 7 + [ANYWHERE],
        compiler_params=params(),

        cost_estimate=cost(SECOND_EXPORTS_COST),
        name="second_exports",
    )(place, *tokens, level_gain, decay_log, keep1, decay_rows[0])
    got2 = [swap(block, core_swap) for block in send2]


    def second_merge(part, *after):
        chunk = pl.BlockSpec((part_rows, dim), lambda g: (part, 0))
        start = pl.BlockSpec((part_rows, dim), lambda g: (0, 0))
        return pl.pallas_call(
            functools.partial(second_merge_kernel, part),
            grid=(1,),
            out_shape=sds(part_rows, dim),
            in_specs=[
                SCALAR,
                pl.BlockSpec(decay_log.shape, lambda g: (0, 0)),
                pl.BlockSpec((heads, dim), lambda g: (half_rows // heads, 0)),
                chunk,
                start,
                start,
            ]
            + [ANYWHERE] * len(after),
            out_specs=start,
            compiler_params=params(),
            cost_estimate=cost(SECOND_MERGE_COST),
            name="second_merge",
        )(place, decay_log, got1, keep2, got2[part], first[part], *after)

    acc = more_local(1, keep2)
    sent = [second_merge(0, decay_rows[1], *got2[1:])]
    acc = more_local(2, sent[0])
    sent.append(second_merge(1, decay_rows[2]))
    front = swap(after(bundle, sent[1]), core_swap)
    second = [swap(block, middle_swap) for block in sent]
    acc = more_local(3, second[0])
    left0, right0, pair_rows = pl.pallas_call(
        pair_kernel,
        grid=(1,),
        out_shape=(sds(tok, heads * dim),) * 2 + (sds(4 * heads, tok),),
        in_specs=[SCALAR]
        + [pl.BlockSpec()] * 6
        + [pl.BlockSpec((heads * dim, dim), lambda g: (0, 0)), ANYWHERE],
        compiler_params=params(),

        cost_estimate=cost(PAIR_USE_COST),
        name="pair_use",
    )(place, *tokens, level_gain, decay_log, front, decay_rows[3])

    third = [swap(second[0], side_swap)]
    first_over = [swap(after(block, pair_rows), core_swap) for block in first]
    second_over = [swap(after(second[0], pair_rows), core_swap)]
    second[1] = after(second[1], pair_rows)
    third.append(swap(second[1], side_swap))
    second_over.append(swap(second[1], core_swap))
    third_over = [swap(after(third[0], pair_rows), core_swap)]

    def side_specs(part, mine):
        def block(place):
            core = lax.rem(place[0], 2)
            return (core if mine else 1 - core) * CHUNKS + part

        lanes = pl.BlockSpec((tok, part_rows), lambda g, place: (0, block(place)))
        level0 = pl.BlockSpec((part_rows, dim), lambda g, place: (block(place), 0))
        half_lanes = pl.BlockSpec((tok, part_rows), lambda g, place: (0, 0))
        start = pl.BlockSpec((part_rows, dim), lambda g, place: (0, 0))
        pair_got = pl.BlockSpec((part_rows, dim), lambda g, place: (part, 0))
        pair1 = pl.BlockSpec((part_rows, dim), lambda g, place: (groups + part, 0))
        pair2 = pl.BlockSpec((part_rows, dim), lambda g, place: (groups + CHUNKS + part, 0))
        return lanes, level0, half_lanes, start, pair_got if mine else pair1, pair2

    small = [
        whole(level_gain.shape),
        whole(decay_log.shape),
        pl.BlockSpec((heads, dim), lambda g, place: (half_rows // heads, 0)),
    ]
    used = {}
    for part in range(CHUNKS):
        for mine in (True, False):
            lanes, level0, half_lanes, start, pair1, pair2 = side_specs(part, mine)
            used[part, mine] = pl.pallas_call(
                functools.partial(first_use_kernel, part, mine),
                grid_spec=pltpu.PrefetchScalarGridSpec(
                    num_scalar_prefetch=1,
                    grid=(1,),
                    in_specs=[lanes] * 4 + small + [start] * 2 + [pair1, start, pair2, level0],
                    out_specs=(half_lanes,) * 2 + (whole((4 * count, tok)),),
                ),
                out_shape=(sds(tok, part_rows),) * 2 + (sds(4 * count, tok),),
                compiler_params=params(),

                cost_estimate=cost(FIRST_USE_COST),
                name="first_use",
            )(
                place,
                *tokens,
                level_gain,
                decay_log,
                got1,
                (first if mine else first_over)[part],
                (second if mine else second_over)[part],
                got1 if mine else front,
                got2[part],
                front,
                front,
            )

    results = ()
    last_rows = {}
    for part in range(CHUNKS):
        if part == 1:
            ready = [last_rows[0, False], used[1, True][2], used[1, False][2]]
            third_over.append(swap(after(third[1], *ready), core_swap))
        for mine in (True, False):
            lanes, level0, half_lanes, start, pair1, pair2 = side_specs(part, mine)
            left1, right1, _ = used[part, mine]
            before = len(results)
            *results, last_rows[part, mine] = pl.pallas_call(
                functools.partial(last_use_kernel, part, mine),
                grid_spec=pltpu.PrefetchScalarGridSpec(
                    num_scalar_prefetch=1,
                    grid=(1,),
                    in_specs=[lanes] * 4
                    + small
                    + [pl.BlockSpec((heads, dim), lambda g, place: (part_rows // heads, 0))]
                    + [start] * 2
                    + [pair1, level0]
                    + [lanes] * 2
                    + [half_lanes] * 2
                    + [lanes] * 4
                    + [ANYWHERE] * before,
                    out_specs=(lanes,) * 4 + (whole((4 * count, tok)),),
                ),
                out_shape=(sds(tok, heads * dim, dtype=BF16),) * 4 + (sds(4 * count, tok),),
                input_output_aliases={21 + at: at for at in range(before)},
                compiler_params=params(),

                cost_estimate=cost(LAST_USE_COST),
                name="last_use",
            )(
                place,
                *tokens,
                level_gain,
                decay_log,
                got1,
                first[0],
                (second if mine else second_over)[part],
                (third if mine else third_over)[part],
                got1 if mine else front,
                front,
                left0,
                right0,
                left1,
                right1,
                *acc,
                *results,
            )
    order = [(part, mine) for mine in (True, False) for part in range(CHUNKS)]
    rows = [used[key][2] for key in order] + [last_rows[key] for key in order]
    grad_gain, grad_decay = pl.pallas_call(
        gather_kernel,
        out_shape=(sds(*level_gain.shape), sds(heads, tok)),
        in_specs=[SCALAR] + [pl.BlockSpec()] * (1 + 2 * groups + len(rows)),
        compiler_params=params(),
        cost_estimate=cost(GATHER_COST),
        name="gather",
    )(place, pair_rows, *gain_rows, *decay_rows, *rows)
    return (*results, grad_gain, grad_decay)


def solution(mesh):
    placed = (
        P(("seq", "ctx"), None),
        P(("seq", "ctx"), None),
        P(("seq", "ctx"), None),
        P(None, None, ("seq", "ctx")),
        P(None, ("seq", "ctx")),
        P(("seq", "ctx"), None),
    )
    return jax.shard_map(
        line_device if mesh.shape["ctx"] == 8 else per_device,
        mesh=mesh,
        in_specs=placed,
        out_specs=(
            P(("seq", "ctx"), None),
            P(("seq", "ctx"), None),
            P(("seq", "ctx"), None),
            P(("seq", "ctx"), None),
            P(None, None, ("seq", "ctx")),
            P(None, ("seq", "ctx")),
        ),
        check_vma=False,
    )
```

```python
import functools

import jax
import jax.numpy as jnp
from jax import lax
from jax.experimental import pallas as pl
from jax.experimental.pallas import tpu as pltpu
from jax.sharding import PartitionSpec as P

TOP_ACCURACY = lax.Precision.HIGHEST


def from_partner(block, axis, distance):
    count = lax.axis_size(axis)
    route = []
    for low in range(count):
        high = low | 1 << distance
        if high != low and high < count:
            route += [(low, high), (high, low)]
    return lax.ppermute(block, axis, route)


def passed_along(value, axis, steps):
    count = lax.axis_size(axis)
    first, last = (max(0, -steps), min(count, count - steps))
    return lax.ppermute(value, axis, [(source, source + steps) for source in range(first, last)])


def level_table(tok, lvl_in):
    places = jnp.arange(tok, dtype=jnp.int32)
    mixing = jnp.bitwise_xor(places[:, None], places[None, :])
    table = jnp.zeros((tok, tok), jnp.int32)
    for power in range(lvl_in):
        table = table + (mixing >= 2**power).astype(jnp.int32)
    return table


def block_front(keys_h, value_rows_head, decay):
    running = jnp.cumsum(decay, axis=1)
    total_sum = running[:, -1]
    scaled_result = keys_h * jnp.exp(total_sum[:, None] - running)[:, :, None]
    return (
        jnp.einsum("ybu,ybe->yue", scaled_result, value_rows_head, precision=TOP_ACCURACY),
        total_sum,
    )


def block_output(queries_h, keys_h, value_rows_head, gain, decay, buckets):
    tok = queries_h.shape[1]
    lvl_in = tok.bit_length() - 1
    running = jnp.cumsum(decay, axis=1)
    places = jnp.arange(tok, dtype=jnp.int32)
    causal = places[:, None] >= places[None, :]
    spread_gap = jnp.where(causal[None], running[:, :, None] - running[:, None, :], 0.0)
    fading = jnp.where(causal[None], jnp.exp(spread_gap), 0.0)
    table = level_table(tok, lvl_in)
    picks = (table[None] == jnp.arange(lvl_in + 1, dtype=jnp.int32)[:, None, None]).astype(
        jnp.float32
    )
    weighting = jnp.einsum("lij,lhi->hij", picks, gain[: lvl_in + 1], precision=TOP_ACCURACY)
    scores = jnp.einsum("hik,hjk->hij", queries_h, keys_h, precision=TOP_ACCURACY)
    result = jnp.einsum(
        "hij,hjv->hiv", scores * weighting * fading, value_rows_head, precision=TOP_ACCURACY
    )
    lifted = queries_h * jnp.exp(running)[:, :, None]
    reach = gain[lvl_in + 1 :][:, :, :, None] * lifted[None]
    return result + jnp.einsum("jhik,jhkv->hiv", reach, buckets, precision=TOP_ACCURACY)


def merge_step(own_total, own_state, offset, other_total, other_state, is_upper):
    bucket = jnp.where(is_upper, jnp.exp(offset)[:, None, None] * other_state, 0.0)
    low_state = jnp.where(is_upper, other_state, own_state)
    high_state = jnp.where(is_upper, own_state, other_state)
    high_total = jnp.where(is_upper, own_total, other_total)
    merged = jnp.exp(high_total)[:, None, None] * low_state + high_state
    new_offset = offset + jnp.where(is_upper, other_total, 0.0)
    return (own_total + other_total, merged, new_offset, bucket)


def partner_grads(
    own_total, own_state, offset, other_total, g_total, g_state, g_offset, g_bucket, is_upper
):
    factor = jnp.exp(jnp.where(is_upper, own_total, other_total))
    d_other_state = jnp.where(
        is_upper,
        factor[:, None, None] * g_state + jnp.exp(offset)[:, None, None] * g_bucket,
        g_state,
    )
    lower_term = factor * jnp.sum(g_state * own_state, axis=(1, 2))
    d_other_total = g_total + jnp.where(is_upper, g_offset, lower_term)
    return (d_other_total, d_other_state)


def own_grads(
    own_total, offset, other_total, other_state, g_total, g_state, g_offset, g_bucket, is_upper
):
    factor = jnp.exp(jnp.where(is_upper, own_total, other_total))
    d_own_state = jnp.where(is_upper, g_state, factor[:, None, None] * g_state)
    upper_total = factor * jnp.sum(g_state * other_state, axis=(1, 2))
    d_own_total = g_total + jnp.where(is_upper, upper_total, 0.0)
    upper_offset = jnp.exp(offset) * jnp.sum(g_bucket * other_state, axis=(1, 2))
    d_offset = g_offset + jnp.where(is_upper, upper_offset, 0.0)
    return (d_own_total, d_own_state, d_offset)


def to_heads(block, heads):
    tokens, width = block.shape
    return block.reshape(tokens, heads, width // heads).transpose(1, 0, 2).astype(jnp.float32)


def from_heads(block):
    heads, tokens, head_dim = block.shape
    return block.transpose(1, 0, 2).reshape(tokens, heads * head_dim)


def per_device(queries, keys_in, value_input, level_gain, decay_log, out_grad):
    heads = decay_log.shape[0]
    query_h = to_heads(queries, heads)
    key_h = to_heads(keys_in, heads)
    value_h = to_heads(value_input, heads)
    cotangent = to_heads(out_grad, heads)
    count = lax.axis_size("ctx")
    depth = count.bit_length() - 1
    position = lax.axis_index("ctx")
    (state, total_sum), front_back = jax.vjp(block_front, key_h, value_h, decay_log)
    own_total = total_sum
    own_state = state
    offset = jnp.zeros_like(total_sum)
    saved = []
    found = []
    top_other = state
    for bit in range(depth):
        other_total, other_state = from_partner((own_total, own_state), "ctx", bit)
        is_upper = jnp.right_shift(position, bit) % 2 == 1
        saved.append((own_total, own_state, offset, other_total))
        if bit == depth - 1:
            top_other = other_state
        own_total, own_state, offset, bucket = merge_step(
            own_total, own_state, offset, other_total, other_state, is_upper
        )
        found.append(bucket)
    buckets = jnp.stack(found)
    mixed, out_back = jax.vjp(block_output, query_h, key_h, value_h, level_gain, decay_log, buckets)
    grad_query, grad_key, grad_value, grad_gain, grad_decay, bucket_gradient = out_back(cotangent)
    grad_total = jnp.zeros_like(total_sum)
    grad_state = jnp.zeros_like(state)
    grad_offset = jnp.zeros_like(total_sum)
    for bit in reversed(range(depth)):
        is_upper = jnp.right_shift(position, bit) % 2 == 1
        level_total, level_state, level_offset, level_other_total = saved[bit]
        d_other_total, d_other_state = partner_grads(
            level_total,
            level_state,
            level_offset,
            level_other_total,
            grad_total,
            grad_state,
            grad_offset,
            bucket_gradient[bit],
            is_upper,
        )
        if bit == depth - 1:
            back_total, back_state = passed_along(
                (d_other_total, d_other_state), "ctx", -(count // 2)
            )
            partner_state = top_other
        else:
            back_total, back_state, partner_state = from_partner(
                (d_other_total, d_other_state, level_state), "ctx", bit
            )
        d_own_total, d_own_state, d_offset = own_grads(
            level_total,
            level_offset,
            level_other_total,
            partner_state,
            grad_total,
            grad_state,
            grad_offset,
            bucket_gradient[bit],
            is_upper,
        )
        grad_total = d_own_total + back_total
        grad_state = d_own_state + back_state
        grad_offset = d_offset
    key_more, value_more, decay_more = front_back((grad_state, grad_total))
    return (
        from_heads(mixed).astype(jnp.bfloat16),
        from_heads(grad_query).astype(jnp.bfloat16),
        from_heads(grad_key + key_more).astype(jnp.bfloat16),
        from_heads(grad_value + value_more).astype(jnp.bfloat16),
        grad_gain,
        grad_decay + decay_more,
    )


F32 = jnp.float32
BF16 = jnp.bfloat16
NT = (((1,), (1,)), ((), ()))
TN = (((0,), (0,)), ((), ()))
NN = (((1,), (0,)), ((), ()))
NEVER = -1e30


def mxu(left, right, dims):
    return lax.dot_general(left, right, dims, preferred_element_type=F32)


def halves(value):
    high = value.astype(BF16)
    low = (value - high.astype(F32)).astype(BF16)
    return high, low


def split_rows(value):
    return jnp.concatenate(halves(value), axis=0)


def split_lanes(value):
    return jnp.concatenate(halves(value), axis=1)


def twice_rows(value):
    return jnp.concatenate([value, value], axis=0)


def twice_lanes(value):
    return jnp.concatenate([value, value], axis=1)


def running_decay(decay):
    tok = decay.shape[1]
    earlier = lax.broadcasted_iota(jnp.int32, (tok, tok), 0)
    later = lax.broadcasted_iota(jnp.int32, (tok, tok), 1)
    upto = (earlier <= later).astype(F32)
    return jnp.dot(decay, upto, precision=TOP_ACCURACY, preferred_element_type=F32)


def last_lane(running):
    return jnp.broadcast_to(running[:, running.shape[1] - 1 :], running.shape)


def columns(rows):
    count, tok = rows.shape
    if count < tok:
        rows = jnp.concatenate([rows, jnp.zeros((tok - count, tok), rows.dtype)], axis=0)
    return rows.T


def half_first(rows, core):
    half = rows.shape[0] // 2
    swapped = jnp.concatenate([rows[half:], rows[:half]], axis=0)
    return jnp.where(core == 0, rows, swapped)


def lane_block(ref, head, width):
    return ref[:, pl.ds(pl.multiple_of(head * width, width), width)]


def take_half(rows, core, low, count):
    half = rows.shape[0] // 2
    return jnp.where(core == 0, rows[low : low + count], rows[half + low : half + low + count])


def outer_products(left, right, weight_column):
    turned = left.T
    return mxu(twice_lanes(turned), split_rows(right.astype(F32) * weight_column), NN)


def first_export_kernel(
    place, query, key, value, cotangent, gain, decay, send, keep, *rest
):
    kept, (lefts, rights, sems) = rest[:6], rest[6:]
    position = place[0]
    core = position % 2
    chip = position // 2
    heads, tok = decay.shape
    width = query.shape[1]
    dim = width // heads
    half = heads // 2
    cross = gain.shape[0] - 3
    wide = half * dim
    state = chip % 2 == 0
    copies = []
    for side in range(2):
        lanes = pl.ds(pl.multiple_of((1 - core if side == 0 else core) * wide, wide), wide)
        for slot, (chosen, plain, into) in enumerate(((key, query, lefts), (value, cotangent, rights))):
            sem = sems.at[2 * side + slot]
            target = into.at[:, pl.ds(side * wide, wide)]

            @pl.when(state)
            def _(chosen=chosen, target=target, sem=sem, lanes=lanes):
                pltpu.make_async_copy(chosen.at[:, lanes], target, sem).start()

            @pl.when(jnp.logical_not(state))
            def _(plain=plain, target=target, sem=sem, lanes=lanes):
                pltpu.make_async_copy(plain.at[:, lanes], target, sem).start()

            copies.append(pltpu.make_async_copy(plain.at[:, lanes], target, sem))
    sources = (query, key, value, cotangent, gain, decay)
    moves = [
        pltpu.make_async_copy(source, target, sems.at[4 + number])
        for number, (source, target) in enumerate(zip(sources, kept))
    ]
    for move in reversed(moves):
        move.start()
    for move in moves[4:]:
        move.wait()
    gains, decays = kept[4:]
    running = running_decay(decays[...])
    total = last_lane(running)
    lift = jnp.exp(running)
    weight = jnp.where(
        state, jnp.exp(total - running), jnp.where(chip == 1, gains[cross + 1], gains[cross + 2]) * lift
    )
    spread = columns(half_first(weight, 1 - core))
    send[pl.ds(half * dim, heads), :] = total
    for index in range(heads):
        if index % half == 0:
            for copy in copies[2 * (index // half) : 2 * (index // half) + 2]:
                copy.wait()
        lanes = slice(index * dim, (index + 1) * dim)
        rows = pl.ds(index % half * dim, dim)
        (send if index < half else keep)[rows, :] = outer_products(
            lefts[:, lanes], rights[:, lanes], spread[:, index : index + 1]
        )
    for move in moves[:4]:
        move.wait()


def second_core(position):
    return jnp.bitwise_xor(position % 2, (position // 2 == 3).astype(jnp.int32))


def second_export_kernel(
    place, query, key, value, cotangent, gain, decay, keep1, after, *outs
):
    *sends, keep, bundle = outs
    position = place[0]
    core = second_core(position)
    chip = position // 2
    heads, tok = decay.shape
    dim = query.shape[1] // heads
    half = heads // 2
    cross = gain.shape[0] - 3
    running = running_decay(decay[...])
    lift = jnp.exp(running)
    fall = jnp.exp(last_lane(running) - running)
    state2 = chip == 1
    state0 = position % 2 == 0
    weight2 = jnp.where(state2, fall, jnp.where(chip == 2, gain[cross + 2], gain[cross + 1]) * lift)
    weight2 = jnp.where(chip == 0, 0.0, weight2)
    weight0 = jnp.where(state0, fall, gain[cross] * lift)
    spread = columns(jnp.concatenate([half_first(weight2, 1 - core), weight0], axis=0))
    bundle[pl.ds(heads * dim, half * dim), :] = keep1[...]
    place_of = [(part, row) for part, send in enumerate(sends) for row in range(send.shape[0] // dim)]
    for index in range(heads):
        mine = index >= half
        head = (core if mine else 1 - core) * half + index % half
        q, k, v, o = (lane_block(ref, head, dim) for ref in (query, key, value, cotangent))
        second = outer_products(
            jnp.where(state2, k, q), jnp.where(state2, v, o), spread[:, index : index + 1]
        )
        if mine:
            keep[pl.ds(index % half * dim, dim), :] = second
            bundle[pl.ds((heads + index) * dim, dim), :] = second
        else:
            part, row = place_of[index]
            sends[part][pl.ds(row * dim, dim), :] = second
    for head in range(heads):
        lanes = slice(head * dim, (head + 1) * dim)
        q, k, v, o = (ref[:, lanes] for ref in (query, key, value, cotangent))
        bundle[pl.ds(head * dim, dim), :] = outer_products(
            jnp.where(state0, k, q),
            jnp.where(state0, v, o),
            spread[:, heads + head : heads + head + 1],
        )


def pair_factors(position, own_total, other_total, is_state):
    even = position % 2 == 0
    scale_own = is_state == even
    return (
        jnp.where(scale_own, jnp.exp(other_total), 1.0),
        jnp.where(scale_own, 1.0, jnp.exp(own_total)),
    )


def first_merge_kernel(place, decay, keep, got, after, *outs):
    position = place[0]
    chip = position // 2
    heads, tok = decay.shape
    half = heads // 2
    dim = keep.shape[0] // half
    own_total = last_lane(running_decay(decay[...]))
    other_total = got[pl.ds(half * dim, heads), :]
    own_factor, other_factor = pair_factors(position, own_total, other_total, chip % 2 == 0)
    own_factor = half_first(own_factor, position % 2)[:half]
    other_factor = half_first(other_factor, position % 2)[:half]
    head = 0
    for part, out in enumerate(outs):
        for index in range(out.shape[0] // dim):
            rows = pl.ds(head * dim, dim)
            out[pl.ds(index * dim, dim), :] = (
                own_factor[head : head + 1] * keep[rows, :]
                + other_factor[head : head + 1] * got[rows, :]
            )
            head += 1
    outs[0][pl.ds(outs[0].shape[0] - heads, heads), :] = own_total + other_total


def second_merge_kernel(low, place, decay, first_got, keep, got, first, *rest):
    out = rest[-1]
    position = place[0]
    chip = position // 2
    heads, tok = decay.shape
    half = heads // 2
    dim = keep.shape[0] // half
    own_total = last_lane(running_decay(decay[...]))
    other_total = first_got[pl.ds(half * dim, heads), :]
    own_factor, other_factor = pair_factors(position, own_total, other_total, chip == 1)
    inner = (chip == 1) | (chip == 2)
    first_factor = jnp.where(inner, jnp.exp(own_total + other_total), 0.0)
    own_factor, other_factor, first_factor = (
        half_first(factor, second_core(position)) for factor in (own_factor, other_factor, first_factor)
    )
    for index in range(out.shape[0] // dim):
        rows = pl.ds(index * dim, dim)
        one = slice(low + index, low + index + 1)
        out[rows, :] = (
            own_factor[one] * keep[pl.ds((low + index) * dim, dim), :]
            + other_factor[one] * got[rows, :]
            + first_factor[one] * first[rows, :]
        )


def lane_sums(value):
    ones = jnp.ones((2 * value.shape[1], value.shape[1]), BF16)
    return mxu(split_lanes(value), ones, NN)


def apply_state(left, right, state, weight):
    high, low = halves(state)
    first = mxu(twice_lanes(left), jnp.concatenate([high, low], axis=0), NN)
    second = mxu(twice_lanes(right), jnp.concatenate([high, low], axis=1), NT)
    sums = lane_sums(first * right.astype(F32))
    return weight * first, weight * second, sums


def local_kernel(low, mine, place, query, key, value, cotangent, gain, decay, *rest):
    acc_out, acc_query, acc_key, acc_value, gain_rows, decay_rows = rest[-6:]
    core = place[0] % 2
    side = core if mine else 1 - core
    heads, tok = decay.shape
    count = decay_rows.shape[0]
    dim = query.shape[1] // heads
    inner_levels = tok.bit_length()
    running = take_half(running_decay(decay[...]), side, low, count)
    gains = [take_half(gain[place_in], side, low, count) for place_in in range(inner_levels)]
    spread = columns(running)
    source = lax.broadcasted_iota(jnp.int32, (tok, tok), 0)
    target = lax.broadcasted_iota(jnp.int32, (tok, tok), 1)
    mixing = jnp.bitwise_xor(source, target)
    level = jnp.zeros((tok, tok), jnp.int32)
    for power in range(inner_levels - 1):
        level = level + (mixing >= 2**power).astype(jnp.int32)
    causal = source <= target
    level = jnp.where(causal, level, -1)
    gathered = jnp.zeros((tok, tok), F32)
    for index in range(count):
        lanes = slice(index * dim, (index + 1) * dim)
        one = slice(index, index + 1)
        head = side * (heads // 2) + low + index
        q, k, v, o = (lane_block(ref, head, dim) for ref in (query, key, value, cotangent))
        scores = mxu(k, q, NT)
        pulls = mxu(v, o, NT)
        fading = jnp.exp(jnp.where(causal, running[one] - spread[:, one], NEVER))
        weighting = jnp.zeros((tok, tok), F32)
        for place_in in range(inner_levels):
            weighting = jnp.where(level == place_in, gains[place_in][one], weighting)
        weighting = weighting * fading
        mixing_part = scores * weighting
        score_grad = pulls * weighting
        product = scores * pulls * fading
        flow = jnp.zeros((1, tok), F32)
        for place_in in range(inner_levels):
            found = jnp.sum(jnp.where(level == place_in, product, 0.0), axis=0, keepdims=True)
            gain_rows[place_in, one, :] = found
            if place_in > 0:
                flow = flow + gains[place_in][one] * found
        decay_rows[one, :] = flow
        left = jnp.where(level > 0, mixing_part * pulls, 0.0)
        gathered = jnp.where(target == index, lane_sums(left), gathered)
        high, low_part = halves(mixing_part)
        acc_out[:, lanes] = mxu(jnp.concatenate([high, low_part], axis=0), twice_rows(v), TN)
        acc_value[:, lanes] = mxu(jnp.concatenate([high, low_part], axis=1), twice_rows(o), NN)
        high, low_part = halves(score_grad)
        acc_query[:, lanes] = mxu(jnp.concatenate([high, low_part], axis=0), twice_rows(k), TN)
        acc_key[:, lanes] = mxu(jnp.concatenate([high, low_part], axis=1), twice_rows(q), NN)
    decay_rows[...] = decay_rows[...] - gathered.T[:count]


def use_rows(rows_out, uses, gathered, extra):
    turned = gathered.T
    count = extra.shape[0]
    decay_row = jnp.zeros((count, turned.shape[1]), F32)
    flow_row = extra
    for number, (forward, weight, lift) in enumerate(uses):
        sums = turned[number * count : (number + 1) * count]
        weighted = weight * sums
        decay_row = decay_row + jnp.where(forward, weighted, -weighted)
        flow_row = flow_row + jnp.where(forward, 0.0, weighted)
        rows_out[(2 + number) * count : (3 + number) * count, :] = lift * sums
    rows_out[:count, :] = decay_row
    rows_out[count : 2 * count, :] = flow_row


def first_use_kernel(
    low,
    mine,
    place,
    query,
    key,
    value,
    cotangent,
    gain,
    decay,
    first_got,
    first,
    second,
    second_got,
    front,
    acc_out,
    acc_query,
    acc_key,
    acc_value,
    *rest,
):
    out_mixed, out_query, out_key, out_value, rows_out = rest[-5:]
    position = place[0]
    core = position % 2
    side = core if mine else 1 - core
    chip = position // 2
    heads, tok = decay.shape
    half = heads // 2
    dim = query.shape[1] // heads
    count = acc_out.shape[1] // dim
    cross = gain.shape[0] - 3
    running = running_decay(decay[...])
    total = last_lane(running)
    other = first_got[pl.ds(half * dim, heads), :]
    odd = core == 1
    forward = chip != 0
    offset = jnp.where(forward == odd, other, 0.0)
    lift0 = jnp.exp(running)
    lift = jnp.exp(running + offset)
    fall0 = jnp.exp(total - running)
    weight0 = jnp.where(odd, gain[cross] * lift0, fall0)
    weight = jnp.where(
        forward,
        jnp.where(chip == 2, gain[cross + 2], gain[cross + 1]) * lift,
        jnp.exp(total - running + offset),
    )
    pair_flow = jnp.where(forward != odd, jnp.exp(total), 0.0)
    chip_flow = jnp.where((chip == 1) | (chip == 2), jnp.exp(total + other), 0.0)
    lift0, lift, weight0, weight, pair_flow, chip_flow = (
        take_half(rows, side, low, count)
        for rows in (jnp.where(odd, lift0, 0.0), lift, weight0, weight, pair_flow, chip_flow)
    )
    spread = columns(jnp.concatenate([weight0, weight], axis=0))
    lane = lax.broadcasted_iota(jnp.int32, (tok, tok), 1)
    gathered = jnp.zeros((tok, tok), F32)
    flows = []
    for index in range(count):
        lanes = slice(index * dim, (index + 1) * dim)
        rows = pl.ds(index * dim, dim)
        kept = pl.ds((low + index) * dim, dim)
        one = slice(index, index + 1)
        head = side * half + low + index
        q, k, v, o = (lane_block(ref, head, dim) for ref in (query, key, value, cotangent))
        level0 = front[pl.ds(pl.multiple_of(head * dim, dim), dim), :]
        pair1 = first_got[kept, :] if mine else front[pl.ds((heads + low + index) * dim, dim), :]
        pair2_kept = front[pl.ds((heads + half + low + index) * dim, dim), :]
        pair2 = jnp.where((chip == 3) == mine, pair2_kept, second_got[rows, :])
        state = jnp.where(chip == 2, second[rows, :], first[rows, :])
        partner = jnp.where(odd, level0, jnp.where(chip == 1, pair1, pair2))
        flows.append(
            pair_flow[one] * jnp.sum(state * partner, axis=0, keepdims=True)
            + chip_flow[one] * jnp.sum(first[rows, :] * second[rows, :], axis=0, keepdims=True)
        )
        left0, right0, sums = apply_state(
            jnp.where(odd, q, k), jnp.where(odd, o, v), level0, spread[:, one]
        )
        gathered = jnp.where(lane == index, sums, gathered)
        left, right, sums = apply_state(
            jnp.where(forward, q, k),
            jnp.where(forward, o, v),
            state,
            spread[:, count + index : count + index + 1],
        )
        gathered = jnp.where(lane == count + index, sums, gathered)
        out_mixed[:, lanes] = (
            acc_out[:, lanes] + jnp.where(odd, left0, 0.0) + jnp.where(forward, left, 0.0)
        )
        out_query[:, lanes] = (
            acc_query[:, lanes] + jnp.where(odd, right0, 0.0) + jnp.where(forward, right, 0.0)
        )
        out_value[:, lanes] = (
            acc_value[:, lanes] + jnp.where(odd, 0.0, left0) + jnp.where(forward, 0.0, left)
        )
        out_key[:, lanes] = (
            acc_key[:, lanes] + jnp.where(odd, 0.0, right0) + jnp.where(forward, 0.0, right)
        )
    use_rows(
        rows_out,
        ((odd, weight0, lift0), (forward, weight, lift)),
        gathered,
        jnp.concatenate(flows, axis=0),
    )


def last_use_kernel(
    low,
    mine,
    parts,
    place,
    query,
    key,
    value,
    cotangent,
    gain,
    decay,
    first_got,
    chip_total,
    second,
    third,
    front,
    acc_out,
    acc_query,
    acc_key,
    acc_value,
    *rest,
):
    ending = parts is not None
    if ending:
        *rest, grad_gain, grad_decay, staged, sems, gain_stage, decay_stage, end_sems = rest
    else:
        *rest, rows_out, staged, sems = rest
    outs = rest[-4:]
    position = place[0]
    core = position % 2
    side = core if mine else 1 - core
    chip = position // 2
    heads, tok = decay.shape
    half = heads // 2
    dim = query.shape[1] // heads
    count = acc_out.shape[1] // dim
    cross = gain.shape[0] - 3
    running = running_decay(decay[...])
    total = last_lane(running)
    other = first_got[pl.ds(half * dim, heads), :]
    chip_rows = chip_total[pl.ds(chip_total.shape[0] - heads, heads), :]
    odd = core == 1
    forward = chip == 3
    chip_offset = jnp.where((chip == 0) | (chip == 3), chip_rows, 0.0)
    offset = jnp.where(forward == odd, other, 0.0) + chip_offset
    lift = jnp.exp(running + offset)
    weight = jnp.where(forward, gain[cross + 2] * lift, jnp.exp(total - running + offset))
    pair_flow = jnp.where(forward != odd, jnp.exp(total + chip_offset), 0.0)
    lift, weight, pair_flow = (
        take_half(rows, side, low, count) for rows in (lift, weight, pair_flow)
    )
    spread = columns(weight)
    lane = lax.broadcasted_iota(jnp.int32, (tok, tok), 1)
    gathered = jnp.zeros((tok, tok), F32)
    flows = []
    copies = []
    if ending:
        early = gain.shape[0] - 2
        copies.append(
            pltpu.make_async_copy(
                gain_stage.at[pl.ds(0, early)], grad_gain.at[pl.ds(0, early)], end_sems.at[0]
            )
        )
        early_gains(parts, rest[:-4], core, gain_stage)
        copies[0].start()
    for index in range(count):
        lanes = slice(index * dim, (index + 1) * dim)
        rows = pl.ds(index * dim, dim)
        one = slice(index, index + 1)
        head = side * half + low + index
        q, k, v, o = (lane_block(ref, head, dim) for ref in (query, key, value, cotangent))
        state = jnp.where(chip == 1, second[rows, :], third[rows, :])
        level0 = front[pl.ds(pl.multiple_of(head * dim, dim), dim), :]
        if mine:
            pair1 = first_got[pl.ds((low + index) * dim, dim), :]
        else:
            pair1 = front[pl.ds((heads + low + index) * dim, dim), :]
        partner = jnp.where(odd, level0, pair1)
        flows.append(pair_flow[one] * jnp.sum(state * partner, axis=0, keepdims=True))
        left, right, sums = apply_state(
            jnp.where(forward, q, k), jnp.where(forward, o, v), state, spread[:, one]
        )
        gathered = jnp.where(lane == index, sums, gathered)
        results = (
            acc_out[:, lanes] + jnp.where(forward, left, 0.0),
            acc_query[:, lanes] + jnp.where(forward, right, 0.0),
            acc_key[:, lanes] + jnp.where(forward, 0.0, right),
            acc_value[:, lanes] + jnp.where(forward, 0.0, left),
        )
        for number, result in enumerate(results):
            staged[number, :, lanes] = result.astype(BF16)
            copy = pltpu.make_async_copy(
                staged.at[number, :, pl.ds(index * dim, dim)],
                outs[number].at[:, pl.ds(pl.multiple_of(head * dim, dim), dim)],
                sems.at[number * count + index],
            )
            copy.start()
            copies.append(copy)
    extra = jnp.concatenate(flows, axis=0)
    if not ending:
        use_rows(rows_out, ((forward, weight, lift),), gathered, extra)
    else:
        sums = gathered.T[:count]
        weighted = weight * sums
        own_rows = (
            jnp.where(forward, weighted, -weighted),
            extra + jnp.where(forward, 0.0, weighted),
            lift * sums,
        )
        finish(parts, rest[:-4], own_rows, core, chip, gain_stage, decay_stage)
        for copy in (
            pltpu.make_async_copy(
                gain_stage.at[pl.ds(early, 2)], grad_gain.at[pl.ds(early, 2)], end_sems.at[1]
            ),
            pltpu.make_async_copy(decay_stage, grad_decay, end_sems.at[2]),
        ):
            copy.start()
            copies.append(copy)
    for copy in copies:
        copy.wait()


def natural(pieces, core):
    return half_first(jnp.concatenate([*pieces[::2], *pieces[1::2]], axis=0), core)


def of_kind(counts, refs, number):
    return [
        ref[number * counts[at // 2] : (number + 1) * counts[at // 2], :]
        for at, ref in enumerate(refs)
    ]


def early_gains(counts, refs, core, grad_gain):
    levels = grad_gain.shape[0]
    groups = 2 * len(counts)
    for place_in in range(levels - 3):
        grad_gain[place_in] = natural([ref[place_in] for ref in refs[:groups]], core)
    first_rows = refs[2 * groups : 3 * groups]
    grad_gain[levels - 3] = natural(of_kind(counts, first_rows, 2), core)


def finish(counts, refs, own_rows, core, chip, grad_gain, grad_decay):
    levels, heads, tok = grad_gain.shape
    groups = 2 * len(counts)
    decay_rows, first_rows = refs[groups : 2 * groups], refs[2 * groups : 3 * groups]
    last_rows = refs[3 * groups : 4 * groups - 1]

    def last(number):
        return natural(of_kind(counts, last_rows, number) + [own_rows[number]], core)

    first, second = natural(of_kind(counts, first_rows, 3), core), last(2)
    grad_gain[levels - 2] = jnp.where(chip % 2 == 1, first, 0.0)
    grad_gain[levels - 1] = jnp.where(chip == 2, first, jnp.where(chip == 3, second, 0.0))
    own = natural([ref[...] for ref in decay_rows], core)
    own = own + natural(of_kind(counts, first_rows, 0), core) + last(0)
    later = natural(of_kind(counts, first_rows, 1), core) + last(1)
    upper = lax.broadcasted_iota(jnp.int32, (tok, tok), 0)
    lower = lax.broadcasted_iota(jnp.int32, (tok, tok), 1)
    from_here = (upper >= lower).astype(F32)
    every = jnp.ones((tok, tok), F32)
    grad_decay[...] = jnp.dot(
        own, from_here, precision=TOP_ACCURACY, preferred_element_type=F32
    ) + jnp.dot(later, every, precision=TOP_ACCURACY, preferred_element_type=F32)


def after(value, *others):
    return lax.optimization_barrier((value, *others))[0]


def sds(*shape, dtype=F32):
    return jax.ShapeDtypeStruct(shape, dtype)


FIRST_LIMIT = 24


def params(mebibytes=24):
    return pltpu.CompilerParams(vmem_limit_bytes=mebibytes * 1024 * 1024)


SCALAR = pl.BlockSpec(memory_space=pltpu.SMEM)
ANYWHERE = pl.BlockSpec(memory_space=pl.ANY)
IN_HBM = pl.BlockSpec(memory_space=pltpu.HBM)
RATE_FIRST = 16
RATE_SECOND = 0.001
RATE_LOCAL = ((.01,.01),(1,16))
RATE_USE = ((4,4),(4,4))
RATE_LAST = ((4,4),(4,4))
RATE_MERGE = (4,4)


def cost(microseconds, rate=16):
    return pl.CostEstimate(flops=int(microseconds * rate * 10**9), bytes_accessed=1, transcendentals=0)


def chunk_heads(half):
    return (half // 2, half - half // 2)


def line_device(queries, keys_in, value_input, level_gain, decay_log, out_grad):
    heads, tok = decay_log.shape
    dim = queries.shape[1] // heads
    half = heads // 2
    counts = chunk_heads(half)
    parts = range(len(counts))
    lows = [sum(counts[:part]) for part in parts]
    inner = tok.bit_length()
    place = lax.axis_index("ctx").astype(jnp.int32).reshape(1)
    tokens = (queries, keys_in, value_input, out_grad)
    inputs = (place, *tokens, level_gain, decay_log)
    core_swap = [(at, at ^ 1) for at in range(8)]
    side_swap = [(at, at ^ 2) for at in range(8)]
    middle_swap = [(0, 1), (1, 0), (2, 4), (4, 2), (3, 5), (5, 3), (6, 7), (7, 6)]

    def swap(block, route):
        return lax.ppermute(block, "ctx", route)

    def call(kernel, out_shape, operands, unread=(), spent=None, name=None, **options):
        return pl.pallas_call(
            kernel,
            out_shape=out_shape,
            in_specs=[SCALAR] + [pl.BlockSpec()] * (len(operands) - 1) + [ANYWHERE] * len(unread),
            compiler_params=params(),
            cost_estimate=spent,
            name=name,
            **options,
        )(*operands, *unread)

    send1, keep1, *kept = pl.pallas_call(
        first_export_kernel,
        out_shape=(pltpu.VMEM((half * dim + heads, dim), F32), pltpu.VMEM((half * dim, dim), F32))
        + tuple(pltpu.VMEM(array.shape, array.dtype) for array in inputs[1:]),
        in_specs=[SCALAR] + [IN_HBM] * 6,
        scratch_shapes=[
            pltpu.VMEM((tok, heads * dim), BF16),
            pltpu.VMEM((tok, heads * dim), BF16),
            pltpu.SemaphoreType.DMA((10,)),
        ],
        compiler_params=params(FIRST_LIMIT),
        cost_estimate=cost(3.3),
        name="first_exports",
    )(place, *(pltpu.with_memory_space_constraint(array, pltpu.HBM) for array in inputs[1:]))
    inputs = (place, *kept)
    decay_log = kept[-1]
    got1 = swap(send1, core_swap)
    local_done = {}

    def local(part, mine, *unread):
        count = counts[part]
        local_done[part, mine] = call(
            functools.partial(local_kernel, lows[part], mine),
            (sds(tok, count * dim),) * 4 + (sds(inner, count, tok), sds(count, tok)),
            inputs,
            unread,
            cost(0.4 * count, RATE_LOCAL[part][not mine]),
            "local",
        )
        return local_done[part, mine][-1]

    done = local(0, True)
    first_sent = call(
        first_merge_kernel,
        tuple(sds(count * dim + (0 if part else heads), dim) for part, count in enumerate(counts)),
        (place, decay_log, keep1, got1),
        (done,),
        spent=cost(0.3),
        name="first_merge",
    )
    first = [swap(block, side_swap) for block in first_sent]

    done = first_sent[-1]
    *send2, keep2, bundle = call(
        second_export_kernel,
        tuple(sds(count * dim, dim) for count in counts) + (sds(half * dim, dim), sds(4 * half * dim, dim)),
        (*inputs, keep1),
        (done,),
        cost(1.6, RATE_SECOND),
        "second_exports",
    )
    got2 = [swap(block, core_swap) for block in send2]

    def second_merge(part, *unread):
        return call(
            functools.partial(second_merge_kernel, lows[part]),
            sds(counts[part] * dim, dim),
            (place, decay_log, got1, keep2, got2[part], first[part]),
            unread,
            cost(0.3, RATE_MERGE[part]),
            "second_merge",
        )

    done = local(0, False, keep2)
    done = local(1, True, done)
    sent = [second_merge(0, done, *got2[1:])]
    done = local(1, False, sent[0])
    sent.append(second_merge(1, done))
    front = swap(bundle, core_swap)
    second = [swap(block, middle_swap) for block in sent]
    third = [swap(second[0], side_swap)]
    second_over = [swap(second[0], core_swap)]
    used = {}

    def first_use(part, mine, *unread):
        count = counts[part]
        used[part, mine] = call(
            functools.partial(first_use_kernel, lows[part], mine),
            (sds(tok, count * dim),) * 4 + (sds(4 * count, tok),),
            (
                *inputs,
                got1,
                (first if mine else first_over)[part],
                (second if mine else second_over)[part],
                got2[part],
                front,
                *local_done[part, mine][:4],
            ),
            unread,
            cost(0.3 * count, RATE_USE[part][not mine]),
            "first_use",
        )
        return used[part, mine][-1]

    results = ()
    last_rows = []

    def last_use(part, mine, ending=False):
        nonlocal results
        count = counts[part]
        operands = (
            *inputs,
            got1,
            first[0],
            (second if mine else second_over)[part],
            (third if mine else third_over)[part],
            front,
            *used[part, mine][:4],
        )
        order = [(at, side) for at in parts for side in (True, False)]
        rows = ()
        if ending:
            rows = (
                *(local_done[key][4] for key in order),
                *(local_done[key][5] for key in order),
                *(used[key][4] for key in order),
                *last_rows,
            )
        before = len(operands) + len(rows)
        tail = (sds(*level_gain.shape), sds(heads, tok)) if ending else (sds(3 * count, tok),)
        ending_scratch = [
            pltpu.VMEM(level_gain.shape, F32),
            pltpu.VMEM((heads, tok), F32),
            pltpu.SemaphoreType.DMA((3,)),
        ]
        found = pl.pallas_call(
            functools.partial(last_use_kernel, lows[part], mine, counts if ending else None),
            out_shape=(sds(tok, heads * dim, dtype=BF16),) * 4 + tail,
            in_specs=[SCALAR]
            + [pl.BlockSpec()] * (before - 1)
            + [ANYWHERE] * len(results),
            out_specs=(ANYWHERE,) * 4 + (ANYWHERE if ending else pl.BlockSpec(),) * len(tail),
            input_output_aliases={before + at: at for at in range(len(results))},
            scratch_shapes=[
                pltpu.VMEM((4, tok, count * dim), BF16),
                pltpu.SemaphoreType.DMA((4 * count,)),
            ]
            + ending_scratch * ending,
            compiler_params=params(),
            cost_estimate=cost(0.25 * count, RATE_LAST[part][not mine]),
            name="last_use",
        )(*operands, *rows, *results)
        results = found[:4]
        last_rows.extend(found[4:])

    done = first_use(0, True)
    first_over = [swap(after(first[0], second[0]), core_swap)]
    done = first_use(0, False, done)
    second[1] = after(second[1], done)
    third.append(swap(second[1], side_swap))
    second_over.append(swap(second[1], core_swap))
    first_over.append(swap(after(first[1], second[1]), core_swap))
    done = first_use(1, True, done)
    third_over = [swap(after(third[0], done), core_swap)]
    done = first_use(1, False, done)
    last_use(0, True)
    last_use(0, False)
    third_over.append(swap(after(third[1], done, last_rows[-1]), core_swap))
    last_use(1, True)
    last_use(1, False, ending=True)
    return (*results, *last_rows[-2:])


def solution(mesh):
    placed = (
        P(("seq", "ctx"), None),
        P(("seq", "ctx"), None),
        P(("seq", "ctx"), None),
        P(None, None, ("seq", "ctx")),
        P(None, ("seq", "ctx")),
        P(("seq", "ctx"), None),
    )
    return jax.shard_map(
        line_device if mesh.shape["ctx"] == 8 else per_device,
        mesh=mesh,
        in_specs=placed,
        out_specs=(
            P(("seq", "ctx"), None),
            P(("seq", "ctx"), None),
            P(("seq", "ctx"), None),
            P(("seq", "ctx"), None),
            P(None, None, ("seq", "ctx")),
            P(None, ("seq", "ctx")),
        ),
        check_vma=False,
    )
```

```python
import functools

import jax
import jax.numpy as jnp
from jax import lax
from jax.experimental import pallas as pl
from jax.experimental.pallas import tpu as pltpu
from jax.sharding import PartitionSpec as P

TOP_ACCURACY = lax.Precision.HIGHEST


def from_partner(block, axis, distance):
    count = lax.axis_size(axis)
    route = []
    for low in range(count):
        high = low | 1 << distance
        if high != low and high < count:
            route += [(low, high), (high, low)]
    return lax.ppermute(block, axis, route)


def passed_along(value, axis, steps):
    count = lax.axis_size(axis)
    first, last = (max(0, -steps), min(count, count - steps))
    return lax.ppermute(value, axis, [(source, source + steps) for source in range(first, last)])


def level_table(tok, lvl_in):
    places = jnp.arange(tok, dtype=jnp.int32)
    mixing = jnp.bitwise_xor(places[:, None], places[None, :])
    table = jnp.zeros((tok, tok), jnp.int32)
    for power in range(lvl_in):
        table = table + (mixing >= 2**power).astype(jnp.int32)
    return table


def block_front(keys_h, value_rows_head, decay):
    running = jnp.cumsum(decay, axis=1)
    total_sum = running[:, -1]
    scaled_result = keys_h * jnp.exp(total_sum[:, None] - running)[:, :, None]
    return (
        jnp.einsum("ybu,ybe->yue", scaled_result, value_rows_head, precision=TOP_ACCURACY),
        total_sum,
    )


def block_output(queries_h, keys_h, value_rows_head, gain, decay, buckets):
    tok = queries_h.shape[1]
    lvl_in = tok.bit_length() - 1
    running = jnp.cumsum(decay, axis=1)
    places = jnp.arange(tok, dtype=jnp.int32)
    causal = places[:, None] >= places[None, :]
    spread_gap = jnp.where(causal[None], running[:, :, None] - running[:, None, :], 0.0)
    fading = jnp.where(causal[None], jnp.exp(spread_gap), 0.0)
    table = level_table(tok, lvl_in)
    picks = (table[None] == jnp.arange(lvl_in + 1, dtype=jnp.int32)[:, None, None]).astype(
        jnp.float32
    )
    weighting = jnp.einsum("lij,lhi->hij", picks, gain[: lvl_in + 1], precision=TOP_ACCURACY)
    scores = jnp.einsum("hik,hjk->hij", queries_h, keys_h, precision=TOP_ACCURACY)
    result = jnp.einsum(
        "hij,hjv->hiv", scores * weighting * fading, value_rows_head, precision=TOP_ACCURACY
    )
    lifted = queries_h * jnp.exp(running)[:, :, None]
    reach = gain[lvl_in + 1 :][:, :, :, None] * lifted[None]
    return result + jnp.einsum("jhik,jhkv->hiv", reach, buckets, precision=TOP_ACCURACY)


def merge_step(own_total, own_state, offset, other_total, other_state, is_upper):
    bucket = jnp.where(is_upper, jnp.exp(offset)[:, None, None] * other_state, 0.0)
    low_state = jnp.where(is_upper, other_state, own_state)
    high_state = jnp.where(is_upper, own_state, other_state)
    high_total = jnp.where(is_upper, own_total, other_total)
    merged = jnp.exp(high_total)[:, None, None] * low_state + high_state
    new_offset = offset + jnp.where(is_upper, other_total, 0.0)
    return (own_total + other_total, merged, new_offset, bucket)


def partner_grads(
    own_total, own_state, offset, other_total, g_total, g_state, g_offset, g_bucket, is_upper
):
    factor = jnp.exp(jnp.where(is_upper, own_total, other_total))
    d_other_state = jnp.where(
        is_upper,
        factor[:, None, None] * g_state + jnp.exp(offset)[:, None, None] * g_bucket,
        g_state,
    )
    lower_term = factor * jnp.sum(g_state * own_state, axis=(1, 2))
    d_other_total = g_total + jnp.where(is_upper, g_offset, lower_term)
    return (d_other_total, d_other_state)


def own_grads(
    own_total, offset, other_total, other_state, g_total, g_state, g_offset, g_bucket, is_upper
):
    factor = jnp.exp(jnp.where(is_upper, own_total, other_total))
    d_own_state = jnp.where(is_upper, g_state, factor[:, None, None] * g_state)
    upper_total = factor * jnp.sum(g_state * other_state, axis=(1, 2))
    d_own_total = g_total + jnp.where(is_upper, upper_total, 0.0)
    upper_offset = jnp.exp(offset) * jnp.sum(g_bucket * other_state, axis=(1, 2))
    d_offset = g_offset + jnp.where(is_upper, upper_offset, 0.0)
    return (d_own_total, d_own_state, d_offset)


def to_heads(block, heads):
    tokens, width = block.shape
    return block.reshape(tokens, heads, width // heads).transpose(1, 0, 2).astype(jnp.float32)


def from_heads(block):
    heads, tokens, head_dim = block.shape
    return block.transpose(1, 0, 2).reshape(tokens, heads * head_dim)


def per_device(queries, keys_in, value_input, level_gain, decay_log, out_grad):
    heads = decay_log.shape[0]
    query_h = to_heads(queries, heads)
    key_h = to_heads(keys_in, heads)
    value_h = to_heads(value_input, heads)
    cotangent = to_heads(out_grad, heads)
    count = lax.axis_size("ctx")
    depth = count.bit_length() - 1
    position = lax.axis_index("ctx")
    (state, total_sum), front_back = jax.vjp(block_front, key_h, value_h, decay_log)
    own_total = total_sum
    own_state = state
    offset = jnp.zeros_like(total_sum)
    saved = []
    found = []
    top_other = state
    for bit in range(depth):
        other_total, other_state = from_partner((own_total, own_state), "ctx", bit)
        is_upper = jnp.right_shift(position, bit) % 2 == 1
        saved.append((own_total, own_state, offset, other_total))
        if bit == depth - 1:
            top_other = other_state
        own_total, own_state, offset, bucket = merge_step(
            own_total, own_state, offset, other_total, other_state, is_upper
        )
        found.append(bucket)
    buckets = jnp.stack(found)
    mixed, out_back = jax.vjp(block_output, query_h, key_h, value_h, level_gain, decay_log, buckets)
    grad_query, grad_key, grad_value, grad_gain, grad_decay, bucket_gradient = out_back(cotangent)
    grad_total = jnp.zeros_like(total_sum)
    grad_state = jnp.zeros_like(state)
    grad_offset = jnp.zeros_like(total_sum)
    for bit in reversed(range(depth)):
        is_upper = jnp.right_shift(position, bit) % 2 == 1
        level_total, level_state, level_offset, level_other_total = saved[bit]
        d_other_total, d_other_state = partner_grads(
            level_total,
            level_state,
            level_offset,
            level_other_total,
            grad_total,
            grad_state,
            grad_offset,
            bucket_gradient[bit],
            is_upper,
        )
        if bit == depth - 1:
            back_total, back_state = passed_along(
                (d_other_total, d_other_state), "ctx", -(count // 2)
            )
            partner_state = top_other
        else:
            back_total, back_state, partner_state = from_partner(
                (d_other_total, d_other_state, level_state), "ctx", bit
            )
        d_own_total, d_own_state, d_offset = own_grads(
            level_total,
            level_offset,
            level_other_total,
            partner_state,
            grad_total,
            grad_state,
            grad_offset,
            bucket_gradient[bit],
            is_upper,
        )
        grad_total = d_own_total + back_total
        grad_state = d_own_state + back_state
        grad_offset = d_offset
    key_more, value_more, decay_more = front_back((grad_state, grad_total))
    return (
        from_heads(mixed).astype(jnp.bfloat16),
        from_heads(grad_query).astype(jnp.bfloat16),
        from_heads(grad_key + key_more).astype(jnp.bfloat16),
        from_heads(grad_value + value_more).astype(jnp.bfloat16),
        grad_gain,
        grad_decay + decay_more,
    )


F32 = jnp.float32
BF16 = jnp.bfloat16
NT = (((1,), (1,)), ((), ()))
TN = (((0,), (0,)), ((), ()))
NN = (((1,), (0,)), ((), ()))
NEVER = -1e30


def mxu(left, right, dims):
    return lax.dot_general(left, right, dims, preferred_element_type=F32)


def halves(value):
    high = value.astype(BF16)
    low = (value - high.astype(F32)).astype(BF16)
    return high, low


def split_rows(value):
    return jnp.concatenate(halves(value), axis=0)


def split_lanes(value):
    return jnp.concatenate(halves(value), axis=1)


def twice_rows(value):
    return jnp.concatenate([value, value], axis=0)


def twice_lanes(value):
    return jnp.concatenate([value, value], axis=1)


def running_decay(decay):
    tok = decay.shape[1]
    earlier = lax.broadcasted_iota(jnp.int32, (tok, tok), 0)
    later = lax.broadcasted_iota(jnp.int32, (tok, tok), 1)
    upto = (earlier <= later).astype(F32)
    return jnp.dot(decay, upto, precision=TOP_ACCURACY, preferred_element_type=F32)


def last_lane(running):
    return jnp.broadcast_to(running[:, running.shape[1] - 1 :], running.shape)


def columns(rows):
    count, tok = rows.shape
    if count < tok:
        rows = jnp.concatenate([rows, jnp.zeros((tok - count, tok), rows.dtype)], axis=0)
    return rows.T


def half_first(rows, core):
    half = rows.shape[0] // 2
    swapped = jnp.concatenate([rows[half:], rows[:half]], axis=0)
    return jnp.where(core == 0, rows, swapped)


def lane_block(ref, head, width):
    return ref[:, pl.ds(pl.multiple_of(head * width, width), width)]


def take_half(rows, core, low, count):
    half = rows.shape[0] // 2
    return jnp.where(core == 0, rows[low : low + count], rows[half + low : half + low + count])


def outer_products(left, right, weight_column):
    turned = left.T
    return mxu(twice_lanes(turned), split_rows(right.astype(F32) * weight_column), NN)


def first_export_half(state, core, weight, query, key, value, cotangent, out, ready):
    heads, tok = weight.shape
    dim = query.shape[1] // heads
    half = heads // 2
    spread = columns(half_first(weight, core))

    def products(left, right):
        for index in range(half):
            head = core * half + index
            out[pl.ds(index * dim, dim), :] = outer_products(
                lane_block(left, head, dim),
                lane_block(right, head, dim),
                spread[:, index : index + 1],
            )

    @pl.when(state)
    def _():
        ready(key, value)
        products(key, value)

    @pl.when(jnp.logical_not(state))
    def _():
        ready(query, cotangent)
        products(query, cotangent)


def first_weights(position, gain, decay):
    chip = position // 2
    cross = gain.shape[0] - 3
    running = running_decay(decay[...])
    total = last_lane(running)
    weight = jnp.where(
        chip % 2 == 0,
        jnp.exp(total - running),
        jnp.where(chip == 1, gain[cross + 1], gain[cross + 2]) * jnp.exp(running),
    )
    return weight, total


def first_export_kernel(
    place, query, key, value, cotangent, gain, decay, send, *rest
):
    kept, sems = rest[:6], rest[6]
    position = place[0]
    core = position % 2
    heads, tok = decay.shape
    half = heads // 2
    wide = query.shape[1] // 2
    state = position // 2 % 2 == 0
    sources = (query, key, value, cotangent)
    names = ("query", "key", "value", "cotangent")
    moves = {}
    for number, (name, source, target) in enumerate(zip(names, sources, kept)):
        for side in range(2):
            lanes = pl.ds(pl.multiple_of((1 - core if side == 0 else core) * wide, wide), wide)
            moves[name, side] = pltpu.make_async_copy(
                source.at[:, lanes], target.at[:, lanes], sems.at[2 * number + side]
            )
    small = [
        pltpu.make_async_copy(source, target, sems.at[8 + number])
        for number, (source, target) in enumerate(zip((gain, decay), kept[4:]))
    ]
    for move in small:
        move.start()

    def start(*order):
        for side in range(2):
            for name in order:
                moves[name, side].start()

    @pl.when(state)
    def _():
        start("key", "value")
        start("query", "cotangent")

    @pl.when(jnp.logical_not(state))
    def _():
        start("query", "cotangent")
        start("key", "value")

    for move in small:
        move.wait()
    weight, total = first_weights(position, *kept[4:])
    send[pl.ds(send.shape[0] - heads, heads), :] = total

    def ready(left, right):
        for name, target in zip(names, kept):
            if target is left or target is right:
                moves[name, 0].wait()

    first_export_half(state, 1 - core, weight, *kept[:4], send, ready)

    @pl.when(state)
    def _():
        for name in ("query", "cotangent"):
            moves[name, 0].wait()

    @pl.when(jnp.logical_not(state))
    def _():
        for name in ("key", "value"):
            moves[name, 0].wait()

    for name in names:
        moves[name, 1].wait()


def own_export_kernel(place, query, key, value, cotangent, gain, decay, after, keep):
    position = place[0]
    weight, _ = first_weights(position, gain, decay)
    first_export_half(
        position // 2 % 2 == 0,
        position % 2,
        weight,
        query,
        key,
        value,
        cotangent,
        keep,
        lambda left, right: None,
    )


def second_core(position):
    return jnp.bitwise_xor(position % 2, (position // 2 == 3).astype(jnp.int32))


def second_export_kernel(
    place, query, key, value, cotangent, gain, decay, keep1, after, *outs
):
    *sends, keep, bundle = outs
    position = place[0]
    core = second_core(position)
    chip = position // 2
    heads, tok = decay.shape
    dim = query.shape[1] // heads
    half = heads // 2
    cross = gain.shape[0] - 3
    running = running_decay(decay[...])
    lift = jnp.exp(running)
    fall = jnp.exp(last_lane(running) - running)
    state2 = chip == 1
    state0 = position % 2 == 0
    weight2 = jnp.where(state2, fall, jnp.where(chip == 2, gain[cross + 2], gain[cross + 1]) * lift)
    weight2 = jnp.where(chip == 0, 0.0, weight2)
    weight0 = jnp.where(state0, fall, gain[cross] * lift)
    spread = columns(jnp.concatenate([half_first(weight2, 1 - core), weight0], axis=0))
    bundle[pl.ds(heads * dim, half * dim), :] = keep1[...]
    place_of = [(part, row) for part, send in enumerate(sends) for row in range(send.shape[0] // dim)]
    for index in range(heads):
        mine = index >= half
        head = (core if mine else 1 - core) * half + index % half
        q, k, v, o = (lane_block(ref, head, dim) for ref in (query, key, value, cotangent))
        second = outer_products(
            jnp.where(state2, k, q), jnp.where(state2, v, o), spread[:, index : index + 1]
        )
        if mine:
            keep[pl.ds(index % half * dim, dim), :] = second
            bundle[pl.ds((heads + index) * dim, dim), :] = second
        else:
            part, row = place_of[index]
            sends[part][pl.ds(row * dim, dim), :] = second
    for head in range(heads):
        lanes = slice(head * dim, (head + 1) * dim)
        q, k, v, o = (ref[:, lanes] for ref in (query, key, value, cotangent))
        bundle[pl.ds(head * dim, dim), :] = outer_products(
            jnp.where(state0, k, q),
            jnp.where(state0, v, o),
            spread[:, heads + head : heads + head + 1],
        )


def pair_factors(position, own_total, other_total, is_state):
    even = position % 2 == 0
    scale_own = is_state == even
    return (
        jnp.where(scale_own, jnp.exp(other_total), 1.0),
        jnp.where(scale_own, 1.0, jnp.exp(own_total)),
    )


def first_merge_kernel(place, decay, keep, got, *outs):
    position = place[0]
    chip = position // 2
    heads, tok = decay.shape
    half = heads // 2
    dim = keep.shape[0] // half
    own_total = last_lane(running_decay(decay[...]))
    other_total = got[pl.ds(half * dim, heads), :]
    own_factor, other_factor = pair_factors(position, own_total, other_total, chip % 2 == 0)
    own_factor = half_first(own_factor, position % 2)[:half]
    other_factor = half_first(other_factor, position % 2)[:half]
    head = 0
    for part, out in enumerate(outs):
        for index in range(out.shape[0] // dim):
            rows = pl.ds(head * dim, dim)
            out[pl.ds(index * dim, dim), :] = (
                own_factor[head : head + 1] * keep[rows, :]
                + other_factor[head : head + 1] * got[rows, :]
            )
            head += 1
    outs[0][pl.ds(outs[0].shape[0] - heads, heads), :] = own_total + other_total


def second_merge_kernel(low, place, decay, first_got, keep, got, first, *rest):
    out = rest[-1]
    position = place[0]
    chip = position // 2
    heads, tok = decay.shape
    half = heads // 2
    dim = keep.shape[0] // half
    own_total = last_lane(running_decay(decay[...]))
    other_total = first_got[pl.ds(half * dim, heads), :]
    own_factor, other_factor = pair_factors(position, own_total, other_total, chip == 1)
    inner = (chip == 1) | (chip == 2)
    first_factor = jnp.where(inner, jnp.exp(own_total + other_total), 0.0)
    own_factor, other_factor, first_factor = (
        half_first(factor, second_core(position)) for factor in (own_factor, other_factor, first_factor)
    )
    for index in range(out.shape[0] // dim):
        rows = pl.ds(index * dim, dim)
        one = slice(low + index, low + index + 1)
        out[rows, :] = (
            own_factor[one] * keep[pl.ds((low + index) * dim, dim), :]
            + other_factor[one] * got[rows, :]
            + first_factor[one] * first[rows, :]
        )


def lane_sums(value):
    ones = jnp.ones((2 * value.shape[1], value.shape[1]), BF16)
    return mxu(split_lanes(value), ones, NN)


def apply_state(left, right, state, weight):
    high, low = halves(state)
    first = mxu(twice_lanes(left), jnp.concatenate([high, low], axis=0), NN)
    second = mxu(twice_lanes(right), jnp.concatenate([high, low], axis=1), NT)
    sums = lane_sums(first * right.astype(F32))
    return weight * first, weight * second, sums


def local_kernel(low, mine, place, query, key, value, cotangent, gain, decay, *rest):
    acc_out, acc_query, acc_key, acc_value, gain_rows, decay_rows = rest[-6:]
    core = place[0] % 2
    side = core if mine else 1 - core
    heads, tok = decay.shape
    count = decay_rows.shape[0]
    dim = query.shape[1] // heads
    inner_levels = tok.bit_length()
    running = take_half(running_decay(decay[...]), side, low, count)
    gains = [take_half(gain[place_in], side, low, count) for place_in in range(inner_levels)]
    spread = columns(running)
    source = lax.broadcasted_iota(jnp.int32, (tok, tok), 0)
    target = lax.broadcasted_iota(jnp.int32, (tok, tok), 1)
    mixing = jnp.bitwise_xor(source, target)
    level = jnp.zeros((tok, tok), jnp.int32)
    for power in range(inner_levels - 1):
        level = level + (mixing >= 2**power).astype(jnp.int32)
    causal = source <= target
    level = jnp.where(causal, level, -1)
    gathered = jnp.zeros((tok, tok), F32)
    for index in range(count):
        lanes = slice(index * dim, (index + 1) * dim)
        one = slice(index, index + 1)
        head = side * (heads // 2) + low + index
        q, k, v, o = (lane_block(ref, head, dim) for ref in (query, key, value, cotangent))
        scores = mxu(k, q, NT)
        pulls = mxu(v, o, NT)
        fading = jnp.exp(jnp.where(causal, running[one] - spread[:, one], NEVER))
        weighting = jnp.zeros((tok, tok), F32)
        for place_in in range(inner_levels):
            weighting = jnp.where(level == place_in, gains[place_in][one], weighting)
        weighting = weighting * fading
        mixing_part = scores * weighting
        score_grad = pulls * weighting
        product = scores * pulls * fading
        flow = jnp.zeros((1, tok), F32)
        for place_in in range(inner_levels):
            found = jnp.sum(jnp.where(level == place_in, product, 0.0), axis=0, keepdims=True)
            gain_rows[place_in, one, :] = found
            if place_in > 0:
                flow = flow + gains[place_in][one] * found
        decay_rows[one, :] = flow
        left = jnp.where(level > 0, mixing_part * pulls, 0.0)
        gathered = jnp.where(target == index, lane_sums(left), gathered)
        high, low_part = halves(mixing_part)
        acc_out[:, lanes] = mxu(jnp.concatenate([high, low_part], axis=0), twice_rows(v), TN)
        acc_value[:, lanes] = mxu(jnp.concatenate([high, low_part], axis=1), twice_rows(o), NN)
        high, low_part = halves(score_grad)
        acc_query[:, lanes] = mxu(jnp.concatenate([high, low_part], axis=0), twice_rows(k), TN)
        acc_key[:, lanes] = mxu(jnp.concatenate([high, low_part], axis=1), twice_rows(q), NN)
    decay_rows[...] = decay_rows[...] - gathered.T[:count]


def use_rows(rows_out, uses, gathered, extra):
    turned = gathered.T
    count = extra.shape[0]
    decay_row = jnp.zeros((count, turned.shape[1]), F32)
    flow_row = extra
    for number, (forward, weight, lift) in enumerate(uses):
        sums = turned[number * count : (number + 1) * count]
        weighted = weight * sums
        decay_row = decay_row + jnp.where(forward, weighted, -weighted)
        flow_row = flow_row + jnp.where(forward, 0.0, weighted)
        rows_out[(2 + number) * count : (3 + number) * count, :] = lift * sums
    rows_out[:count, :] = decay_row
    rows_out[count : 2 * count, :] = flow_row


def first_use_kernel(
    low,
    mine,
    place,
    query,
    key,
    value,
    cotangent,
    gain,
    decay,
    first_got,
    first,
    second,
    second_got,
    front,
    acc_out,
    acc_query,
    acc_key,
    acc_value,
    *rest,
):
    out_mixed, out_query, out_key, out_value, rows_out = rest[-5:]
    position = place[0]
    core = position % 2
    side = core if mine else 1 - core
    chip = position // 2
    heads, tok = decay.shape
    half = heads // 2
    dim = query.shape[1] // heads
    count = acc_out.shape[1] // dim
    cross = gain.shape[0] - 3
    running = running_decay(decay[...])
    total = last_lane(running)
    other = first_got[pl.ds(half * dim, heads), :]
    odd = core == 1
    forward = chip != 0
    offset = jnp.where(forward == odd, other, 0.0)
    lift0 = jnp.exp(running)
    lift = jnp.exp(running + offset)
    fall0 = jnp.exp(total - running)
    weight0 = jnp.where(odd, gain[cross] * lift0, fall0)
    weight = jnp.where(
        forward,
        jnp.where(chip == 2, gain[cross + 2], gain[cross + 1]) * lift,
        jnp.exp(total - running + offset),
    )
    pair_flow = jnp.where(forward != odd, jnp.exp(total), 0.0)
    chip_flow = jnp.where((chip == 1) | (chip == 2), jnp.exp(total + other), 0.0)
    lift0, lift, weight0, weight, pair_flow, chip_flow = (
        take_half(rows, side, low, count)
        for rows in (jnp.where(odd, lift0, 0.0), lift, weight0, weight, pair_flow, chip_flow)
    )
    spread = columns(jnp.concatenate([weight0, weight], axis=0))
    lane = lax.broadcasted_iota(jnp.int32, (tok, tok), 1)
    gathered = jnp.zeros((tok, tok), F32)
    flows = []
    for index in range(count):
        lanes = slice(index * dim, (index + 1) * dim)
        rows = pl.ds(index * dim, dim)
        kept = pl.ds((low + index) * dim, dim)
        one = slice(index, index + 1)
        head = side * half + low + index
        q, k, v, o = (lane_block(ref, head, dim) for ref in (query, key, value, cotangent))
        level0 = front[pl.ds(pl.multiple_of(head * dim, dim), dim), :]
        pair1 = first_got[kept, :] if mine else front[pl.ds((heads + low + index) * dim, dim), :]
        pair2_kept = front[pl.ds((heads + half + low + index) * dim, dim), :]
        pair2 = jnp.where((chip == 3) == mine, pair2_kept, second_got[rows, :])
        state = jnp.where(chip == 2, second[rows, :], first[rows, :])
        partner = jnp.where(odd, level0, jnp.where(chip == 1, pair1, pair2))
        flows.append(
            pair_flow[one] * jnp.sum(state * partner, axis=0, keepdims=True)
            + chip_flow[one] * jnp.sum(first[rows, :] * second[rows, :], axis=0, keepdims=True)
        )
        left0, right0, sums = apply_state(
            jnp.where(odd, q, k), jnp.where(odd, o, v), level0, spread[:, one]
        )
        gathered = jnp.where(lane == index, sums, gathered)
        left, right, sums = apply_state(
            jnp.where(forward, q, k),
            jnp.where(forward, o, v),
            state,
            spread[:, count + index : count + index + 1],
        )
        gathered = jnp.where(lane == count + index, sums, gathered)
        out_mixed[:, lanes] = (
            acc_out[:, lanes] + jnp.where(odd, left0, 0.0) + jnp.where(forward, left, 0.0)
        )
        out_query[:, lanes] = (
            acc_query[:, lanes] + jnp.where(odd, right0, 0.0) + jnp.where(forward, right, 0.0)
        )
        out_value[:, lanes] = (
            acc_value[:, lanes] + jnp.where(odd, 0.0, left0) + jnp.where(forward, 0.0, left)
        )
        out_key[:, lanes] = (
            acc_key[:, lanes] + jnp.where(odd, 0.0, right0) + jnp.where(forward, 0.0, right)
        )
    use_rows(
        rows_out,
        ((odd, weight0, lift0), (forward, weight, lift)),
        gathered,
        jnp.concatenate(flows, axis=0),
    )


def last_use_kernel(
    low,
    mine,
    parts,
    place,
    query,
    key,
    value,
    cotangent,
    gain,
    decay,
    first_got,
    chip_total,
    second,
    third,
    front,
    acc_out,
    acc_query,
    acc_key,
    acc_value,
    *rest,
):
    ending = parts is not None
    if ending:
        *rest, grad_gain, grad_decay, staged, sems, gain_stage, decay_stage, end_sems = rest
    else:
        *rest, rows_out, staged, sems = rest
    outs = rest[-4:]
    position = place[0]
    core = position % 2
    side = core if mine else 1 - core
    chip = position // 2
    heads, tok = decay.shape
    half = heads // 2
    dim = query.shape[1] // heads
    count = acc_out.shape[1] // dim
    cross = gain.shape[0] - 3
    running = running_decay(decay[...])
    total = last_lane(running)
    other = first_got[pl.ds(half * dim, heads), :]
    chip_rows = chip_total[pl.ds(chip_total.shape[0] - heads, heads), :]
    odd = core == 1
    forward = chip == 3
    chip_offset = jnp.where((chip == 0) | (chip == 3), chip_rows, 0.0)
    offset = jnp.where(forward == odd, other, 0.0) + chip_offset
    lift = jnp.exp(running + offset)
    weight = jnp.where(forward, gain[cross + 2] * lift, jnp.exp(total - running + offset))
    pair_flow = jnp.where(forward != odd, jnp.exp(total + chip_offset), 0.0)
    lift, weight, pair_flow = (
        take_half(rows, side, low, count) for rows in (lift, weight, pair_flow)
    )
    spread = columns(weight)
    lane = lax.broadcasted_iota(jnp.int32, (tok, tok), 1)
    gathered = jnp.zeros((tok, tok), F32)
    flows = []
    copies = []
    if ending:
        early = gain.shape[0] - 2
        copies.append(
            pltpu.make_async_copy(
                gain_stage.at[pl.ds(0, early)], grad_gain.at[pl.ds(0, early)], end_sems.at[0]
            )
        )
        early_gains(parts, rest[:-4], core, gain_stage)
        copies[0].start()
    for index in range(count):
        lanes = slice(index * dim, (index + 1) * dim)
        rows = pl.ds(index * dim, dim)
        one = slice(index, index + 1)
        head = side * half + low + index
        q, k, v, o = (lane_block(ref, head, dim) for ref in (query, key, value, cotangent))
        state = jnp.where(chip == 1, second[rows, :], third[rows, :])
        level0 = front[pl.ds(pl.multiple_of(head * dim, dim), dim), :]
        if mine:
            pair1 = first_got[pl.ds((low + index) * dim, dim), :]
        else:
            pair1 = front[pl.ds((heads + low + index) * dim, dim), :]
        partner = jnp.where(odd, level0, pair1)
        flows.append(pair_flow[one] * jnp.sum(state * partner, axis=0, keepdims=True))
        left, right, sums = apply_state(
            jnp.where(forward, q, k), jnp.where(forward, o, v), state, spread[:, one]
        )
        gathered = jnp.where(lane == index, sums, gathered)
        results = (
            acc_out[:, lanes] + jnp.where(forward, left, 0.0),
            acc_query[:, lanes] + jnp.where(forward, right, 0.0),
            acc_key[:, lanes] + jnp.where(forward, 0.0, right),
            acc_value[:, lanes] + jnp.where(forward, 0.0, left),
        )
        for number, result in enumerate(results):
            staged[number, :, lanes] = result.astype(BF16)
            copy = pltpu.make_async_copy(
                staged.at[number, :, pl.ds(index * dim, dim)],
                outs[number].at[:, pl.ds(pl.multiple_of(head * dim, dim), dim)],
                sems.at[number * count + index],
            )
            copy.start()
            copies.append(copy)
    extra = jnp.concatenate(flows, axis=0)
    if not ending:
        use_rows(rows_out, ((forward, weight, lift),), gathered, extra)
    else:
        sums = gathered.T[:count]
        weighted = weight * sums
        own_rows = (
            jnp.where(forward, weighted, -weighted),
            extra + jnp.where(forward, 0.0, weighted),
            lift * sums,
        )
        finish(parts, rest[:-4], own_rows, core, chip, gain_stage, decay_stage)
        for copy in (
            pltpu.make_async_copy(
                gain_stage.at[pl.ds(early, 2)], grad_gain.at[pl.ds(early, 2)], end_sems.at[1]
            ),
            pltpu.make_async_copy(decay_stage, grad_decay, end_sems.at[2]),
        ):
            copy.start()
            copies.append(copy)
    for copy in copies:
        copy.wait()


def natural(pieces, core):
    return half_first(jnp.concatenate([*pieces[::2], *pieces[1::2]], axis=0), core)


def of_kind(counts, refs, number):
    return [
        ref[number * counts[at // 2] : (number + 1) * counts[at // 2], :]
        for at, ref in enumerate(refs)
    ]


def early_gains(counts, refs, core, grad_gain):
    levels = grad_gain.shape[0]
    groups = 2 * len(counts)
    for place_in in range(levels - 3):
        grad_gain[place_in] = natural([ref[place_in] for ref in refs[:groups]], core)
    first_rows = refs[2 * groups : 3 * groups]
    grad_gain[levels - 3] = natural(of_kind(counts, first_rows, 2), core)


def finish(counts, refs, own_rows, core, chip, grad_gain, grad_decay):
    levels, heads, tok = grad_gain.shape
    groups = 2 * len(counts)
    decay_rows, first_rows = refs[groups : 2 * groups], refs[2 * groups : 3 * groups]
    last_rows = refs[3 * groups : 4 * groups - 1]

    def last(number):
        return natural(of_kind(counts, last_rows, number) + [own_rows[number]], core)

    first, second = natural(of_kind(counts, first_rows, 3), core), last(2)
    grad_gain[levels - 2] = jnp.where(chip % 2 == 1, first, 0.0)
    grad_gain[levels - 1] = jnp.where(chip == 2, first, jnp.where(chip == 3, second, 0.0))
    own = natural([ref[...] for ref in decay_rows], core)
    own = own + natural(of_kind(counts, first_rows, 0), core) + last(0)
    later = natural(of_kind(counts, first_rows, 1), core) + last(1)
    upper = lax.broadcasted_iota(jnp.int32, (tok, tok), 0)
    lower = lax.broadcasted_iota(jnp.int32, (tok, tok), 1)
    from_here = (upper >= lower).astype(BF16)
    sums = jnp.concatenate([twice_rows(from_here), jnp.ones((2 * tok, tok), BF16)], axis=0)
    grad_decay[...] = mxu(
        jnp.concatenate([split_lanes(own), split_lanes(later)], axis=1), sums, NN
    )


def after(value, *others):
    return lax.optimization_barrier((value, *others))[0]


def sds(*shape, dtype=F32):
    return jax.ShapeDtypeStruct(shape, dtype)


FIRST_LIMIT = 24


def params(mebibytes=24):
    return pltpu.CompilerParams(vmem_limit_bytes=mebibytes * 1024 * 1024)


SCALAR = pl.BlockSpec(memory_space=pltpu.SMEM)
ANYWHERE = pl.BlockSpec(memory_space=pl.ANY)
IN_HBM = pl.BlockSpec(memory_space=pltpu.HBM)
RATE_FIRST = 16
RATE_SECOND = 0.001
RATE_LOCAL = ((.01,.01),(1,16))
RATE_USE = ((4,4),(4,4))
RATE_LAST = ((4,4),(4,4))
RATE_MERGE = (4,4)


def cost(microseconds, rate=16):
    return pl.CostEstimate(flops=int(microseconds * rate * 10**9), bytes_accessed=1, transcendentals=0)


def chunk_heads(half):
    return (half // 2, half - half // 2)


def line_device(queries, keys_in, value_input, level_gain, decay_log, out_grad):
    heads, tok = decay_log.shape
    dim = queries.shape[1] // heads
    half = heads // 2
    counts = chunk_heads(half)
    parts = range(len(counts))
    lows = [sum(counts[:part]) for part in parts]
    inner = tok.bit_length()
    place = lax.axis_index("ctx").astype(jnp.int32).reshape(1)
    tokens = (queries, keys_in, value_input, out_grad)
    inputs = (place, *tokens, level_gain, decay_log)
    core_swap = [(at, at ^ 1) for at in range(8)]
    side_swap = [(at, at ^ 2) for at in range(8)]
    middle_swap = [(0, 1), (1, 0), (2, 4), (4, 2), (3, 5), (5, 3), (6, 7), (7, 6)]

    def swap(block, route):
        return lax.ppermute(block, "ctx", route)

    def call(kernel, out_shape, operands, unread=(), spent=None, name=None, **options):
        return pl.pallas_call(
            kernel,
            out_shape=out_shape,
            in_specs=[SCALAR] + [pl.BlockSpec()] * (len(operands) - 1) + [ANYWHERE] * len(unread),
            compiler_params=params(),
            cost_estimate=spent,
            name=name,
            **options,
        )(*operands, *unread)

    send1, *kept = pl.pallas_call(
        first_export_kernel,
        out_shape=(pltpu.VMEM((half * dim + heads, dim), F32),)
        + tuple(pltpu.VMEM(array.shape, array.dtype) for array in inputs[1:]),
        in_specs=[SCALAR] + [IN_HBM] * 6,
        scratch_shapes=[pltpu.SemaphoreType.DMA((10,))],
        compiler_params=params(),
        cost_estimate=cost(2),
        name="first_exports",
    )(place, *(pltpu.with_memory_space_constraint(array, pltpu.HBM) for array in inputs[1:]))
    inputs = (place, *kept)
    decay_log = kept[-1]
    got1 = swap(send1, core_swap)
    keep1 = call(
        own_export_kernel,
        sds(half * dim, dim),
        inputs,
        (send1,),
        cost(0.8, RATE_FIRST),
        "own_exports",
    )
    first_sent = call(
        first_merge_kernel,
        tuple(sds(count * dim + (0 if part else heads), dim) for part, count in enumerate(counts)),
        (place, decay_log, keep1, got1),
        spent=cost(0.3),
        name="first_merge",
    )
    first = [swap(first_sent[0], side_swap)]

    local_done = {}

    def local(part, mine, *unread):
        count = counts[part]
        local_done[part, mine] = call(
            functools.partial(local_kernel, lows[part], mine),
            (sds(tok, count * dim),) * 4 + (sds(inner, count, tok), sds(count, tok)),
            inputs,
            unread,
            cost(0.4 * count, RATE_LOCAL[part][not mine]),
            "local",
        )
        return local_done[part, mine][-1]

    done = first_sent[-1]
    *send2, keep2, bundle = call(
        second_export_kernel,
        tuple(sds(count * dim, dim) for count in counts) + (sds(half * dim, dim), sds(4 * half * dim, dim)),
        (*inputs, keep1),
        (done,),
        cost(1.6, RATE_SECOND),
        "second_exports",
    )
    got2 = [swap(block, core_swap) for block in send2]

    def second_merge(part, *unread):
        return call(
            functools.partial(second_merge_kernel, lows[part]),
            sds(counts[part] * dim, dim),
            (place, decay_log, got1, keep2, got2[part], first[part]),
            unread,
            cost(0.3, RATE_MERGE[part]),
            "second_merge",
        )

    done = local(0, True, keep2)
    first.append(swap(after(first_sent[1], done), side_swap))
    done = local(0, False, done)
    sent = [second_merge(0, done, *got2[1:])]
    done = local(1, True, sent[0])
    sent.append(second_merge(1, done))
    front = swap(bundle, core_swap)
    second = [swap(block, middle_swap) for block in sent]
    third = [swap(second[0], side_swap)]
    second_over = [swap(second[0], core_swap)]
    done = local(1, False, second[0])

    used = {}

    def first_use(part, mine, *unread):
        count = counts[part]
        used[part, mine] = call(
            functools.partial(first_use_kernel, lows[part], mine),
            (sds(tok, count * dim),) * 4 + (sds(4 * count, tok),),
            (
                *inputs,
                got1,
                (first if mine else first_over)[part],
                (second if mine else second_over)[part],
                got2[part],
                front,
                *local_done[part, mine][:4],
            ),
            unread,
            cost(0.3 * count, RATE_USE[part][not mine]),
            "first_use",
        )
        return used[part, mine][-1]

    results = ()
    last_rows = []

    def last_use(part, mine, ending=False):
        nonlocal results
        count = counts[part]
        operands = (
            *inputs,
            got1,
            first[0],
            (second if mine else second_over)[part],
            (third if mine else third_over)[part],
            front,
            *used[part, mine][:4],
        )
        order = [(at, side) for at in parts for side in (True, False)]
        rows = ()
        if ending:
            rows = (
                *(local_done[key][4] for key in order),
                *(local_done[key][5] for key in order),
                *(used[key][4] for key in order),
                *last_rows,
            )
        before = len(operands) + len(rows)
        tail = (sds(*level_gain.shape), sds(heads, tok)) if ending else (sds(3 * count, tok),)
        ending_scratch = [
            pltpu.VMEM(level_gain.shape, F32),
            pltpu.VMEM((heads, tok), F32),
            pltpu.SemaphoreType.DMA((3,)),
        ]
        found = pl.pallas_call(
            functools.partial(last_use_kernel, lows[part], mine, counts if ending else None),
            out_shape=(sds(tok, heads * dim, dtype=BF16),) * 4 + tail,
            in_specs=[SCALAR]
            + [pl.BlockSpec()] * (before - 1)
            + [ANYWHERE] * len(results),
            out_specs=(ANYWHERE,) * 4 + (ANYWHERE if ending else pl.BlockSpec(),) * len(tail),
            input_output_aliases={before + at: at for at in range(len(results))},
            scratch_shapes=[
                pltpu.VMEM((4, tok, count * dim), BF16),
                pltpu.SemaphoreType.DMA((4 * count,)),
            ]
            + ending_scratch * ending,
            compiler_params=params(),
            cost_estimate=cost(0.25 * count, RATE_LAST[part][not mine]),
            name="last_use",
        )(*operands, *rows, *results)
        results = found[:4]
        last_rows.extend(found[4:])

    done = first_use(0, True, done)
    first_over = [swap(after(first[0], second[0]), core_swap)]
    done = first_use(0, False, done)
    second[1] = after(second[1], done)
    third.append(swap(second[1], side_swap))
    second_over.append(swap(second[1], core_swap))
    first_over.append(swap(after(first[1], second[1]), core_swap))
    done = first_use(1, True, done)
    third_over = [swap(after(third[0], done), core_swap)]
    done = first_use(1, False, done)
    last_use(0, True)
    last_use(0, False)
    third_over.append(swap(after(third[1], done, last_rows[-1]), core_swap))
    last_use(1, True)
    last_use(1, False, ending=True)
    return (*results, *last_rows[-2:])


def solution(mesh):
    placed = (
        P(("seq", "ctx"), None),
        P(("seq", "ctx"), None),
        P(("seq", "ctx"), None),
        P(None, None, ("seq", "ctx")),
        P(None, ("seq", "ctx")),
        P(("seq", "ctx"), None),
    )
    return jax.shard_map(
        line_device if mesh.shape["ctx"] == 8 else per_device,
        mesh=mesh,
        in_specs=placed,
        out_specs=(
            P(("seq", "ctx"), None),
            P(("seq", "ctx"), None),
            P(("seq", "ctx"), None),
            P(("seq", "ctx"), None),
            P(None, None, ("seq", "ctx")),
            P(None, ("seq", "ctx")),
        ),
        check_vma=False,
    )
```

```python
import functools

import jax
import jax.numpy as jnp
from jax import lax
from jax.experimental import pallas as pl
from jax.experimental.pallas import tpu as pltpu
from jax.sharding import PartitionSpec as P

TOP_ACCURACY = lax.Precision.HIGHEST


def from_partner(block, axis, distance):
    count = lax.axis_size(axis)
    route = []
    for low in range(count):
        high = low | 1 << distance
        if high != low and high < count:
            route += [(low, high), (high, low)]
    return lax.ppermute(block, axis, route)


def passed_along(value, axis, steps):
    count = lax.axis_size(axis)
    first, last = (max(0, -steps), min(count, count - steps))
    return lax.ppermute(value, axis, [(source, source + steps) for source in range(first, last)])


def level_table(tok, lvl_in):
    places = jnp.arange(tok, dtype=jnp.int32)
    mixing = jnp.bitwise_xor(places[:, None], places[None, :])
    table = jnp.zeros((tok, tok), jnp.int32)
    for power in range(lvl_in):
        table = table + (mixing >= 2**power).astype(jnp.int32)
    return table


def block_front(keys_h, value_rows_head, decay):
    running = jnp.cumsum(decay, axis=1)
    total_sum = running[:, -1]
    scaled_result = keys_h * jnp.exp(total_sum[:, None] - running)[:, :, None]
    return (
        jnp.einsum("ybu,ybe->yue", scaled_result, value_rows_head, precision=TOP_ACCURACY),
        total_sum,
    )


def block_output(queries_h, keys_h, value_rows_head, gain, decay, buckets):
    tok = queries_h.shape[1]
    lvl_in = tok.bit_length() - 1
    running = jnp.cumsum(decay, axis=1)
    places = jnp.arange(tok, dtype=jnp.int32)
    causal = places[:, None] >= places[None, :]
    spread_gap = jnp.where(causal[None], running[:, :, None] - running[:, None, :], 0.0)
    fading = jnp.where(causal[None], jnp.exp(spread_gap), 0.0)
    table = level_table(tok, lvl_in)
    picks = (table[None] == jnp.arange(lvl_in + 1, dtype=jnp.int32)[:, None, None]).astype(
        jnp.float32
    )
    weighting = jnp.einsum("lij,lhi->hij", picks, gain[: lvl_in + 1], precision=TOP_ACCURACY)
    scores = jnp.einsum("hik,hjk->hij", queries_h, keys_h, precision=TOP_ACCURACY)
    result = jnp.einsum(
        "hij,hjv->hiv", scores * weighting * fading, value_rows_head, precision=TOP_ACCURACY
    )
    lifted = queries_h * jnp.exp(running)[:, :, None]
    reach = gain[lvl_in + 1 :][:, :, :, None] * lifted[None]
    return result + jnp.einsum("jhik,jhkv->hiv", reach, buckets, precision=TOP_ACCURACY)


def merge_step(own_total, own_state, offset, other_total, other_state, is_upper):
    bucket = jnp.where(is_upper, jnp.exp(offset)[:, None, None] * other_state, 0.0)
    low_state = jnp.where(is_upper, other_state, own_state)
    high_state = jnp.where(is_upper, own_state, other_state)
    high_total = jnp.where(is_upper, own_total, other_total)
    merged = jnp.exp(high_total)[:, None, None] * low_state + high_state
    new_offset = offset + jnp.where(is_upper, other_total, 0.0)
    return (own_total + other_total, merged, new_offset, bucket)


def partner_grads(
    own_total, own_state, offset, other_total, g_total, g_state, g_offset, g_bucket, is_upper
):
    factor = jnp.exp(jnp.where(is_upper, own_total, other_total))
    d_other_state = jnp.where(
        is_upper,
        factor[:, None, None] * g_state + jnp.exp(offset)[:, None, None] * g_bucket,
        g_state,
    )
    lower_term = factor * jnp.sum(g_state * own_state, axis=(1, 2))
    d_other_total = g_total + jnp.where(is_upper, g_offset, lower_term)
    return (d_other_total, d_other_state)


def own_grads(
    own_total, offset, other_total, other_state, g_total, g_state, g_offset, g_bucket, is_upper
):
    factor = jnp.exp(jnp.where(is_upper, own_total, other_total))
    d_own_state = jnp.where(is_upper, g_state, factor[:, None, None] * g_state)
    upper_total = factor * jnp.sum(g_state * other_state, axis=(1, 2))
    d_own_total = g_total + jnp.where(is_upper, upper_total, 0.0)
    upper_offset = jnp.exp(offset) * jnp.sum(g_bucket * other_state, axis=(1, 2))
    d_offset = g_offset + jnp.where(is_upper, upper_offset, 0.0)
    return (d_own_total, d_own_state, d_offset)


def to_heads(block, heads):
    tokens, width = block.shape
    return block.reshape(tokens, heads, width // heads).transpose(1, 0, 2).astype(jnp.float32)


def from_heads(block):
    heads, tokens, head_dim = block.shape
    return block.transpose(1, 0, 2).reshape(tokens, heads * head_dim)


def per_device(queries, keys_in, value_input, level_gain, decay_log, out_grad):
    heads = decay_log.shape[0]
    query_h = to_heads(queries, heads)
    key_h = to_heads(keys_in, heads)
    value_h = to_heads(value_input, heads)
    cotangent = to_heads(out_grad, heads)
    count = lax.axis_size("ctx")
    depth = count.bit_length() - 1
    position = lax.axis_index("ctx")
    (state, total_sum), front_back = jax.vjp(block_front, key_h, value_h, decay_log)
    own_total = total_sum
    own_state = state
    offset = jnp.zeros_like(total_sum)
    saved = []
    found = []
    top_other = state
    for bit in range(depth):
        other_total, other_state = from_partner((own_total, own_state), "ctx", bit)
        is_upper = jnp.right_shift(position, bit) % 2 == 1
        saved.append((own_total, own_state, offset, other_total))
        if bit == depth - 1:
            top_other = other_state
        own_total, own_state, offset, bucket = merge_step(
            own_total, own_state, offset, other_total, other_state, is_upper
        )
        found.append(bucket)
    buckets = jnp.stack(found)
    mixed, out_back = jax.vjp(block_output, query_h, key_h, value_h, level_gain, decay_log, buckets)
    grad_query, grad_key, grad_value, grad_gain, grad_decay, bucket_gradient = out_back(cotangent)
    grad_total = jnp.zeros_like(total_sum)
    grad_state = jnp.zeros_like(state)
    grad_offset = jnp.zeros_like(total_sum)
    for bit in reversed(range(depth)):
        is_upper = jnp.right_shift(position, bit) % 2 == 1
        level_total, level_state, level_offset, level_other_total = saved[bit]
        d_other_total, d_other_state = partner_grads(
            level_total,
            level_state,
            level_offset,
            level_other_total,
            grad_total,
            grad_state,
            grad_offset,
            bucket_gradient[bit],
            is_upper,
        )
        if bit == depth - 1:
            back_total, back_state = passed_along(
                (d_other_total, d_other_state), "ctx", -(count // 2)
            )
            partner_state = top_other
        else:
            back_total, back_state, partner_state = from_partner(
                (d_other_total, d_other_state, level_state), "ctx", bit
            )
        d_own_total, d_own_state, d_offset = own_grads(
            level_total,
            level_offset,
            level_other_total,
            partner_state,
            grad_total,
            grad_state,
            grad_offset,
            bucket_gradient[bit],
            is_upper,
        )
        grad_total = d_own_total + back_total
        grad_state = d_own_state + back_state
        grad_offset = d_offset
    key_more, value_more, decay_more = front_back((grad_state, grad_total))
    return (
        from_heads(mixed).astype(jnp.bfloat16),
        from_heads(grad_query).astype(jnp.bfloat16),
        from_heads(grad_key + key_more).astype(jnp.bfloat16),
        from_heads(grad_value + value_more).astype(jnp.bfloat16),
        grad_gain,
        grad_decay + decay_more,
    )


F32 = jnp.float32
BF16 = jnp.bfloat16
NT = (((1,), (1,)), ((), ()))
TN = (((0,), (0,)), ((), ()))
NN = (((1,), (0,)), ((), ()))
NEVER = -1e30


def mxu(left, right, dims):
    return lax.dot_general(left, right, dims, preferred_element_type=F32)


def halves(value):
    high = value.astype(BF16)
    low = (value - high.astype(F32)).astype(BF16)
    return high, low


def split_rows(value):
    return jnp.concatenate(halves(value), axis=0)


def split_lanes(value):
    return jnp.concatenate(halves(value), axis=1)


def twice_rows(value):
    return jnp.concatenate([value, value], axis=0)


def twice_lanes(value):
    return jnp.concatenate([value, value], axis=1)


def running_decay(decay):
    tok = decay.shape[1]
    earlier = lax.broadcasted_iota(jnp.int32, (tok, tok), 0)
    later = lax.broadcasted_iota(jnp.int32, (tok, tok), 1)
    upto = (earlier <= later).astype(F32)
    return jnp.dot(decay, upto, precision=TOP_ACCURACY, preferred_element_type=F32)


def last_lane(running):
    return jnp.broadcast_to(running[:, running.shape[1] - 1 :], running.shape)


def columns(rows):
    count, tok = rows.shape
    if count < tok:
        rows = jnp.concatenate([rows, jnp.zeros((tok - count, tok), rows.dtype)], axis=0)
    return rows.T


def half_first(rows, core):
    half = rows.shape[0] // 2
    swapped = jnp.concatenate([rows[half:], rows[:half]], axis=0)
    return jnp.where(core == 0, rows, swapped)


def lane_block(ref, head, width):
    return ref[:, pl.ds(pl.multiple_of(head * width, width), width)]


def take_half(rows, core, low, count):
    half = rows.shape[0] // 2
    return jnp.where(core == 0, rows[low : low + count], rows[half + low : half + low + count])


def outer_products(left, right, weight_column):
    turned = left.T
    return mxu(twice_lanes(turned), split_rows(right.astype(F32) * weight_column), NN)


def first_export_half(state, core, weight, query, key, value, cotangent, outs, ready):
    heads, tok = weight.shape
    dim = query.shape[1] // heads
    half = heads // 2
    spread = columns(half_first(weight, core))
    targets = [(out, row) for out in outs for row in range(out.shape[0] // dim)]

    def products(left, right):
        for index in range(half):
            head = core * half + index
            out, row = targets[index]
            out[pl.ds(row * dim, dim), :] = outer_products(
                lane_block(left, head, dim),
                lane_block(right, head, dim),
                spread[:, index : index + 1],
            )

    @pl.when(state)
    def _():
        ready(key, value)
        products(key, value)

    @pl.when(jnp.logical_not(state))
    def _():
        ready(query, cotangent)
        products(query, cotangent)


def first_weights(position, gain, decay):
    chip = position // 2
    cross = gain.shape[0] - 3
    running = running_decay(decay[...])
    total = last_lane(running)
    weight = jnp.where(
        chip % 2 == 0,
        jnp.exp(total - running),
        jnp.where(chip == 1, gain[cross + 1], gain[cross + 2]) * jnp.exp(running),
    )
    return weight, total


def first_export_kernel(
    place, query, key, value, cotangent, gain, decay, *rest
):
    sends, kept, sems = rest[:-7], rest[-7:-1], rest[-1]
    position = place[0]
    core = position % 2
    heads, tok = decay.shape
    half = heads // 2
    wide = query.shape[1] // 2
    state = position // 2 % 2 == 0
    sources = (query, key, value, cotangent)
    names = ("query", "key", "value", "cotangent")
    moves = {}
    for number, (name, source, target) in enumerate(zip(names, sources, kept)):
        for side in range(2):
            lanes = pl.ds(pl.multiple_of((1 - core if side == 0 else core) * wide, wide), wide)
            moves[name, side] = pltpu.make_async_copy(
                source.at[:, lanes], target.at[:, lanes], sems.at[2 * number + side]
            )
    small = [
        pltpu.make_async_copy(source, target, sems.at[8 + number])
        for number, (source, target) in enumerate(zip((gain, decay), kept[4:]))
    ]
    for move in small:
        move.start()

    def start(*order):
        for side in range(2):
            for name in order:
                moves[name, side].start()

    @pl.when(state)
    def _():
        start("key", "value")
        start("query", "cotangent")

    @pl.when(jnp.logical_not(state))
    def _():
        start("query", "cotangent")
        start("key", "value")

    for move in small:
        move.wait()
    weight, total = first_weights(position, *kept[4:])
    sends[0][pl.ds(sends[0].shape[0] - heads, heads), :] = total

    def ready(left, right):
        for name, target in zip(names, kept):
            if target is left or target is right:
                moves[name, 0].wait()

    first_export_half(state, 1 - core, weight, *kept[:4], sends, ready)

    @pl.when(state)
    def _():
        for name in ("query", "cotangent"):
            moves[name, 0].wait()

    @pl.when(jnp.logical_not(state))
    def _():
        for name in ("key", "value"):
            moves[name, 0].wait()

    for name in names:
        moves[name, 1].wait()


def own_export_kernel(place, query, key, value, cotangent, gain, decay, after, keep, totals):
    position = place[0]
    weight, total = first_weights(position, gain, decay)
    totals[...] = total
    first_export_half(
        position // 2 % 2 == 0,
        position % 2,
        weight,
        query,
        key,
        value,
        cotangent,
        [keep],
        lambda left, right: None,
    )


def second_core(position):
    return jnp.bitwise_xor(position % 2, (position // 2 == 3).astype(jnp.int32))


def second_export_kernel(
    place, query, key, value, cotangent, gain, decay, keep1, first_got, after, *outs
):
    *sends, keep, bundle, factors = outs
    position = place[0]
    core = second_core(position)
    chip = position // 2
    heads, tok = decay.shape
    dim = query.shape[1] // heads
    half = heads // 2
    cross = gain.shape[0] - 3
    running = running_decay(decay[...])
    lift = jnp.exp(running)
    fall = jnp.exp(last_lane(running) - running)
    state2 = chip == 1
    state0 = position % 2 == 0
    weight2 = jnp.where(state2, fall, jnp.where(chip == 2, gain[cross + 2], gain[cross + 1]) * lift)
    weight2 = jnp.where(chip == 0, 0.0, weight2)
    weight0 = jnp.where(state0, fall, gain[cross] * lift)
    spread = columns(jnp.concatenate([half_first(weight2, 1 - core), weight0], axis=0))
    own_total = last_lane(running)
    other_total = first_got[pl.ds(first_got.shape[0] - heads, heads), :]
    inner = (chip == 1) | (chip == 2)
    merged = (
        *pair_factors(position, own_total, other_total, chip == 1),
        jnp.where(inner, jnp.exp(own_total + other_total), 0.0),
    )
    for kind, rows in enumerate(merged):
        factors[kind * half : (kind + 1) * half, :] = half_first(rows, core)[:half]
    bundle[pl.ds(heads * dim, half * dim), :] = keep1[...]
    place_of = [(part, row) for part, send in enumerate(sends) for row in range(send.shape[0] // dim)]
    for index in range(heads):
        mine = index >= half
        head = (core if mine else 1 - core) * half + index % half
        q, k, v, o = (lane_block(ref, head, dim) for ref in (query, key, value, cotangent))
        second = outer_products(
            jnp.where(state2, k, q), jnp.where(state2, v, o), spread[:, index : index + 1]
        )
        if mine:
            keep[pl.ds(index % half * dim, dim), :] = second
            bundle[pl.ds((heads + index) * dim, dim), :] = second
        else:
            part, row = place_of[index]
            sends[part][pl.ds(row * dim, dim), :] = second
    for head in range(heads):
        lanes = slice(head * dim, (head + 1) * dim)
        q, k, v, o = (ref[:, lanes] for ref in (query, key, value, cotangent))
        bundle[pl.ds(head * dim, dim), :] = outer_products(
            jnp.where(state0, k, q),
            jnp.where(state0, v, o),
            spread[:, heads + head : heads + head + 1],
        )


def pair_factors(position, own_total, other_total, is_state):
    even = position % 2 == 0
    scale_own = is_state == even
    return (
        jnp.where(scale_own, jnp.exp(other_total), 1.0),
        jnp.where(scale_own, 1.0, jnp.exp(own_total)),
    )


def first_merge_kernel(low, place, totals, first_got, keep, got, *rest):
    out = rest[-1]
    position = place[0]
    chip = position // 2
    heads, dim = totals.shape[0], keep.shape[1]
    own_total = totals[...]
    other_total = first_got[pl.ds(first_got.shape[0] - heads, heads), :]
    count = out.shape[0] // dim
    factors = pair_factors(position, own_total, other_total, chip % 2 == 0)
    own_factor, other_factor = (take_half(rows, position % 2, low, count) for rows in factors)
    for index in range(count):
        rows = pl.ds(index * dim, dim)
        one = slice(index, index + 1)
        out[rows, :] = (
            own_factor[one] * keep[pl.ds((low + index) * dim, dim), :]
            + other_factor[one] * got[rows, :]
        )
    if low == 0:
        out[pl.ds(count * dim, heads), :] = own_total + other_total


def second_merge_kernel(low, factors, keep, got, first, *rest):
    out = rest[-1]
    dim = keep.shape[1]
    half = keep.shape[0] // dim
    for index in range(out.shape[0] // dim):
        rows = pl.ds(index * dim, dim)
        own, other, earlier = (
            factors[kind * half + low + index : kind * half + low + index + 1, :] for kind in range(3)
        )
        out[rows, :] = (
            own * keep[pl.ds((low + index) * dim, dim), :]
            + other * got[rows, :]
            + earlier * first[rows, :]
        )


def lane_sums(value):
    ones = jnp.ones((2 * value.shape[1], value.shape[1]), BF16)
    return mxu(split_lanes(value), ones, NN)


def apply_state(left, right, state, weight):
    high, low = halves(state)
    first = mxu(twice_lanes(left), jnp.concatenate([high, low], axis=0), NN)
    second = mxu(twice_lanes(right), jnp.concatenate([high, low], axis=1), NT)
    sums = lane_sums(first * right.astype(F32))
    return weight * first, weight * second, sums


def local_kernel(low, mine, place, query, key, value, cotangent, gain, decay, *rest):
    acc_out, acc_query, acc_key, acc_value, gain_rows, decay_rows = rest[-6:]
    core = place[0] % 2
    side = core if mine else 1 - core
    heads, tok = decay.shape
    count = decay_rows.shape[0]
    dim = query.shape[1] // heads
    inner_levels = tok.bit_length()
    running = take_half(running_decay(decay[...]), side, low, count)
    gains = [take_half(gain[place_in], side, low, count) for place_in in range(inner_levels)]
    spread = columns(running)
    source = lax.broadcasted_iota(jnp.int32, (tok, tok), 0)
    target = lax.broadcasted_iota(jnp.int32, (tok, tok), 1)
    mixing = jnp.bitwise_xor(source, target)
    level = jnp.zeros((tok, tok), jnp.int32)
    for power in range(inner_levels - 1):
        level = level + (mixing >= 2**power).astype(jnp.int32)
    causal = source <= target
    level = jnp.where(causal, level, -1)
    gathered = jnp.zeros((tok, tok), F32)
    for index in range(count):
        lanes = slice(index * dim, (index + 1) * dim)
        one = slice(index, index + 1)
        head = side * (heads // 2) + low + index
        q, k, v, o = (lane_block(ref, head, dim) for ref in (query, key, value, cotangent))
        scores = mxu(k, q, NT)
        pulls = mxu(v, o, NT)
        fading = jnp.exp(jnp.where(causal, running[one] - spread[:, one], NEVER))
        weighting = jnp.zeros((tok, tok), F32)
        for place_in in range(inner_levels):
            weighting = jnp.where(level == place_in, gains[place_in][one], weighting)
        weighting = weighting * fading
        mixing_part = scores * weighting
        score_grad = pulls * weighting
        product = scores * pulls * fading
        flow = jnp.zeros((1, tok), F32)
        for place_in in range(inner_levels):
            found = jnp.sum(jnp.where(level == place_in, product, 0.0), axis=0, keepdims=True)
            gain_rows[place_in, one, :] = found
            if place_in > 0:
                flow = flow + gains[place_in][one] * found
        decay_rows[one, :] = flow
        left = jnp.where(level > 0, mixing_part * pulls, 0.0)
        gathered = jnp.where(target == index, lane_sums(left), gathered)
        high, low_part = halves(mixing_part)
        acc_out[:, lanes] = mxu(jnp.concatenate([high, low_part], axis=0), twice_rows(v), TN)
        acc_value[:, lanes] = mxu(jnp.concatenate([high, low_part], axis=1), twice_rows(o), NN)
        high, low_part = halves(score_grad)
        acc_query[:, lanes] = mxu(jnp.concatenate([high, low_part], axis=0), twice_rows(k), TN)
        acc_key[:, lanes] = mxu(jnp.concatenate([high, low_part], axis=1), twice_rows(q), NN)
    decay_rows[...] = decay_rows[...] - gathered.T[:count]


def use_rows(rows_out, uses, gathered, extra):
    turned = gathered.T
    count = extra.shape[0]
    decay_row = jnp.zeros((count, turned.shape[1]), F32)
    flow_row = extra
    for number, (forward, weight, lift) in enumerate(uses):
        sums = turned[number * count : (number + 1) * count]
        weighted = weight * sums
        decay_row = decay_row + jnp.where(forward, weighted, -weighted)
        flow_row = flow_row + jnp.where(forward, 0.0, weighted)
        rows_out[(2 + number) * count : (3 + number) * count, :] = lift * sums
    rows_out[:count, :] = decay_row
    rows_out[count : 2 * count, :] = flow_row


def first_use_kernel(
    low,
    mine,
    place,
    query,
    key,
    value,
    cotangent,
    gain,
    decay,
    first_got,
    pair_got,
    first,
    second,
    second_got,
    front,
    acc_out,
    acc_query,
    acc_key,
    acc_value,
    *rest,
):
    out_mixed, out_query, out_key, out_value, rows_out = rest[-5:]
    position = place[0]
    core = position % 2
    side = core if mine else 1 - core
    chip = position // 2
    heads, tok = decay.shape
    half = heads // 2
    dim = query.shape[1] // heads
    count = acc_out.shape[1] // dim
    cross = gain.shape[0] - 3
    running = running_decay(decay[...])
    total = last_lane(running)
    other = first_got[pl.ds(first_got.shape[0] - heads, heads), :]
    odd = core == 1
    forward = chip != 0
    offset = jnp.where(forward == odd, other, 0.0)
    lift0 = jnp.exp(running)
    lift = jnp.exp(running + offset)
    fall0 = jnp.exp(total - running)
    weight0 = jnp.where(odd, gain[cross] * lift0, fall0)
    weight = jnp.where(
        forward,
        jnp.where(chip == 2, gain[cross + 2], gain[cross + 1]) * lift,
        jnp.exp(total - running + offset),
    )
    pair_flow = jnp.where(forward != odd, jnp.exp(total), 0.0)
    chip_flow = jnp.where((chip == 1) | (chip == 2), jnp.exp(total + other), 0.0)
    lift0, lift, weight0, weight, pair_flow, chip_flow = (
        take_half(rows, side, low, count)
        for rows in (jnp.where(odd, lift0, 0.0), lift, weight0, weight, pair_flow, chip_flow)
    )
    spread = columns(jnp.concatenate([weight0, weight], axis=0))
    lane = lax.broadcasted_iota(jnp.int32, (tok, tok), 1)
    gathered = jnp.zeros((tok, tok), F32)
    flows = []
    for index in range(count):
        lanes = slice(index * dim, (index + 1) * dim)
        rows = pl.ds(index * dim, dim)
        one = slice(index, index + 1)
        head = side * half + low + index
        q, k, v, o = (lane_block(ref, head, dim) for ref in (query, key, value, cotangent))
        level0 = front[pl.ds(pl.multiple_of(head * dim, dim), dim), :]
        pair1 = pair_got[rows, :] if mine else front[pl.ds((heads + low + index) * dim, dim), :]
        pair2_kept = front[pl.ds((heads + half + low + index) * dim, dim), :]
        pair2 = jnp.where((chip == 3) == mine, pair2_kept, second_got[rows, :])
        state = jnp.where(chip == 2, second[rows, :], first[rows, :])
        partner = jnp.where(odd, level0, jnp.where(chip == 1, pair1, pair2))
        flows.append(
            pair_flow[one] * jnp.sum(state * partner, axis=0, keepdims=True)
            + chip_flow[one] * jnp.sum(first[rows, :] * second[rows, :], axis=0, keepdims=True)
        )
        left0, right0, sums = apply_state(
            jnp.where(odd, q, k), jnp.where(odd, o, v), level0, spread[:, one]
        )
        gathered = jnp.where(lane == index, sums, gathered)
        left, right, sums = apply_state(
            jnp.where(forward, q, k),
            jnp.where(forward, o, v),
            state,
            spread[:, count + index : count + index + 1],
        )
        gathered = jnp.where(lane == count + index, sums, gathered)
        out_mixed[:, lanes] = (
            acc_out[:, lanes] + jnp.where(odd, left0, 0.0) + jnp.where(forward, left, 0.0)
        )
        out_query[:, lanes] = (
            acc_query[:, lanes] + jnp.where(odd, right0, 0.0) + jnp.where(forward, right, 0.0)
        )
        out_value[:, lanes] = (
            acc_value[:, lanes] + jnp.where(odd, 0.0, left0) + jnp.where(forward, 0.0, left)
        )
        out_key[:, lanes] = (
            acc_key[:, lanes] + jnp.where(odd, 0.0, right0) + jnp.where(forward, 0.0, right)
        )
    use_rows(
        rows_out,
        ((odd, weight0, lift0), (forward, weight, lift)),
        gathered,
        jnp.concatenate(flows, axis=0),
    )


def last_use_kernel(
    low,
    mine,
    parts,
    place,
    query,
    key,
    value,
    cotangent,
    gain,
    decay,
    first_got,
    pair_got,
    chip_total,
    second,
    third,
    front,
    acc_out,
    acc_query,
    acc_key,
    acc_value,
    *rest,
):
    ending = parts is not None
    if ending:
        *rest, grad_gain, grad_decay, staged, sems, gain_stage, decay_stage, end_sems = rest
    elif mine:
        *rest, rows_out = rest
    else:
        *rest, rows_out, staged, sems = rest
    outs, before = rest[-4:], rest[:4]
    if not mine:
        rest = rest[4:]
    position = place[0]
    core = position % 2
    side = core if mine else 1 - core
    chip = position // 2
    heads, tok = decay.shape
    half = heads // 2
    dim = query.shape[1] // heads
    count = acc_out.shape[1] // dim
    cross = gain.shape[0] - 3
    running = running_decay(decay[...])
    total = last_lane(running)
    other = first_got[pl.ds(first_got.shape[0] - heads, heads), :]
    chip_rows = chip_total[pl.ds(chip_total.shape[0] - heads, heads), :]
    odd = core == 1
    forward = chip == 3
    chip_offset = jnp.where((chip == 0) | (chip == 3), chip_rows, 0.0)
    offset = jnp.where(forward == odd, other, 0.0) + chip_offset
    lift = jnp.exp(running + offset)
    weight = jnp.where(forward, gain[cross + 2] * lift, jnp.exp(total - running + offset))
    pair_flow = jnp.where(forward != odd, jnp.exp(total + chip_offset), 0.0)
    lift, weight, pair_flow = (
        take_half(rows, side, low, count) for rows in (lift, weight, pair_flow)
    )
    spread = columns(weight)
    lane = lax.broadcasted_iota(jnp.int32, (tok, tok), 1)
    gathered = jnp.zeros((tok, tok), F32)
    flows = []
    copies = []
    if not mine:
        wide = before[0].shape[1]
        start = pl.multiple_of(core * half * dim + low * dim, dim)
        for number in range(4):
            copy = pltpu.make_async_copy(
                before[number], outs[number].at[:, pl.ds(start, wide)], sems.at[4 * count + number]
            )
            copy.start()
            copies.append(copy)
    if ending:
        early = gain.shape[0] - 2
        copies.append(
            pltpu.make_async_copy(
                gain_stage.at[pl.ds(0, early)], grad_gain.at[pl.ds(0, early)], end_sems.at[0]
            )
        )
        early_gains(parts, rest[:-4], core, gain_stage)
        copies[-1].start()
    for index in range(count):
        lanes = slice(index * dim, (index + 1) * dim)
        rows = pl.ds(index * dim, dim)
        one = slice(index, index + 1)
        head = side * half + low + index
        q, k, v, o = (lane_block(ref, head, dim) for ref in (query, key, value, cotangent))
        state = jnp.where(chip == 1, second[rows, :], third[rows, :])
        level0 = front[pl.ds(pl.multiple_of(head * dim, dim), dim), :]
        if mine:
            pair1 = pair_got[rows, :]
        else:
            pair1 = front[pl.ds((heads + low + index) * dim, dim), :]
        partner = jnp.where(odd, level0, pair1)
        flows.append(pair_flow[one] * jnp.sum(state * partner, axis=0, keepdims=True))
        left, right, sums = apply_state(
            jnp.where(forward, q, k), jnp.where(forward, o, v), state, spread[:, one]
        )
        gathered = jnp.where(lane == index, sums, gathered)
        results = (
            acc_out[:, lanes] + jnp.where(forward, left, 0.0),
            acc_query[:, lanes] + jnp.where(forward, right, 0.0),
            acc_key[:, lanes] + jnp.where(forward, 0.0, right),
            acc_value[:, lanes] + jnp.where(forward, 0.0, left),
        )
        for number, result in enumerate(results):
            if mine:
                outs[number][:, lanes] = result.astype(BF16)
                continue
            staged[number, :, lanes] = result.astype(BF16)
            copy = pltpu.make_async_copy(
                staged.at[number, :, pl.ds(index * dim, dim)],
                outs[number].at[:, pl.ds(pl.multiple_of(head * dim, dim), dim)],
                sems.at[number * count + index],
            )
            copy.start()
            copies.append(copy)
    extra = jnp.concatenate(flows, axis=0)
    if not ending:
        use_rows(rows_out, ((forward, weight, lift),), gathered, extra)
    else:
        sums = gathered.T[:count]
        weighted = weight * sums
        own_rows = (
            jnp.where(forward, weighted, -weighted),
            extra + jnp.where(forward, 0.0, weighted),
            lift * sums,
        )
        finish(parts, rest[:-4], own_rows, core, chip, gain_stage, decay_stage)
        for copy in (
            pltpu.make_async_copy(
                gain_stage.at[pl.ds(early, 2)], grad_gain.at[pl.ds(early, 2)], end_sems.at[1]
            ),
            pltpu.make_async_copy(decay_stage, grad_decay, end_sems.at[2]),
        ):
            copy.start()
            copies.append(copy)
    for copy in copies:
        copy.wait()


def natural(pieces, core):
    return half_first(jnp.concatenate([*pieces[::2], *pieces[1::2]], axis=0), core)


def of_kind(counts, refs, number):
    return [
        ref[number * counts[at // 2] : (number + 1) * counts[at // 2], :]
        for at, ref in enumerate(refs)
    ]


def early_gains(counts, refs, core, grad_gain):
    levels = grad_gain.shape[0]
    groups = 2 * len(counts)
    for place_in in range(levels - 3):
        grad_gain[place_in] = natural([ref[place_in] for ref in refs[:groups]], core)
    first_rows = refs[2 * groups : 3 * groups]
    grad_gain[levels - 3] = natural(of_kind(counts, first_rows, 2), core)


def finish(counts, refs, own_rows, core, chip, grad_gain, grad_decay):
    levels, heads, tok = grad_gain.shape
    groups = 2 * len(counts)
    decay_rows, first_rows = refs[groups : 2 * groups], refs[2 * groups : 3 * groups]
    last_rows = refs[3 * groups : 4 * groups - 1]

    def last(number):
        return natural(of_kind(counts, last_rows, number) + [own_rows[number]], core)

    first, second = natural(of_kind(counts, first_rows, 3), core), last(2)
    grad_gain[levels - 2] = jnp.where(chip % 2 == 1, first, 0.0)
    grad_gain[levels - 1] = jnp.where(chip == 2, first, jnp.where(chip == 3, second, 0.0))
    own = natural([ref[...] for ref in decay_rows], core)
    own = own + natural(of_kind(counts, first_rows, 0), core) + last(0)
    later = natural(of_kind(counts, first_rows, 1), core) + last(1)
    upper = lax.broadcasted_iota(jnp.int32, (tok, tok), 0)
    lower = lax.broadcasted_iota(jnp.int32, (tok, tok), 1)
    from_here = (upper >= lower).astype(BF16)
    sums = jnp.concatenate([twice_rows(from_here), jnp.ones((2 * tok, tok), BF16)], axis=0)
    grad_decay[...] = mxu(
        jnp.concatenate([split_lanes(own), split_lanes(later)], axis=1), sums, NN
    )


def after(value, *others):
    return lax.optimization_barrier((value, *others))[0]


def sds(*shape, dtype=F32):
    return jax.ShapeDtypeStruct(shape, dtype)


FIRST_LIMIT = 24


def params(mebibytes=24):
    return pltpu.CompilerParams(vmem_limit_bytes=mebibytes * 1024 * 1024)


SCALAR = pl.BlockSpec(memory_space=pltpu.SMEM)
ANYWHERE = pl.BlockSpec(memory_space=pl.ANY)
IN_HBM = pl.BlockSpec(memory_space=pltpu.HBM)
RATE_FIRST = 16
RATE_SECOND = 0.001
RATE_LOCAL = ((.01,.01),(1,16))
RATE_USE = ((4,4),(4,4))
RATE_LAST = ((16,4),(4,4))
RATE_MERGE = (4,4)


def cost(microseconds, rate=16):
    return pl.CostEstimate(flops=int(microseconds * rate * 10**9), bytes_accessed=1, transcendentals=0)


def chunk_heads(half):
    return (half // 2, half - half // 2)


def line_device(queries, keys_in, value_input, level_gain, decay_log, out_grad):
    heads, tok = decay_log.shape
    dim = queries.shape[1] // heads
    half = heads // 2
    counts = chunk_heads(half)
    parts = range(len(counts))
    lows = [sum(counts[:part]) for part in parts]
    inner = tok.bit_length()
    place = lax.axis_index("ctx").astype(jnp.int32).reshape(1)
    tokens = (queries, keys_in, value_input, out_grad)
    inputs = (place, *tokens, level_gain, decay_log)
    core_swap = [(at, at ^ 1) for at in range(8)]
    side_swap = [(at, at ^ 2) for at in range(8)]
    middle_swap = [(0, 1), (1, 0), (2, 4), (4, 2), (3, 5), (5, 3), (6, 7), (7, 6)]

    def swap(block, route):
        return lax.ppermute(block, "ctx", route)

    def call(kernel, out_shape, operands, unread=(), spent=None, name=None, **options):
        return pl.pallas_call(
            kernel,
            out_shape=out_shape,
            in_specs=[SCALAR] + [pl.BlockSpec()] * (len(operands) - 1) + [ANYWHERE] * len(unread),
            compiler_params=params(),
            cost_estimate=spent,
            name=name,
            **options,
        )(*operands, *unread)

    found = pl.pallas_call(
        first_export_kernel,
        out_shape=tuple(
            pltpu.VMEM((count * dim + (0 if part else heads), dim), F32)
            for part, count in enumerate(counts)
        )
        + tuple(pltpu.VMEM(array.shape, array.dtype) for array in inputs[1:]),
        in_specs=[SCALAR] + [IN_HBM] * 6,
        scratch_shapes=[pltpu.SemaphoreType.DMA((10,))],
        compiler_params=params(),
        cost_estimate=cost(2),
        name="first_exports",
    )(place, *(pltpu.with_memory_space_constraint(array, pltpu.HBM) for array in inputs[1:]))
    send1, kept = found[: len(counts)], found[len(counts) :]
    inputs = (place, *kept)
    decay_log = kept[-1]
    got1 = [swap(block, core_swap) for block in send1]
    keep1, totals = call(
        own_export_kernel,
        (sds(half * dim, dim), sds(heads, tok)),
        inputs,
        (send1[0],),
        cost(0.8, RATE_FIRST),
        "own_exports",
    )

    def first_merge(part, *unread):
        return call(
            functools.partial(first_merge_kernel, lows[part]),
            sds(counts[part] * dim + (0 if part else heads), dim),
            (place, totals, got1[0], keep1, got1[part]),
            unread,
            cost(0.2, RATE_FIRST),
            "first_merge",
        )

    first_sent = [first_merge(0)]
    first = [swap(first_sent[0], side_swap)]

    local_done = {}

    def local(part, mine, *unread):
        count = counts[part]
        local_done[part, mine] = call(
            functools.partial(local_kernel, lows[part], mine),
            (sds(tok, count * dim),) * 4 + (sds(inner, count, tok), sds(count, tok)),
            inputs,
            unread,
            cost(0.4 * count, RATE_LOCAL[part][not mine]),
            "local",
        )
        return local_done[part, mine][-1]

    done = first_sent[-1]
    *send2, keep2, bundle, factors = call(
        second_export_kernel,
        tuple(sds(count * dim, dim) for count in counts)
        + (sds(half * dim, dim), sds(4 * half * dim, dim), sds(3 * half, tok)),
        (*inputs, keep1, got1[0]),
        (done,),
        cost(1.6, RATE_SECOND),
        "second_exports",
    )
    got2 = [swap(block, core_swap) for block in send2]

    def second_merge(part, *unread):
        return pl.pallas_call(
            functools.partial(second_merge_kernel, lows[part]),
            out_shape=sds(counts[part] * dim, dim),
            in_specs=[pl.BlockSpec()] * 4 + [ANYWHERE] * len(unread),
            compiler_params=params(),
            cost_estimate=cost(0.3, RATE_MERGE[part]),
            name="second_merge",
        )(factors, keep2, got2[part], first[part], *unread)

    done = local(0, True, keep2)
    first_sent.append(first_merge(1, done))
    first.append(swap(first_sent[1], side_swap))
    done = local(0, False, done)
    sent = [second_merge(0, done, *got2[1:])]
    done = local(1, True, sent[0])
    sent.append(second_merge(1, done))
    front = swap(bundle, core_swap)
    second = [swap(block, middle_swap) for block in sent]
    third = [swap(second[0], side_swap)]
    second_over = [swap(second[0], core_swap)]
    done = local(1, False, second[0])

    used = {}

    def first_use(part, mine, *unread):
        count = counts[part]
        used[part, mine] = call(
            functools.partial(first_use_kernel, lows[part], mine),
            (sds(tok, count * dim),) * 4 + (sds(4 * count, tok),),
            (
                *inputs,
                got1[0],
                got1[part],
                (first if mine else first_over)[part],
                (second if mine else second_over)[part],
                got2[part],
                front,
                *local_done[part, mine][:4],
            ),
            unread,
            cost(0.3 * count, RATE_USE[part][not mine]),
            "first_use",
        )
        return used[part, mine][-1]

    results = ()
    last_rows, held = [], {}

    def last_use(part, mine, ending=False):
        nonlocal results
        count = counts[part]
        operands = (
            *inputs,
            got1[0],
            got1[part],
            first[0],
            (second if mine else second_over)[part],
            (third if mine else third_over)[part],
            front,
            *used[part, mine][:4],
        )
        order = [(at, side) for at in parts for side in (True, False)]
        rows = ()
        if ending:
            rows = (
                *(local_done[key][4] for key in order),
                *(local_done[key][5] for key in order),
                *(used[key][4] for key in order),
                *last_rows,
            )
        if mine:
            *found, last = call(
                functools.partial(last_use_kernel, lows[part], mine, None),
                (sds(tok, count * dim, dtype=BF16),) * 4 + (sds(3 * count, tok),),
                operands,
                spent=cost(0.15 * count, RATE_LAST[part][0]),
                name="last_use",
            )
            held[part] = found
            last_rows.append(last)
            return
        operands = (*operands, *held[part])
        before = len(operands) + len(rows)
        tail = (sds(*level_gain.shape), sds(heads, tok)) if ending else (sds(3 * count, tok),)
        ending_scratch = [
            pltpu.VMEM(level_gain.shape, F32),
            pltpu.VMEM((heads, tok), F32),
            pltpu.SemaphoreType.DMA((3,)),
        ]
        found = pl.pallas_call(
            functools.partial(last_use_kernel, lows[part], mine, counts if ending else None),
            out_shape=(sds(tok, heads * dim, dtype=BF16),) * 4 + tail,
            in_specs=[SCALAR] + [pl.BlockSpec()] * (before - 1) + [ANYWHERE] * len(results),
            out_specs=(ANYWHERE,) * 4 + (ANYWHERE if ending else pl.BlockSpec(),) * len(tail),
            input_output_aliases={before + at: at for at in range(len(results))},
            scratch_shapes=[
                pltpu.VMEM((4, tok, count * dim), BF16),
                pltpu.SemaphoreType.DMA((4 * count + 4,)),
            ]
            + ending_scratch * ending,
            compiler_params=params(),
            cost_estimate=cost(0.25 * count, RATE_LAST[part][1]),
            name="last_use",
        )(*operands, *rows, *results)
        results = found[:4]
        last_rows.extend(found[4:])

    done = first_use(0, True, done)
    first_over = [swap(after(first[0], second[0]), core_swap)]
    done = first_use(0, False, done)
    second[1] = after(second[1], done)
    third.append(swap(second[1], side_swap))
    second_over.append(swap(second[1], core_swap))
    first_over.append(swap(after(first[1], second[1]), core_swap))
    done = first_use(1, True, done)
    third_over = [swap(after(third[0], done), core_swap)]
    done = first_use(1, False, done)
    last_use(0, True)
    last_use(0, False)
    third_over.append(swap(after(third[1], done, last_rows[-1]), core_swap))
    last_use(1, True)
    last_use(1, False, ending=True)
    return (*results, *last_rows[-2:])


def solution(mesh):
    placed = (
        P(("seq", "ctx"), None),
        P(("seq", "ctx"), None),
        P(("seq", "ctx"), None),
        P(None, None, ("seq", "ctx")),
        P(None, ("seq", "ctx")),
        P(("seq", "ctx"), None),
    )
    return jax.shard_map(
        line_device if mesh.shape["ctx"] == 8 else per_device,
        mesh=mesh,
        in_specs=placed,
        out_specs=(
            P(("seq", "ctx"), None),
            P(("seq", "ctx"), None),
            P(("seq", "ctx"), None),
            P(("seq", "ctx"), None),
            P(None, None, ("seq", "ctx")),
            P(None, ("seq", "ctx")),
        ),
        check_vma=False,
    )
```

```python
import functools

import jax
import jax.numpy as jnp
from jax import lax
from jax.experimental import pallas as pl
from jax.experimental.pallas import tpu as pltpu
from jax.sharding import PartitionSpec as P

TOP_ACCURACY = lax.Precision.HIGHEST


def from_partner(block, axis, distance):
    count = lax.axis_size(axis)
    route = []
    for low in range(count):
        high = low | 1 << distance
        if high != low and high < count:
            route += [(low, high), (high, low)]
    return lax.ppermute(block, axis, route)


def passed_along(value, axis, steps):
    count = lax.axis_size(axis)
    first, last = (max(0, -steps), min(count, count - steps))
    return lax.ppermute(value, axis, [(source, source + steps) for source in range(first, last)])


def level_table(tok, lvl_in):
    places = jnp.arange(tok, dtype=jnp.int32)
    mixing = jnp.bitwise_xor(places[:, None], places[None, :])
    table = jnp.zeros((tok, tok), jnp.int32)
    for power in range(lvl_in):
        table = table + (mixing >= 2**power).astype(jnp.int32)
    return table


def block_front(keys_h, value_rows_head, decay):
    running = jnp.cumsum(decay, axis=1)
    total_sum = running[:, -1]
    scaled_result = keys_h * jnp.exp(total_sum[:, None] - running)[:, :, None]
    return (
        jnp.einsum("ybu,ybe->yue", scaled_result, value_rows_head, precision=TOP_ACCURACY),
        total_sum,
    )


def block_output(queries_h, keys_h, value_rows_head, gain, decay, buckets):
    tok = queries_h.shape[1]
    lvl_in = tok.bit_length() - 1
    running = jnp.cumsum(decay, axis=1)
    places = jnp.arange(tok, dtype=jnp.int32)
    causal = places[:, None] >= places[None, :]
    spread_gap = jnp.where(causal[None], running[:, :, None] - running[:, None, :], 0.0)
    fading = jnp.where(causal[None], jnp.exp(spread_gap), 0.0)
    table = level_table(tok, lvl_in)
    picks = (table[None] == jnp.arange(lvl_in + 1, dtype=jnp.int32)[:, None, None]).astype(
        jnp.float32
    )
    weighting = jnp.einsum("lij,lhi->hij", picks, gain[: lvl_in + 1], precision=TOP_ACCURACY)
    scores = jnp.einsum("hik,hjk->hij", queries_h, keys_h, precision=TOP_ACCURACY)
    result = jnp.einsum(
        "hij,hjv->hiv", scores * weighting * fading, value_rows_head, precision=TOP_ACCURACY
    )
    lifted = queries_h * jnp.exp(running)[:, :, None]
    reach = gain[lvl_in + 1 :][:, :, :, None] * lifted[None]
    return result + jnp.einsum("jhik,jhkv->hiv", reach, buckets, precision=TOP_ACCURACY)


def merge_step(own_total, own_state, offset, other_total, other_state, is_upper):
    bucket = jnp.where(is_upper, jnp.exp(offset)[:, None, None] * other_state, 0.0)
    low_state = jnp.where(is_upper, other_state, own_state)
    high_state = jnp.where(is_upper, own_state, other_state)
    high_total = jnp.where(is_upper, own_total, other_total)
    merged = jnp.exp(high_total)[:, None, None] * low_state + high_state
    new_offset = offset + jnp.where(is_upper, other_total, 0.0)
    return (own_total + other_total, merged, new_offset, bucket)


def partner_grads(
    own_total, own_state, offset, other_total, g_total, g_state, g_offset, g_bucket, is_upper
):
    factor = jnp.exp(jnp.where(is_upper, own_total, other_total))
    d_other_state = jnp.where(
        is_upper,
        factor[:, None, None] * g_state + jnp.exp(offset)[:, None, None] * g_bucket,
        g_state,
    )
    lower_term = factor * jnp.sum(g_state * own_state, axis=(1, 2))
    d_other_total = g_total + jnp.where(is_upper, g_offset, lower_term)
    return (d_other_total, d_other_state)


def own_grads(
    own_total, offset, other_total, other_state, g_total, g_state, g_offset, g_bucket, is_upper
):
    factor = jnp.exp(jnp.where(is_upper, own_total, other_total))
    d_own_state = jnp.where(is_upper, g_state, factor[:, None, None] * g_state)
    upper_total = factor * jnp.sum(g_state * other_state, axis=(1, 2))
    d_own_total = g_total + jnp.where(is_upper, upper_total, 0.0)
    upper_offset = jnp.exp(offset) * jnp.sum(g_bucket * other_state, axis=(1, 2))
    d_offset = g_offset + jnp.where(is_upper, upper_offset, 0.0)
    return (d_own_total, d_own_state, d_offset)


def to_heads(block, heads):
    tokens, width = block.shape
    return block.reshape(tokens, heads, width // heads).transpose(1, 0, 2).astype(jnp.float32)


def from_heads(block):
    heads, tokens, head_dim = block.shape
    return block.transpose(1, 0, 2).reshape(tokens, heads * head_dim)


def per_device(queries, keys_in, value_input, level_gain, decay_log, out_grad):
    heads = decay_log.shape[0]
    query_h = to_heads(queries, heads)
    key_h = to_heads(keys_in, heads)
    value_h = to_heads(value_input, heads)
    cotangent = to_heads(out_grad, heads)
    count = lax.axis_size("ctx")
    depth = count.bit_length() - 1
    position = lax.axis_index("ctx")
    (state, total_sum), front_back = jax.vjp(block_front, key_h, value_h, decay_log)
    own_total = total_sum
    own_state = state
    offset = jnp.zeros_like(total_sum)
    saved = []
    found = []
    top_other = state
    for bit in range(depth):
        other_total, other_state = from_partner((own_total, own_state), "ctx", bit)
        is_upper = jnp.right_shift(position, bit) % 2 == 1
        saved.append((own_total, own_state, offset, other_total))
        if bit == depth - 1:
            top_other = other_state
        own_total, own_state, offset, bucket = merge_step(
            own_total, own_state, offset, other_total, other_state, is_upper
        )
        found.append(bucket)
    buckets = jnp.stack(found)
    mixed, out_back = jax.vjp(block_output, query_h, key_h, value_h, level_gain, decay_log, buckets)
    grad_query, grad_key, grad_value, grad_gain, grad_decay, bucket_gradient = out_back(cotangent)
    grad_total = jnp.zeros_like(total_sum)
    grad_state = jnp.zeros_like(state)
    grad_offset = jnp.zeros_like(total_sum)
    for bit in reversed(range(depth)):
        is_upper = jnp.right_shift(position, bit) % 2 == 1
        level_total, level_state, level_offset, level_other_total = saved[bit]
        d_other_total, d_other_state = partner_grads(
            level_total,
            level_state,
            level_offset,
            level_other_total,
            grad_total,
            grad_state,
            grad_offset,
            bucket_gradient[bit],
            is_upper,
        )
        if bit == depth - 1:
            back_total, back_state = passed_along(
                (d_other_total, d_other_state), "ctx", -(count // 2)
            )
            partner_state = top_other
        else:
            back_total, back_state, partner_state = from_partner(
                (d_other_total, d_other_state, level_state), "ctx", bit
            )
        d_own_total, d_own_state, d_offset = own_grads(
            level_total,
            level_offset,
            level_other_total,
            partner_state,
            grad_total,
            grad_state,
            grad_offset,
            bucket_gradient[bit],
            is_upper,
        )
        grad_total = d_own_total + back_total
        grad_state = d_own_state + back_state
        grad_offset = d_offset
    key_more, value_more, decay_more = front_back((grad_state, grad_total))
    return (
        from_heads(mixed).astype(jnp.bfloat16),
        from_heads(grad_query).astype(jnp.bfloat16),
        from_heads(grad_key + key_more).astype(jnp.bfloat16),
        from_heads(grad_value + value_more).astype(jnp.bfloat16),
        grad_gain,
        grad_decay + decay_more,
    )


F32 = jnp.float32
BF16 = jnp.bfloat16
NT = (((1,), (1,)), ((), ()))
TN = (((0,), (0,)), ((), ()))
NN = (((1,), (0,)), ((), ()))
NEVER = -1e30


def mxu(left, right, dims):
    return lax.dot_general(left, right, dims, preferred_element_type=F32)


def halves(value):
    high = value.astype(BF16)
    low = (value - high.astype(F32)).astype(BF16)
    return high, low


def split_rows(value):
    return jnp.concatenate(halves(value), axis=0)


def split_lanes(value):
    return jnp.concatenate(halves(value), axis=1)


def twice_rows(value):
    return jnp.concatenate([value, value], axis=0)


def twice_lanes(value):
    return jnp.concatenate([value, value], axis=1)


def running_decay(decay):
    tok = decay.shape[1]
    earlier = lax.broadcasted_iota(jnp.int32, (tok, tok), 0)
    later = lax.broadcasted_iota(jnp.int32, (tok, tok), 1)
    upto = (earlier <= later).astype(BF16)
    high, _ = halves(decay)
    middle, low = halves(decay - high.astype(F32))
    return mxu(
        jnp.concatenate([high, middle, low], axis=1),
        jnp.concatenate([upto, upto, upto], axis=0),
        NN,
    )


def last_lane(running):
    return jnp.broadcast_to(running[:, running.shape[1] - 1 :], running.shape)


def columns(rows):
    count, tok = rows.shape
    if count < tok:
        rows = jnp.concatenate([rows, jnp.zeros((tok - count, tok), rows.dtype)], axis=0)
    return rows.T


def half_first(rows, core):
    half = rows.shape[0] // 2
    swapped = jnp.concatenate([rows[half:], rows[:half]], axis=0)
    return jnp.where(core == 0, rows, swapped)


def lane_block(ref, head, width):
    return ref[:, pl.ds(pl.multiple_of(head * width, width), width)]


def take_half(rows, core, low, count):
    half = rows.shape[0] // 2
    return jnp.where(core == 0, rows[low : low + count], rows[half + low : half + low + count])


def outer_products(left, right, weight_column):
    turned = left.T
    return mxu(twice_lanes(turned), split_rows(right.astype(F32) * weight_column), NN)


def first_export_half(state, core, weight, query, key, value, cotangent, outs, ready):
    heads, tok = weight.shape
    dim = query.shape[1] // heads
    half = heads // 2
    spread = columns(half_first(weight, core))
    targets = [(out, row) for out in outs for row in range(out.shape[0] // dim)]

    def products(left, right):
        for index in range(half):
            head = core * half + index
            out, row = targets[index]
            out[pl.ds(row * dim, dim), :] = outer_products(
                lane_block(left, head, dim),
                lane_block(right, head, dim),
                spread[:, index : index + 1],
            )

    @pl.when(state)
    def _():
        ready(key, value)
        products(key, value)

    @pl.when(jnp.logical_not(state))
    def _():
        ready(query, cotangent)
        products(query, cotangent)


def first_weights(position, gain, decay):
    chip = position // 2
    cross = gain.shape[0] - 3
    running = decay[...]
    total = last_lane(running)
    weight = jnp.where(
        chip % 2 == 0,
        jnp.exp(total - running),
        jnp.where(chip == 1, gain[cross + 1], gain[cross + 2]) * jnp.exp(running),
    )
    return weight, total


def first_export_kernel(
    place, query, key, value, cotangent, gain, decay, *rest
):
    sends, kept, raw, sems = rest[:-8], rest[-8:-2], rest[-2], rest[-1]
    position = place[0]
    core = position % 2
    heads, tok = decay.shape
    half = heads // 2
    wide = query.shape[1] // 2
    state = position // 2 % 2 == 0
    sources = (query, key, value, cotangent)
    names = ("query", "key", "value", "cotangent")
    moves = {}
    for number, (name, source, target) in enumerate(zip(names, sources, kept)):
        for side in range(2):
            lanes = pl.ds(pl.multiple_of((1 - core if side == 0 else core) * wide, wide), wide)
            moves[name, side] = pltpu.make_async_copy(
                source.at[:, lanes], target.at[:, lanes], sems.at[2 * number + side]
            )
    small = [
        pltpu.make_async_copy(source, target, sems.at[8 + number])
        for number, (source, target) in enumerate(zip((gain, decay), (kept[4], raw)))
    ]
    for move in small:
        move.start()

    def start(*order):
        for side in range(2):
            for name in order:
                moves[name, side].start()

    @pl.when(state)
    def _():
        start("key", "value")
        start("query", "cotangent")

    @pl.when(jnp.logical_not(state))
    def _():
        start("query", "cotangent")
        start("key", "value")

    for move in small:
        move.wait()
    kept[5][...] = running_decay(raw[...])
    weight, total = first_weights(position, *kept[4:])
    sends[0][pl.ds(sends[0].shape[0] - heads, heads), :] = total

    def ready(left, right):
        for name, target in zip(names, kept):
            if target is left or target is right:
                moves[name, 0].wait()

    first_export_half(state, 1 - core, weight, *kept[:4], sends, ready)

    @pl.when(state)
    def _():
        for name in ("query", "cotangent"):
            moves[name, 0].wait()

    @pl.when(jnp.logical_not(state))
    def _():
        for name in ("key", "value"):
            moves[name, 0].wait()

    for name in names:
        moves[name, 1].wait()


def own_export_kernel(place, query, key, value, cotangent, gain, decay, after, keep, totals):
    position = place[0]
    weight, total = first_weights(position, gain, decay)
    totals[...] = total
    first_export_half(
        position // 2 % 2 == 0,
        position % 2,
        weight,
        query,
        key,
        value,
        cotangent,
        [keep],
        lambda left, right: None,
    )


def second_core(position):
    return jnp.bitwise_xor(position % 2, (position // 2 == 3).astype(jnp.int32))


def second_export_kernel(
    place, query, key, value, cotangent, gain, decay, keep1, first_got, after, *outs
):
    *sends, keep, bundle, factors = outs
    position = place[0]
    core = second_core(position)
    chip = position // 2
    heads, tok = decay.shape
    dim = query.shape[1] // heads
    half = heads // 2
    cross = gain.shape[0] - 3
    running = decay[...]
    lift = jnp.exp(running)
    fall = jnp.exp(last_lane(running) - running)
    state2 = chip == 1
    state0 = position % 2 == 0
    weight2 = jnp.where(state2, fall, jnp.where(chip == 2, gain[cross + 2], gain[cross + 1]) * lift)
    weight2 = jnp.where(chip == 0, 0.0, weight2)
    weight0 = jnp.where(state0, fall, gain[cross] * lift)
    spread = columns(jnp.concatenate([half_first(weight2, 1 - core), weight0], axis=0))
    own_total = last_lane(running)
    other_total = first_got[pl.ds(first_got.shape[0] - heads, heads), :]
    inner = (chip == 1) | (chip == 2)
    merged = (
        *pair_factors(position, own_total, other_total, chip == 1),
        jnp.where(inner, jnp.exp(own_total + other_total), 0.0),
    )
    for kind, rows in enumerate(merged):
        factors[kind * half : (kind + 1) * half, :] = half_first(rows, core)[:half]
    bundle[pl.ds(heads * dim, half * dim), :] = keep1[...]
    place_of = [(part, row) for part, send in enumerate(sends) for row in range(send.shape[0] // dim)]
    for index in range(heads):
        mine = index >= half
        head = (core if mine else 1 - core) * half + index % half
        q, k, v, o = (lane_block(ref, head, dim) for ref in (query, key, value, cotangent))
        second = outer_products(
            jnp.where(state2, k, q), jnp.where(state2, v, o), spread[:, index : index + 1]
        )
        if mine:
            keep[pl.ds(index % half * dim, dim), :] = second
            bundle[pl.ds((heads + index) * dim, dim), :] = second
        else:
            part, row = place_of[index]
            sends[part][pl.ds(row * dim, dim), :] = second
    for head in range(heads):
        lanes = slice(head * dim, (head + 1) * dim)
        q, k, v, o = (ref[:, lanes] for ref in (query, key, value, cotangent))
        bundle[pl.ds(head * dim, dim), :] = outer_products(
            jnp.where(state0, k, q),
            jnp.where(state0, v, o),
            spread[:, heads + head : heads + head + 1],
        )


def pair_factors(position, own_total, other_total, is_state):
    even = position % 2 == 0
    scale_own = is_state == even
    return (
        jnp.where(scale_own, jnp.exp(other_total), 1.0),
        jnp.where(scale_own, 1.0, jnp.exp(own_total)),
    )


def first_merge_kernel(low, place, totals, first_got, keep, got, *rest):
    out = rest[-1]
    position = place[0]
    chip = position // 2
    heads, dim = totals.shape[0], keep.shape[1]
    own_total = totals[...]
    other_total = first_got[pl.ds(first_got.shape[0] - heads, heads), :]
    count = out.shape[0] // dim
    factors = pair_factors(position, own_total, other_total, chip % 2 == 0)
    own_factor, other_factor = (take_half(rows, position % 2, low, count) for rows in factors)
    for index in range(count):
        rows = pl.ds(index * dim, dim)
        one = slice(index, index + 1)
        out[rows, :] = (
            own_factor[one] * keep[pl.ds((low + index) * dim, dim), :]
            + other_factor[one] * got[rows, :]
        )
    if low == 0:
        out[pl.ds(count * dim, heads), :] = own_total + other_total


def second_merge_kernel(low, factors, keep, got, first, *rest):
    out = rest[-1]
    dim = keep.shape[1]
    half = keep.shape[0] // dim
    for index in range(out.shape[0] // dim):
        rows = pl.ds(index * dim, dim)
        own, other, earlier = (
            factors[kind * half + low + index : kind * half + low + index + 1, :] for kind in range(3)
        )
        out[rows, :] = (
            own * keep[pl.ds((low + index) * dim, dim), :]
            + other * got[rows, :]
            + earlier * first[rows, :]
        )


def lane_sums(value):
    ones = jnp.ones((2 * value.shape[1], value.shape[1]), BF16)
    return mxu(split_lanes(value), ones, NN)


def row_sums(value):
    ones = jnp.ones((16, 2 * value.shape[1]), BF16)
    return mxu(ones, split_lanes(value), NT)[:1]


def apply_state(left, right, state, weight, summed=lane_sums):
    high, low = halves(state)
    first = mxu(twice_lanes(left), jnp.concatenate([high, low], axis=0), NN)
    second = mxu(twice_lanes(right), jnp.concatenate([high, low], axis=1), NT)
    sums = summed(first * right.astype(F32))
    return weight * first, weight * second, sums


def local_kernel(low, mine, place, query, key, value, cotangent, gain, decay, *rest):
    acc_out, acc_query, acc_key, acc_value, gain_rows, decay_rows = rest[-6:]
    core = place[0] % 2
    side = core if mine else 1 - core
    heads, tok = decay.shape
    count = decay_rows.shape[0]
    dim = query.shape[1] // heads
    inner_levels = tok.bit_length()
    running = take_half(decay[...], side, low, count)
    gains = [take_half(gain[place_in], side, low, count) for place_in in range(inner_levels)]
    spread = columns(running)
    source = lax.broadcasted_iota(jnp.int32, (tok, tok), 0)
    target = lax.broadcasted_iota(jnp.int32, (tok, tok), 1)
    mixing = jnp.bitwise_xor(source, target)
    level = jnp.zeros((tok, tok), jnp.int32)
    for power in range(inner_levels - 1):
        level = level + (mixing >= 2**power).astype(jnp.int32)
    causal = source <= target
    level = jnp.where(causal, level, -1)
    gathered = jnp.zeros((tok, tok), F32)
    for index in range(count):
        lanes = slice(index * dim, (index + 1) * dim)
        one = slice(index, index + 1)
        head = side * (heads // 2) + low + index
        q, k, v, o = (lane_block(ref, head, dim) for ref in (query, key, value, cotangent))
        scores = mxu(k, q, NT)
        pulls = mxu(v, o, NT)
        fading = jnp.exp(jnp.where(causal, running[one] - spread[:, one], NEVER))
        weighting = jnp.zeros((tok, tok), F32)
        for place_in in range(inner_levels):
            weighting = jnp.where(level == place_in, gains[place_in][one], weighting)
        weighting = weighting * fading
        mixing_part = scores * weighting
        score_grad = pulls * weighting
        product = scores * pulls * fading
        flow = jnp.zeros((1, tok), F32)
        for place_in in range(inner_levels):
            found = jnp.sum(jnp.where(level == place_in, product, 0.0), axis=0, keepdims=True)
            gain_rows[place_in, one, :] = found
            if place_in > 0:
                flow = flow + gains[place_in][one] * found
        decay_rows[one, :] = flow
        left = jnp.where(level > 0, mixing_part * pulls, 0.0)
        gathered = jnp.where(target == index, lane_sums(left), gathered)
        high, low_part = halves(mixing_part)
        acc_out[:, lanes] = mxu(jnp.concatenate([high, low_part], axis=0), twice_rows(v), TN)
        acc_value[:, lanes] = mxu(jnp.concatenate([high, low_part], axis=1), twice_rows(o), NN)
        high, low_part = halves(score_grad)
        acc_query[:, lanes] = mxu(jnp.concatenate([high, low_part], axis=0), twice_rows(k), TN)
        acc_key[:, lanes] = mxu(jnp.concatenate([high, low_part], axis=1), twice_rows(q), NN)
    decay_rows[...] = decay_rows[...] - gathered.T[:count]


def use_rows(rows_out, uses, gathered, extra):
    turned = gathered.T
    count = extra.shape[0]
    decay_row = jnp.zeros((count, turned.shape[1]), F32)
    flow_row = extra
    for number, (forward, weight, lift) in enumerate(uses):
        sums = turned[number * count : (number + 1) * count]
        weighted = weight * sums
        decay_row = decay_row + jnp.where(forward, weighted, -weighted)
        flow_row = flow_row + jnp.where(forward, 0.0, weighted)
        rows_out[(2 + number) * count : (3 + number) * count, :] = lift * sums
    rows_out[:count, :] = decay_row
    rows_out[count : 2 * count, :] = flow_row


def first_use_kernel(
    low,
    mine,
    place,
    query,
    key,
    value,
    cotangent,
    gain,
    decay,
    first_got,
    pair_got,
    first,
    second,
    second_got,
    front,
    acc_out,
    acc_query,
    acc_key,
    acc_value,
    *rest,
):
    out_mixed, out_query, out_key, out_value, rows_out = rest[-5:]
    position = place[0]
    core = position % 2
    side = core if mine else 1 - core
    chip = position // 2
    heads, tok = decay.shape
    half = heads // 2
    dim = query.shape[1] // heads
    count = acc_out.shape[1] // dim
    cross = gain.shape[0] - 3
    running = decay[...]
    total = last_lane(running)
    other = first_got[pl.ds(first_got.shape[0] - heads, heads), :]
    odd = core == 1
    forward = chip != 0
    offset = jnp.where(forward == odd, other, 0.0)
    lift0 = jnp.exp(running)
    lift = jnp.exp(running + offset)
    fall0 = jnp.exp(total - running)
    weight0 = jnp.where(odd, gain[cross] * lift0, fall0)
    weight = jnp.where(
        forward,
        jnp.where(chip == 2, gain[cross + 2], gain[cross + 1]) * lift,
        jnp.exp(total - running + offset),
    )
    pair_flow = jnp.where(forward != odd, jnp.exp(total), 0.0)
    chip_flow = jnp.where((chip == 1) | (chip == 2), jnp.exp(total + other), 0.0)
    lift0, lift, weight0, weight, pair_flow, chip_flow = (
        take_half(rows, side, low, count)
        for rows in (jnp.where(odd, lift0, 0.0), lift, weight0, weight, pair_flow, chip_flow)
    )
    spread = columns(jnp.concatenate([weight0, weight], axis=0))
    lane = lax.broadcasted_iota(jnp.int32, (tok, tok), 1)
    gathered = jnp.zeros((tok, tok), F32)
    flows = []
    for index in range(count):
        lanes = slice(index * dim, (index + 1) * dim)
        rows = pl.ds(index * dim, dim)
        one = slice(index, index + 1)
        head = side * half + low + index
        q, k, v, o = (lane_block(ref, head, dim) for ref in (query, key, value, cotangent))
        level0 = front[pl.ds(pl.multiple_of(head * dim, dim), dim), :]
        pair1 = pair_got[rows, :] if mine else front[pl.ds((heads + low + index) * dim, dim), :]
        pair2_kept = front[pl.ds((heads + half + low + index) * dim, dim), :]
        pair2 = jnp.where((chip == 3) == mine, pair2_kept, second_got[rows, :])
        state = jnp.where(chip == 2, second[rows, :], first[rows, :])
        partner = jnp.where(odd, level0, jnp.where(chip == 1, pair1, pair2))
        flows.append(
            pair_flow[one] * jnp.sum(state * partner, axis=0, keepdims=True)
            + chip_flow[one] * jnp.sum(first[rows, :] * second[rows, :], axis=0, keepdims=True)
        )
        left0, right0, sums = apply_state(
            jnp.where(odd, q, k), jnp.where(odd, o, v), level0, spread[:, one]
        )
        gathered = jnp.where(lane == index, sums, gathered)
        left, right, sums = apply_state(
            jnp.where(forward, q, k),
            jnp.where(forward, o, v),
            state,
            spread[:, count + index : count + index + 1],
        )
        gathered = jnp.where(lane == count + index, sums, gathered)
        out_mixed[:, lanes] = (
            acc_out[:, lanes] + jnp.where(odd, left0, 0.0) + jnp.where(forward, left, 0.0)
        )
        out_query[:, lanes] = (
            acc_query[:, lanes] + jnp.where(odd, right0, 0.0) + jnp.where(forward, right, 0.0)
        )
        out_value[:, lanes] = (
            acc_value[:, lanes] + jnp.where(odd, 0.0, left0) + jnp.where(forward, 0.0, left)
        )
        out_key[:, lanes] = (
            acc_key[:, lanes] + jnp.where(odd, 0.0, right0) + jnp.where(forward, 0.0, right)
        )
    use_rows(
        rows_out,
        ((odd, weight0, lift0), (forward, weight, lift)),
        gathered,
        jnp.concatenate(flows, axis=0),
    )


def last_use_kernel(
    low,
    mine,
    parts,
    place,
    query,
    key,
    value,
    cotangent,
    gain,
    decay,
    first_got,
    pair_got,
    chip_total,
    second,
    third,
    front,
    acc_out,
    acc_query,
    acc_key,
    acc_value,
    *rest,
):
    ending = parts is not None
    if ending:
        *rest, grad_gain, grad_decay, staged, sems, gain_stage, decay_stage, end_sems = rest
    elif mine:
        *rest, rows_out = rest
    else:
        *rest, rows_out, staged, sems = rest
    outs, before = rest[-4:], rest[:4]
    if not mine:
        rest = rest[4:]
    position = place[0]
    core = position % 2
    side = core if mine else 1 - core
    chip = position // 2
    heads, tok = decay.shape
    half = heads // 2
    dim = query.shape[1] // heads
    count = acc_out.shape[1] // dim
    cross = gain.shape[0] - 3
    running = decay[...]
    total = last_lane(running)
    other = first_got[pl.ds(first_got.shape[0] - heads, heads), :]
    chip_rows = chip_total[pl.ds(chip_total.shape[0] - heads, heads), :]
    odd = core == 1
    forward = chip == 3
    chip_offset = jnp.where((chip == 0) | (chip == 3), chip_rows, 0.0)
    offset = jnp.where(forward == odd, other, 0.0) + chip_offset
    lift = jnp.exp(running + offset)
    weight = jnp.where(forward, gain[cross + 2] * lift, jnp.exp(total - running + offset))
    pair_flow = jnp.where(forward != odd, jnp.exp(total + chip_offset), 0.0)
    lift, weight, pair_flow = (
        take_half(rows, side, low, count) for rows in (lift, weight, pair_flow)
    )
    spread = columns(weight)
    lane = lax.broadcasted_iota(jnp.int32, (tok, tok), 1)
    gathered = jnp.zeros((tok, tok), F32)
    flows, summed = [], []
    copies = []
    if not mine:
        wide = before[0].shape[1]
        start = pl.multiple_of(core * half * dim + low * dim, dim)
        for number in range(4):
            copy = pltpu.make_async_copy(
                before[number], outs[number].at[:, pl.ds(start, wide)], sems.at[4 * count + number]
            )
            copy.start()
            copies.append(copy)
    if ending:
        early = gain.shape[0] - 2
        copies.append(
            pltpu.make_async_copy(
                gain_stage.at[pl.ds(0, early)], grad_gain.at[pl.ds(0, early)], end_sems.at[0]
            )
        )
        early_gains(parts, rest[:-4], core, gain_stage)
        copies[-1].start()
    for index in range(count):
        lanes = slice(index * dim, (index + 1) * dim)
        rows = pl.ds(index * dim, dim)
        one = slice(index, index + 1)
        head = side * half + low + index
        q, k, v, o = (lane_block(ref, head, dim) for ref in (query, key, value, cotangent))
        state = jnp.where(chip == 1, second[rows, :], third[rows, :])
        level0 = front[pl.ds(pl.multiple_of(head * dim, dim), dim), :]
        if mine:
            pair1 = pair_got[rows, :]
        else:
            pair1 = front[pl.ds((heads + low + index) * dim, dim), :]
        partner = jnp.where(odd, level0, pair1)
        flows.append(pair_flow[one] * jnp.sum(state * partner, axis=0, keepdims=True))
        left, right, sums = apply_state(
            jnp.where(forward, q, k),
            jnp.where(forward, o, v),
            state,
            spread[:, one],
            row_sums if ending else lane_sums,
        )
        if ending:
            summed.append(sums)
        else:
            gathered = jnp.where(lane == index, sums, gathered)
        results = (
            acc_out[:, lanes] + jnp.where(forward, left, 0.0),
            acc_query[:, lanes] + jnp.where(forward, right, 0.0),
            acc_key[:, lanes] + jnp.where(forward, 0.0, right),
            acc_value[:, lanes] + jnp.where(forward, 0.0, left),
        )
        for number, result in enumerate(results):
            if mine:
                outs[number][:, lanes] = result.astype(BF16)
                continue
            staged[number, :, lanes] = result.astype(BF16)
            copy = pltpu.make_async_copy(
                staged.at[number, :, pl.ds(index * dim, dim)],
                outs[number].at[:, pl.ds(pl.multiple_of(head * dim, dim), dim)],
                sems.at[number * count + index],
            )
            copy.start()
            copies.append(copy)
    extra = jnp.concatenate(flows, axis=0)
    if not ending:
        use_rows(rows_out, ((forward, weight, lift),), gathered, extra)
    else:
        sums = jnp.concatenate(summed, axis=0)
        weighted = weight * sums
        own_rows = (
            jnp.where(forward, weighted, -weighted),
            extra + jnp.where(forward, 0.0, weighted),
            lift * sums,
        )
        finish(parts, rest[:-4], own_rows, core, chip, gain_stage, decay_stage)
        for copy in (
            pltpu.make_async_copy(
                gain_stage.at[pl.ds(early, 2)], grad_gain.at[pl.ds(early, 2)], end_sems.at[1]
            ),
            pltpu.make_async_copy(decay_stage, grad_decay, end_sems.at[2]),
        ):
            copy.start()
            copies.append(copy)
    for copy in copies:
        copy.wait()


def natural(pieces, core):
    return half_first(jnp.concatenate([*pieces[::2], *pieces[1::2]], axis=0), core)


def of_kind(counts, refs, number):
    return [
        ref[number * counts[at // 2] : (number + 1) * counts[at // 2], :]
        for at, ref in enumerate(refs)
    ]


def early_gains(counts, refs, core, grad_gain):
    levels = grad_gain.shape[0]
    groups = 2 * len(counts)
    for place_in in range(levels - 3):
        grad_gain[place_in] = natural([ref[place_in] for ref in refs[:groups]], core)
    first_rows = refs[2 * groups : 3 * groups]
    grad_gain[levels - 3] = natural(of_kind(counts, first_rows, 2), core)


def finish(counts, refs, own_rows, core, chip, grad_gain, grad_decay):
    levels, heads, tok = grad_gain.shape
    groups = 2 * len(counts)
    decay_rows, first_rows = refs[groups : 2 * groups], refs[2 * groups : 3 * groups]
    last_rows = refs[3 * groups : 4 * groups - 1]

    def last(number):
        return natural(of_kind(counts, last_rows, number) + [own_rows[number]], core)

    first, second = natural(of_kind(counts, first_rows, 3), core), last(2)
    grad_gain[levels - 2] = jnp.where(chip % 2 == 1, first, 0.0)
    grad_gain[levels - 1] = jnp.where(chip == 2, first, jnp.where(chip == 3, second, 0.0))
    own = natural([ref[...] for ref in decay_rows], core)
    own = own + natural(of_kind(counts, first_rows, 0), core) + last(0)
    later = natural(of_kind(counts, first_rows, 1), core) + last(1)
    upper = lax.broadcasted_iota(jnp.int32, (tok, tok), 0)
    lower = lax.broadcasted_iota(jnp.int32, (tok, tok), 1)
    from_here = (upper >= lower).astype(BF16)
    sums = jnp.concatenate([twice_rows(from_here), jnp.ones((2 * tok, tok), BF16)], axis=0)
    grad_decay[...] = mxu(
        jnp.concatenate([split_lanes(own), split_lanes(later)], axis=1), sums, NN
    )


def after(value, *others):
    return lax.optimization_barrier((value, *others))[0]


def sds(*shape, dtype=F32):
    return jax.ShapeDtypeStruct(shape, dtype)


FIRST_LIMIT = 24


def params(mebibytes=24):
    return pltpu.CompilerParams(vmem_limit_bytes=mebibytes * 1024 * 1024)


SCALAR = pl.BlockSpec(memory_space=pltpu.SMEM)
ANYWHERE = pl.BlockSpec(memory_space=pl.ANY)
IN_HBM = pl.BlockSpec(memory_space=pltpu.HBM)
RATE_FIRST = 16
RATE_SECOND = 0.001
RATE_LOCAL = ((.01,.01),(16,1))
RATE_USE = ((4,4),(4,4))
RATE_LAST = ((16,4),(4,4))
RATE_MERGE = (4,4)


def cost(microseconds, rate=16):
    return pl.CostEstimate(flops=int(microseconds * rate * 10**9), bytes_accessed=1, transcendentals=0)


def chunk_heads(half):
    return (half // 2, half - half // 2)


def line_device(queries, keys_in, value_input, level_gain, decay_log, out_grad):
    heads, tok = decay_log.shape
    dim = queries.shape[1] // heads
    half = heads // 2
    counts = chunk_heads(half)
    parts = range(len(counts))
    lows = [sum(counts[:part]) for part in parts]
    inner = tok.bit_length()
    place = lax.axis_index("ctx").astype(jnp.int32).reshape(1)
    tokens = (queries, keys_in, value_input, out_grad)
    inputs = (place, *tokens, level_gain, decay_log)
    core_swap = [(at, at ^ 1) for at in range(8)]
    side_swap = [(at, at ^ 2) for at in range(8)]
    middle_swap = [(0, 1), (1, 0), (2, 4), (4, 2), (3, 5), (5, 3), (6, 7), (7, 6)]

    def swap(block, route):
        return lax.ppermute(block, "ctx", route)

    def call(kernel, out_shape, operands, unread=(), spent=None, name=None, **options):
        return pl.pallas_call(
            kernel,
            out_shape=out_shape,
            in_specs=[SCALAR] + [pl.BlockSpec()] * (len(operands) - 1) + [ANYWHERE] * len(unread),
            compiler_params=params(),
            cost_estimate=spent,
            name=name,
            **options,
        )(*operands, *unread)

    found = pl.pallas_call(
        first_export_kernel,
        out_shape=tuple(
            pltpu.VMEM((count * dim + (0 if part else heads), dim), F32)
            for part, count in enumerate(counts)
        )
        + tuple(pltpu.VMEM(array.shape, array.dtype) for array in inputs[1:]),
        in_specs=[SCALAR] + [IN_HBM] * 6,
        scratch_shapes=[pltpu.VMEM((heads, tok), F32), pltpu.SemaphoreType.DMA((10,))],
        compiler_params=params(),
        cost_estimate=cost(2),
        name="first_exports",
    )(place, *(pltpu.with_memory_space_constraint(array, pltpu.HBM) for array in inputs[1:]))
    send1, kept = found[: len(counts)], found[len(counts) :]
    inputs = (place, *kept)
    got1 = [swap(block, core_swap) for block in send1]
    keep1, totals = call(
        own_export_kernel,
        (sds(half * dim, dim), sds(heads, tok)),
        inputs,
        (send1[0],),
        cost(0.8, RATE_FIRST),
        "own_exports",
    )

    def first_merge(part, *unread):
        return call(
            functools.partial(first_merge_kernel, lows[part]),
            sds(counts[part] * dim + (0 if part else heads), dim),
            (place, totals, got1[0], keep1, got1[part]),
            unread,
            cost(0.2, RATE_FIRST),
            "first_merge",
        )

    first_sent = [first_merge(0)]
    first = [swap(first_sent[0], side_swap)]

    local_done = {}

    def local(part, mine, *unread):
        count = counts[part]
        local_done[part, mine] = call(
            functools.partial(local_kernel, lows[part], mine),
            (sds(tok, count * dim),) * 4 + (sds(inner, count, tok), sds(count, tok)),
            inputs,
            unread,
            cost(0.4 * count, RATE_LOCAL[part][not mine]),
            "local",
        )
        return local_done[part, mine][-1]

    done = first_sent[-1]
    *send2, keep2, bundle, factors = call(
        second_export_kernel,
        tuple(sds(count * dim, dim) for count in counts)
        + (sds(half * dim, dim), sds(4 * half * dim, dim), sds(3 * half, tok)),
        (*inputs, keep1, got1[0]),
        (done,),
        cost(1.6, RATE_SECOND),
        "second_exports",
    )
    got2 = [swap(block, core_swap) for block in send2]

    def second_merge(part, *unread):
        return pl.pallas_call(
            functools.partial(second_merge_kernel, lows[part]),
            out_shape=sds(counts[part] * dim, dim),
            in_specs=[pl.BlockSpec()] * 4 + [ANYWHERE] * len(unread),
            compiler_params=params(),
            cost_estimate=cost(0.3, RATE_MERGE[part]),
            name="second_merge",
        )(factors, keep2, got2[part], first[part], *unread)

    done = local(0, True, keep2)
    first_sent.append(first_merge(1, done))
    first.append(swap(first_sent[1], side_swap))
    done = local(0, False, done)
    sent = [second_merge(0, done, *got2[1:])]
    done = local(1, True, sent[0])
    done = local(1, False, done)
    sent.append(second_merge(1, done))
    front = swap(bundle, core_swap)
    second = [swap(block, middle_swap) for block in sent]
    third = [swap(second[0], side_swap)]
    second_over = [swap(second[0], core_swap)]
    done = second[0]

    used = {}

    def first_use(part, mine, *unread):
        count = counts[part]
        used[part, mine] = call(
            functools.partial(first_use_kernel, lows[part], mine),
            (sds(tok, count * dim),) * 4 + (sds(4 * count, tok),),
            (
                *inputs,
                got1[0],
                got1[part],
                (first if mine else first_over)[part],
                (second if mine else second_over)[part],
                got2[part],
                front,
                *local_done[part, mine][:4],
            ),
            unread,
            cost(0.3 * count, RATE_USE[part][not mine]),
            "first_use",
        )
        return used[part, mine][-1]

    results = ()
    last_rows, held = [], {}

    def last_use(part, mine, ending=False):
        nonlocal results
        count = counts[part]
        operands = (
            *inputs,
            got1[0],
            got1[part],
            first[0],
            (second if mine else second_over)[part],
            (third if mine else third_over)[part],
            front,
            *used[part, mine][:4],
        )
        order = [(at, side) for at in parts for side in (True, False)]
        rows = ()
        if ending:
            rows = (
                *(local_done[key][4] for key in order),
                *(local_done[key][5] for key in order),
                *(used[key][4] for key in order),
                *last_rows,
            )
        if mine:
            *found, last = call(
                functools.partial(last_use_kernel, lows[part], mine, None),
                (sds(tok, count * dim, dtype=BF16),) * 4 + (sds(3 * count, tok),),
                operands,
                spent=cost(0.15 * count, RATE_LAST[part][0]),
                name="last_use",
            )
            held[part] = found
            last_rows.append(last)
            return
        operands = (*operands, *held[part])
        before = len(operands) + len(rows)
        tail = (sds(*level_gain.shape), sds(heads, tok)) if ending else (sds(3 * count, tok),)
        ending_scratch = [
            pltpu.VMEM(level_gain.shape, F32),
            pltpu.VMEM((heads, tok), F32),
            pltpu.SemaphoreType.DMA((3,)),
        ]
        found = pl.pallas_call(
            functools.partial(last_use_kernel, lows[part], mine, counts if ending else None),
            out_shape=(sds(tok, heads * dim, dtype=BF16),) * 4 + tail,
            in_specs=[SCALAR] + [pl.BlockSpec()] * (before - 1) + [ANYWHERE] * len(results),
            out_specs=(ANYWHERE,) * 4 + (ANYWHERE if ending else pl.BlockSpec(),) * len(tail),
            input_output_aliases={before + at: at for at in range(len(results))},
            scratch_shapes=[
                pltpu.VMEM((4, tok, count * dim), BF16),
                pltpu.SemaphoreType.DMA((4 * count + 4,)),
            ]
            + ending_scratch * ending,
            compiler_params=params(),
            cost_estimate=cost(0.25 * count, RATE_LAST[part][1]),
            name="last_use",
        )(*operands, *rows, *results)
        results = found[:4]
        last_rows.extend(found[4:])

    first_over = [swap(after(first[0], sent[0]), core_swap)]
    done = first_use(0, True, done, first_over[0])
    done = first_use(0, False, done)
    second[1] = after(second[1], done)
    third.append(swap(second[1], side_swap))
    second_over.append(swap(second[1], core_swap))
    first_over.append(swap(after(first[1], second[1]), core_swap))
    done = first_use(1, True, done)
    done = first_use(1, False, done)
    third_over = [swap(after(third[0], done), core_swap)]
    last_use(0, True)
    last_use(0, False)
    third_over.append(swap(after(third[1], done, last_rows[-1]), core_swap))
    last_use(1, True)
    last_use(1, False, ending=True)
    return (*results, *last_rows[-2:])


def solution(mesh):
    placed = (
        P(("seq", "ctx"), None),
        P(("seq", "ctx"), None),
        P(("seq", "ctx"), None),
        P(None, None, ("seq", "ctx")),
        P(None, ("seq", "ctx")),
        P(("seq", "ctx"), None),
    )
    return jax.shard_map(
        line_device if mesh.shape["ctx"] == 8 else per_device,
        mesh=mesh,
        in_specs=placed,
        out_specs=(
            P(("seq", "ctx"), None),
            P(("seq", "ctx"), None),
            P(("seq", "ctx"), None),
            P(("seq", "ctx"), None),
            P(None, None, ("seq", "ctx")),
            P(None, ("seq", "ctx")),
        ),
        check_vma=False,
    )
```

```python
import functools

import jax
import jax.numpy as jnp
from jax import lax
from jax.experimental import pallas as pl
from jax.experimental.pallas import tpu as pltpu
from jax.sharding import PartitionSpec as P

TOP_ACCURACY = lax.Precision.HIGHEST


def from_partner(block, axis, distance):
    count = lax.axis_size(axis)
    route = []
    for low in range(count):
        high = low | 1 << distance
        if high != low and high < count:
            route += [(low, high), (high, low)]
    return lax.ppermute(block, axis, route)


def passed_along(value, axis, steps):
    count = lax.axis_size(axis)
    first, last = (max(0, -steps), min(count, count - steps))
    return lax.ppermute(value, axis, [(source, source + steps) for source in range(first, last)])


def level_table(tok, lvl_in):
    places = jnp.arange(tok, dtype=jnp.int32)
    mixing = jnp.bitwise_xor(places[:, None], places[None, :])
    table = jnp.zeros((tok, tok), jnp.int32)
    for power in range(lvl_in):
        table = table + (mixing >= 2**power).astype(jnp.int32)
    return table


def block_front(keys_h, value_rows_head, decay):
    running = jnp.cumsum(decay, axis=1)
    total_sum = running[:, -1]
    scaled_result = keys_h * jnp.exp(total_sum[:, None] - running)[:, :, None]
    return (
        jnp.einsum("ybu,ybe->yue", scaled_result, value_rows_head, precision=TOP_ACCURACY),
        total_sum,
    )


def block_output(queries_h, keys_h, value_rows_head, gain, decay, buckets):
    tok = queries_h.shape[1]
    lvl_in = tok.bit_length() - 1
    running = jnp.cumsum(decay, axis=1)
    places = jnp.arange(tok, dtype=jnp.int32)
    causal = places[:, None] >= places[None, :]
    spread_gap = jnp.where(causal[None], running[:, :, None] - running[:, None, :], 0.0)
    fading = jnp.where(causal[None], jnp.exp(spread_gap), 0.0)
    table = level_table(tok, lvl_in)
    picks = (table[None] == jnp.arange(lvl_in + 1, dtype=jnp.int32)[:, None, None]).astype(
        jnp.float32
    )
    weighting = jnp.einsum("lij,lhi->hij", picks, gain[: lvl_in + 1], precision=TOP_ACCURACY)
    scores = jnp.einsum("hik,hjk->hij", queries_h, keys_h, precision=TOP_ACCURACY)
    result = jnp.einsum(
        "hij,hjv->hiv", scores * weighting * fading, value_rows_head, precision=TOP_ACCURACY
    )
    lifted = queries_h * jnp.exp(running)[:, :, None]
    reach = gain[lvl_in + 1 :][:, :, :, None] * lifted[None]
    return result + jnp.einsum("jhik,jhkv->hiv", reach, buckets, precision=TOP_ACCURACY)


def merge_step(own_total, own_state, offset, other_total, other_state, is_upper):
    bucket = jnp.where(is_upper, jnp.exp(offset)[:, None, None] * other_state, 0.0)
    low_state = jnp.where(is_upper, other_state, own_state)
    high_state = jnp.where(is_upper, own_state, other_state)
    high_total = jnp.where(is_upper, own_total, other_total)
    merged = jnp.exp(high_total)[:, None, None] * low_state + high_state
    new_offset = offset + jnp.where(is_upper, other_total, 0.0)
    return (own_total + other_total, merged, new_offset, bucket)


def partner_grads(
    own_total, own_state, offset, other_total, g_total, g_state, g_offset, g_bucket, is_upper
):
    factor = jnp.exp(jnp.where(is_upper, own_total, other_total))
    d_other_state = jnp.where(
        is_upper,
        factor[:, None, None] * g_state + jnp.exp(offset)[:, None, None] * g_bucket,
        g_state,
    )
    lower_term = factor * jnp.sum(g_state * own_state, axis=(1, 2))
    d_other_total = g_total + jnp.where(is_upper, g_offset, lower_term)
    return (d_other_total, d_other_state)


def own_grads(
    own_total, offset, other_total, other_state, g_total, g_state, g_offset, g_bucket, is_upper
):
    factor = jnp.exp(jnp.where(is_upper, own_total, other_total))
    d_own_state = jnp.where(is_upper, g_state, factor[:, None, None] * g_state)
    upper_total = factor * jnp.sum(g_state * other_state, axis=(1, 2))
    d_own_total = g_total + jnp.where(is_upper, upper_total, 0.0)
    upper_offset = jnp.exp(offset) * jnp.sum(g_bucket * other_state, axis=(1, 2))
    d_offset = g_offset + jnp.where(is_upper, upper_offset, 0.0)
    return (d_own_total, d_own_state, d_offset)


def to_heads(block, heads):
    tokens, width = block.shape
    return block.reshape(tokens, heads, width // heads).transpose(1, 0, 2).astype(jnp.float32)


def from_heads(block):
    heads, tokens, head_dim = block.shape
    return block.transpose(1, 0, 2).reshape(tokens, heads * head_dim)


def per_device(queries, keys_in, value_input, level_gain, decay_log, out_grad):
    heads = decay_log.shape[0]
    query_h = to_heads(queries, heads)
    key_h = to_heads(keys_in, heads)
    value_h = to_heads(value_input, heads)
    cotangent = to_heads(out_grad, heads)
    count = lax.axis_size("ctx")
    depth = count.bit_length() - 1
    position = lax.axis_index("ctx")
    (state, total_sum), front_back = jax.vjp(block_front, key_h, value_h, decay_log)
    own_total = total_sum
    own_state = state
    offset = jnp.zeros_like(total_sum)
    saved = []
    found = []
    top_other = state
    for bit in range(depth):
        other_total, other_state = from_partner((own_total, own_state), "ctx", bit)
        is_upper = jnp.right_shift(position, bit) % 2 == 1
        saved.append((own_total, own_state, offset, other_total))
        if bit == depth - 1:
            top_other = other_state
        own_total, own_state, offset, bucket = merge_step(
            own_total, own_state, offset, other_total, other_state, is_upper
        )
        found.append(bucket)
    buckets = jnp.stack(found)
    mixed, out_back = jax.vjp(block_output, query_h, key_h, value_h, level_gain, decay_log, buckets)
    grad_query, grad_key, grad_value, grad_gain, grad_decay, bucket_gradient = out_back(cotangent)
    grad_total = jnp.zeros_like(total_sum)
    grad_state = jnp.zeros_like(state)
    grad_offset = jnp.zeros_like(total_sum)
    for bit in reversed(range(depth)):
        is_upper = jnp.right_shift(position, bit) % 2 == 1
        level_total, level_state, level_offset, level_other_total = saved[bit]
        d_other_total, d_other_state = partner_grads(
            level_total,
            level_state,
            level_offset,
            level_other_total,
            grad_total,
            grad_state,
            grad_offset,
            bucket_gradient[bit],
            is_upper,
        )
        if bit == depth - 1:
            back_total, back_state = passed_along(
                (d_other_total, d_other_state), "ctx", -(count // 2)
            )
            partner_state = top_other
        else:
            back_total, back_state, partner_state = from_partner(
                (d_other_total, d_other_state, level_state), "ctx", bit
            )
        d_own_total, d_own_state, d_offset = own_grads(
            level_total,
            level_offset,
            level_other_total,
            partner_state,
            grad_total,
            grad_state,
            grad_offset,
            bucket_gradient[bit],
            is_upper,
        )
        grad_total = d_own_total + back_total
        grad_state = d_own_state + back_state
        grad_offset = d_offset
    key_more, value_more, decay_more = front_back((grad_state, grad_total))
    return (
        from_heads(mixed).astype(jnp.bfloat16),
        from_heads(grad_query).astype(jnp.bfloat16),
        from_heads(grad_key + key_more).astype(jnp.bfloat16),
        from_heads(grad_value + value_more).astype(jnp.bfloat16),
        grad_gain,
        grad_decay + decay_more,
    )


F32 = jnp.float32
BF16 = jnp.bfloat16
NT = (((1,), (1,)), ((), ()))
TN = (((0,), (0,)), ((), ()))
NN = (((1,), (0,)), ((), ()))
NEVER = -1e30


def mxu(left, right, dims):
    return lax.dot_general(left, right, dims, preferred_element_type=F32)


def halves(value):
    high = value.astype(BF16)
    low = (value - high.astype(F32)).astype(BF16)
    return high, low


def split_rows(value):
    return jnp.concatenate(halves(value), axis=0)


def split_lanes(value):
    return jnp.concatenate(halves(value), axis=1)


def twice_rows(value):
    return jnp.concatenate([value, value], axis=0)


def twice_lanes(value):
    return jnp.concatenate([value, value], axis=1)


def running_decay(decay):
    tok = decay.shape[1]
    earlier = lax.broadcasted_iota(jnp.int32, (tok, tok), 0)
    later = lax.broadcasted_iota(jnp.int32, (tok, tok), 1)
    upto = (earlier <= later).astype(BF16)
    high, _ = halves(decay)
    middle, low = halves(decay - high.astype(F32))
    return mxu(
        jnp.concatenate([high, middle, low], axis=1),
        jnp.concatenate([upto, upto, upto], axis=0),
        NN,
    )


def last_lane(running):
    return jnp.broadcast_to(running[:, running.shape[1] - 1 :], running.shape)


def columns(rows):
    count, tok = rows.shape
    if count < tok:
        rows = jnp.concatenate([rows, jnp.zeros((tok - count, tok), rows.dtype)], axis=0)
    return rows.T


def half_first(rows, core):
    half = rows.shape[0] // 2
    swapped = jnp.concatenate([rows[half:], rows[:half]], axis=0)
    return jnp.where(core == 0, rows, swapped)


def lane_block(ref, head, width):
    return ref[:, pl.ds(pl.multiple_of(head * width, width), width)]


def take_half(rows, core, low, count):
    half = rows.shape[0] // 2
    return jnp.where(core == 0, rows[low : low + count], rows[half + low : half + low + count])


def outer_products(left, right, weight_column):
    turned = left.T
    return mxu(twice_lanes(turned), split_rows(right.astype(F32) * weight_column), NN)


def first_export_half(state, core, weight, query, key, value, cotangent, outs, ready):
    heads, tok = weight.shape
    dim = query.shape[1] // heads
    half = heads // 2
    spread = columns(half_first(weight, core))
    targets = [(out, row) for out in outs for row in range(out.shape[0] // dim)]

    def products(left, right):
        for index in range(half):
            head = core * half + index
            out, row = targets[index]
            out[pl.ds(row * dim, dim), :] = outer_products(
                lane_block(left, head, dim),
                lane_block(right, head, dim),
                spread[:, index : index + 1],
            )

    @pl.when(state)
    def _():
        ready(key, value)
        products(key, value)

    @pl.when(jnp.logical_not(state))
    def _():
        ready(query, cotangent)
        products(query, cotangent)


def first_weights(position, gain, decay):
    chip = position // 2
    cross = gain.shape[0] - 3
    running = decay[...]
    total = last_lane(running)
    weight = jnp.where(
        chip % 2 == 0,
        jnp.exp(total - running),
        jnp.where(chip == 1, gain[cross + 1], gain[cross + 2]) * jnp.exp(running),
    )
    return weight, total


def first_export_kernel(
    place, query, key, value, cotangent, gain, decay, *rest
):
    sends, kept, raw, sems = rest[:-8], rest[-8:-2], rest[-2], rest[-1]
    position = place[0]
    core = position % 2
    heads, tok = decay.shape
    half = heads // 2
    wide = query.shape[1] // 2
    state = position // 2 % 2 == 0
    sources = (query, key, value, cotangent)
    names = ("query", "key", "value", "cotangent")
    moves = {}
    for number, (name, source, target) in enumerate(zip(names, sources, kept)):
        for side in range(2):
            lanes = pl.ds(pl.multiple_of((1 - core if side == 0 else core) * wide, wide), wide)
            moves[name, side] = pltpu.make_async_copy(
                source.at[:, lanes], target.at[:, lanes], sems.at[2 * number + side]
            )
    small = [
        pltpu.make_async_copy(source, target, sems.at[8 + number])
        for number, (source, target) in enumerate(zip((gain, decay), (kept[4], raw)))
    ]
    for move in small:
        move.start()

    def start(*order):
        for side in range(2):
            for name in order:
                moves[name, side].start()

    @pl.when(state)
    def _():
        start("key", "value")
        start("query", "cotangent")

    @pl.when(jnp.logical_not(state))
    def _():
        start("query", "cotangent")
        start("key", "value")

    for move in small:
        move.wait()
    kept[5][...] = running_decay(raw[...])
    weight, total = first_weights(position, *kept[4:])
    sends[0][pl.ds(sends[0].shape[0] - heads, heads), :] = total

    def ready(left, right):
        for name, target in zip(names, kept):
            if target is left or target is right:
                moves[name, 0].wait()

    first_export_half(state, 1 - core, weight, *kept[:4], sends, ready)

    @pl.when(state)
    def _():
        for name in ("query", "cotangent"):
            moves[name, 0].wait()

    @pl.when(jnp.logical_not(state))
    def _():
        for name in ("key", "value"):
            moves[name, 0].wait()

    for name in names:
        moves[name, 1].wait()


def own_export_kernel(place, query, key, value, cotangent, gain, decay, after, keep, totals):
    position = place[0]
    weight, total = first_weights(position, gain, decay)
    totals[...] = total
    first_export_half(
        position // 2 % 2 == 0,
        position % 2,
        weight,
        query,
        key,
        value,
        cotangent,
        [keep],
        lambda left, right: None,
    )


def second_core(position):
    return jnp.bitwise_xor(position % 2, (position // 2 == 3).astype(jnp.int32))


def second_export_kernel(
    place, query, key, value, cotangent, gain, decay, keep1, first_got, after, *outs
):
    *sends, keep, bundle, factors = outs
    position = place[0]
    core = second_core(position)
    chip = position // 2
    heads, tok = decay.shape
    dim = query.shape[1] // heads
    half = heads // 2
    cross = gain.shape[0] - 3
    running = decay[...]
    lift = jnp.exp(running)
    fall = jnp.exp(last_lane(running) - running)
    state2 = chip == 1
    state0 = position % 2 == 0
    weight2 = jnp.where(state2, fall, jnp.where(chip == 2, gain[cross + 2], gain[cross + 1]) * lift)
    weight2 = jnp.where(chip == 0, 0.0, weight2)
    weight0 = jnp.where(state0, fall, gain[cross] * lift)
    spread = columns(jnp.concatenate([half_first(weight2, 1 - core), weight0], axis=0))
    own_total = last_lane(running)
    other_total = first_got[pl.ds(first_got.shape[0] - heads, heads), :]
    inner = (chip == 1) | (chip == 2)
    merged = (
        *pair_factors(position, own_total, other_total, chip == 1),
        jnp.where(inner, jnp.exp(own_total + other_total), 0.0),
    )
    for kind, rows in enumerate(merged):
        factors[kind * half : (kind + 1) * half, :] = half_first(rows, core)[:half]
    bundle[pl.ds(heads * dim, half * dim), :] = keep1[...]
    place_of = [(part, row) for part, send in enumerate(sends) for row in range(send.shape[0] // dim)]
    for index in range(heads):
        mine = index >= half
        head = (core if mine else 1 - core) * half + index % half
        q, k, v, o = (lane_block(ref, head, dim) for ref in (query, key, value, cotangent))
        second = outer_products(
            jnp.where(state2, k, q), jnp.where(state2, v, o), spread[:, index : index + 1]
        )
        if mine:
            keep[pl.ds(index % half * dim, dim), :] = second
            bundle[pl.ds((heads + index) * dim, dim), :] = second
        else:
            part, row = place_of[index]
            sends[part][pl.ds(row * dim, dim), :] = second
    for head in range(heads):
        lanes = slice(head * dim, (head + 1) * dim)
        q, k, v, o = (ref[:, lanes] for ref in (query, key, value, cotangent))
        bundle[pl.ds(head * dim, dim), :] = outer_products(
            jnp.where(state0, k, q),
            jnp.where(state0, v, o),
            spread[:, heads + head : heads + head + 1],
        )


def pair_factors(position, own_total, other_total, is_state):
    even = position % 2 == 0
    scale_own = is_state == even
    return (
        jnp.where(scale_own, jnp.exp(other_total), 1.0),
        jnp.where(scale_own, 1.0, jnp.exp(own_total)),
    )


def first_merge_kernel(low, last, place, totals, first_got, keep, got, *rest):
    out = rest[-1]
    position = place[0]
    chip = position // 2
    heads, dim = totals.shape[0], keep.shape[1]
    own_total = totals[...]
    other_total = first_got[pl.ds(first_got.shape[0] - heads, heads), :]
    count = got.shape[0] // dim
    factors = pair_factors(position, own_total, other_total, chip % 2 == 0)
    own_factor, other_factor = (take_half(rows, position % 2, low, count) for rows in factors)
    for index in range(count):
        rows = pl.ds(index * dim, dim)
        one = slice(index, index + 1)
        out[rows, :] = (
            own_factor[one] * keep[pl.ds((low + index) * dim, dim), :]
            + other_factor[one] * got[rows, :]
        )
    if last:
        out[pl.ds(count * dim, heads), :] = own_total + other_total


def second_merge_kernel(low, factors, keep, got, first, *rest):
    out = rest[-1]
    dim = keep.shape[1]
    half = keep.shape[0] // dim
    for index in range(out.shape[0] // dim):
        rows = pl.ds(index * dim, dim)
        own, other, earlier = (
            factors[kind * half + low + index : kind * half + low + index + 1, :] for kind in range(3)
        )
        out[rows, :] = (
            own * keep[pl.ds((low + index) * dim, dim), :]
            + other * got[rows, :]
            + earlier * first[rows, :]
        )


def lane_sums(value):
    ones = jnp.ones((2 * value.shape[1], value.shape[1]), BF16)
    return mxu(split_lanes(value), ones, NN)


def row_sums(value):
    ones = jnp.ones((16, 2 * value.shape[1]), BF16)
    return mxu(ones, split_lanes(value), NT)[:1]


def apply_state(left, right, state, weight, summed=lane_sums):
    high, low = halves(state)
    first = mxu(twice_lanes(left), jnp.concatenate([high, low], axis=0), NN)
    second = mxu(twice_lanes(right), jnp.concatenate([high, low], axis=1), NT)
    sums = summed(first * right.astype(F32))
    return weight * first, weight * second, sums


def local_kernel(low, mine, place, query, key, value, cotangent, gain, decay, *rest):
    acc_out, acc_query, acc_key, acc_value, gain_rows, decay_rows = rest[-6:]
    core = place[0] % 2
    side = core if mine else 1 - core
    heads, tok = decay.shape
    count = decay_rows.shape[0]
    dim = query.shape[1] // heads
    inner_levels = tok.bit_length()
    running = take_half(decay[...], side, low, count)
    gains = [take_half(gain[place_in], side, low, count) for place_in in range(inner_levels)]
    spread = columns(running)
    source = lax.broadcasted_iota(jnp.int32, (tok, tok), 0)
    target = lax.broadcasted_iota(jnp.int32, (tok, tok), 1)
    mixing = jnp.bitwise_xor(source, target)
    level = jnp.zeros((tok, tok), jnp.int32)
    for power in range(inner_levels - 1):
        level = level + (mixing >= 2**power).astype(jnp.int32)
    causal = source <= target
    level = jnp.where(causal, level, -1)
    gathered = jnp.zeros((tok, tok), F32)
    for index in range(count):
        lanes = slice(index * dim, (index + 1) * dim)
        one = slice(index, index + 1)
        head = side * (heads // 2) + low + index
        q, k, v, o = (lane_block(ref, head, dim) for ref in (query, key, value, cotangent))
        scores = mxu(k, q, NT)
        pulls = mxu(v, o, NT)
        fading = jnp.exp(jnp.where(causal, running[one] - spread[:, one], NEVER))
        weighting = jnp.zeros((tok, tok), F32)
        for place_in in range(inner_levels):
            weighting = jnp.where(level == place_in, gains[place_in][one], weighting)
        weighting = weighting * fading
        mixing_part = scores * weighting
        score_grad = pulls * weighting
        product = scores * pulls * fading
        flow = jnp.zeros((1, tok), F32)
        for place_in in range(inner_levels):
            found = jnp.sum(jnp.where(level == place_in, product, 0.0), axis=0, keepdims=True)
            gain_rows[place_in, one, :] = found
            if place_in > 0:
                flow = flow + gains[place_in][one] * found
        decay_rows[one, :] = flow
        left = jnp.where(level > 0, mixing_part * pulls, 0.0)
        gathered = jnp.where(target == index, lane_sums(left), gathered)
        high, low_part = halves(mixing_part)
        acc_out[:, lanes] = mxu(jnp.concatenate([high, low_part], axis=0), twice_rows(v), TN)
        acc_value[:, lanes] = mxu(jnp.concatenate([high, low_part], axis=1), twice_rows(o), NN)
        high, low_part = halves(score_grad)
        acc_query[:, lanes] = mxu(jnp.concatenate([high, low_part], axis=0), twice_rows(k), TN)
        acc_key[:, lanes] = mxu(jnp.concatenate([high, low_part], axis=1), twice_rows(q), NN)
    decay_rows[...] = decay_rows[...] - gathered.T[:count]


def use_rows(rows_out, uses, gathered, extra):
    turned = gathered.T
    count = extra.shape[0]
    decay_row = jnp.zeros((count, turned.shape[1]), F32)
    flow_row = extra
    for number, (forward, weight, lift) in enumerate(uses):
        sums = turned[number * count : (number + 1) * count]
        weighted = weight * sums
        decay_row = decay_row + jnp.where(forward, weighted, -weighted)
        flow_row = flow_row + jnp.where(forward, 0.0, weighted)
        rows_out[(2 + number) * count : (3 + number) * count, :] = lift * sums
    rows_out[:count, :] = decay_row
    rows_out[count : 2 * count, :] = flow_row


def first_use_kernel(
    low,
    mine,
    place,
    query,
    key,
    value,
    cotangent,
    gain,
    decay,
    first_got,
    pair_got,
    first,
    second,
    second_got,
    front,
    acc_out,
    acc_query,
    acc_key,
    acc_value,
    *rest,
):
    out_mixed, out_query, out_key, out_value, rows_out = rest[-5:]
    position = place[0]
    core = position % 2
    side = core if mine else 1 - core
    chip = position // 2
    heads, tok = decay.shape
    half = heads // 2
    dim = query.shape[1] // heads
    count = acc_out.shape[1] // dim
    cross = gain.shape[0] - 3
    running = decay[...]
    total = last_lane(running)
    other = first_got[pl.ds(first_got.shape[0] - heads, heads), :]
    odd = core == 1
    forward = chip != 0
    offset = jnp.where(forward == odd, other, 0.0)
    lift0 = jnp.exp(running)
    lift = jnp.exp(running + offset)
    fall0 = jnp.exp(total - running)
    weight0 = jnp.where(odd, gain[cross] * lift0, fall0)
    weight = jnp.where(
        forward,
        jnp.where(chip == 2, gain[cross + 2], gain[cross + 1]) * lift,
        jnp.exp(total - running + offset),
    )
    pair_flow = jnp.where(forward != odd, jnp.exp(total), 0.0)
    chip_flow = jnp.where((chip == 1) | (chip == 2), jnp.exp(total + other), 0.0)
    lift0, lift, weight0, weight, pair_flow, chip_flow = (
        take_half(rows, side, low, count)
        for rows in (jnp.where(odd, lift0, 0.0), lift, weight0, weight, pair_flow, chip_flow)
    )
    spread = columns(jnp.concatenate([weight0, weight], axis=0))
    lane = lax.broadcasted_iota(jnp.int32, (tok, tok), 1)
    gathered = jnp.zeros((tok, tok), F32)
    flows = []
    for index in range(count):
        lanes = slice(index * dim, (index + 1) * dim)
        rows = pl.ds(index * dim, dim)
        one = slice(index, index + 1)
        head = side * half + low + index
        q, k, v, o = (lane_block(ref, head, dim) for ref in (query, key, value, cotangent))
        level0 = front[pl.ds(pl.multiple_of(head * dim, dim), dim), :]
        pair1 = pair_got[rows, :] if mine else front[pl.ds((heads + low + index) * dim, dim), :]
        pair2_kept = front[pl.ds((heads + half + low + index) * dim, dim), :]
        pair2 = jnp.where((chip == 3) == mine, pair2_kept, second_got[rows, :])
        state = jnp.where(chip == 2, second[rows, :], first[rows, :])
        partner = jnp.where(odd, level0, jnp.where(chip == 1, pair1, pair2))
        flows.append(
            pair_flow[one] * jnp.sum(state * partner, axis=0, keepdims=True)
            + chip_flow[one] * jnp.sum(first[rows, :] * second[rows, :], axis=0, keepdims=True)
        )
        left0, right0, sums = apply_state(
            jnp.where(odd, q, k), jnp.where(odd, o, v), level0, spread[:, one]
        )
        gathered = jnp.where(lane == index, sums, gathered)
        left, right, sums = apply_state(
            jnp.where(forward, q, k),
            jnp.where(forward, o, v),
            state,
            spread[:, count + index : count + index + 1],
        )
        gathered = jnp.where(lane == count + index, sums, gathered)
        out_mixed[:, lanes] = (
            acc_out[:, lanes] + jnp.where(odd, left0, 0.0) + jnp.where(forward, left, 0.0)
        )
        out_query[:, lanes] = (
            acc_query[:, lanes] + jnp.where(odd, right0, 0.0) + jnp.where(forward, right, 0.0)
        )
        out_value[:, lanes] = (
            acc_value[:, lanes] + jnp.where(odd, 0.0, left0) + jnp.where(forward, 0.0, left)
        )
        out_key[:, lanes] = (
            acc_key[:, lanes] + jnp.where(odd, 0.0, right0) + jnp.where(forward, 0.0, right)
        )
    use_rows(
        rows_out,
        ((odd, weight0, lift0), (forward, weight, lift)),
        gathered,
        jnp.concatenate(flows, axis=0),
    )


def last_use_kernel(
    low,
    mine,
    parts,
    place,
    query,
    key,
    value,
    cotangent,
    gain,
    decay,
    first_got,
    pair_got,
    chip_total,
    second,
    third,
    front,
    acc_out,
    acc_query,
    acc_key,
    acc_value,
    *rest,
):
    ending = parts is not None
    if ending:
        *rest, grad_gain, grad_decay, staged, sems, gain_stage, decay_stage, end_sems = rest
    elif mine:
        *rest, rows_out = rest
    else:
        *rest, rows_out, staged, sems = rest
    outs, before = rest[-4:], rest[:4]
    if not mine:
        rest = rest[4:]
    position = place[0]
    core = position % 2
    side = core if mine else 1 - core
    chip = position // 2
    heads, tok = decay.shape
    half = heads // 2
    dim = query.shape[1] // heads
    count = acc_out.shape[1] // dim
    cross = gain.shape[0] - 3
    running = decay[...]
    total = last_lane(running)
    other = first_got[pl.ds(first_got.shape[0] - heads, heads), :]
    chip_rows = chip_total[pl.ds(chip_total.shape[0] - heads, heads), :]
    odd = core == 1
    forward = chip == 3
    chip_offset = jnp.where((chip == 0) | (chip == 3), chip_rows, 0.0)
    offset = jnp.where(forward == odd, other, 0.0) + chip_offset
    lift = jnp.exp(running + offset)
    weight = jnp.where(forward, gain[cross + 2] * lift, jnp.exp(total - running + offset))
    pair_flow = jnp.where(forward != odd, jnp.exp(total + chip_offset), 0.0)
    lift, weight, pair_flow = (
        take_half(rows, side, low, count) for rows in (lift, weight, pair_flow)
    )
    spread = columns(weight)
    lane = lax.broadcasted_iota(jnp.int32, (tok, tok), 1)
    gathered = jnp.zeros((tok, tok), F32)
    flows, summed = [], []
    copies = []
    if not mine:
        wide = before[0].shape[1]
        start = pl.multiple_of(core * half * dim + low * dim, dim)
        for number in range(4):
            copy = pltpu.make_async_copy(
                before[number], outs[number].at[:, pl.ds(start, wide)], sems.at[4 * count + number]
            )
            copy.start()
            copies.append(copy)
    if ending:
        early = gain.shape[0] - 2
        copies.append(
            pltpu.make_async_copy(
                gain_stage.at[pl.ds(0, early)], grad_gain.at[pl.ds(0, early)], end_sems.at[0]
            )
        )
        early_gains(parts, rest[:-4], core, gain_stage)
        copies[-1].start()
    for index in range(count):
        lanes = slice(index * dim, (index + 1) * dim)
        rows = pl.ds(index * dim, dim)
        one = slice(index, index + 1)
        head = side * half + low + index
        q, k, v, o = (lane_block(ref, head, dim) for ref in (query, key, value, cotangent))
        state = jnp.where(chip == 1, second[rows, :], third[rows, :])
        level0 = front[pl.ds(pl.multiple_of(head * dim, dim), dim), :]
        if mine:
            pair1 = pair_got[rows, :]
        else:
            pair1 = front[pl.ds((heads + low + index) * dim, dim), :]
        partner = jnp.where(odd, level0, pair1)
        flows.append(pair_flow[one] * jnp.sum(state * partner, axis=0, keepdims=True))
        left, right, sums = apply_state(
            jnp.where(forward, q, k),
            jnp.where(forward, o, v),
            state,
            spread[:, one],
            row_sums if ending else lane_sums,
        )
        if ending:
            summed.append(sums)
        else:
            gathered = jnp.where(lane == index, sums, gathered)
        results = (
            acc_out[:, lanes] + jnp.where(forward, left, 0.0),
            acc_query[:, lanes] + jnp.where(forward, right, 0.0),
            acc_key[:, lanes] + jnp.where(forward, 0.0, right),
            acc_value[:, lanes] + jnp.where(forward, 0.0, left),
        )
        for number, result in enumerate(results):
            if mine:
                outs[number][:, lanes] = result.astype(BF16)
                continue
            staged[number, :, lanes] = result.astype(BF16)
            copy = pltpu.make_async_copy(
                staged.at[number, :, pl.ds(index * dim, dim)],
                outs[number].at[:, pl.ds(pl.multiple_of(head * dim, dim), dim)],
                sems.at[number * count + index],
            )
            copy.start()
            copies.append(copy)
    extra = jnp.concatenate(flows, axis=0)
    if not ending:
        use_rows(rows_out, ((forward, weight, lift),), gathered, extra)
    else:
        sums = jnp.concatenate(summed, axis=0)
        weighted = weight * sums
        own_rows = (
            jnp.where(forward, weighted, -weighted),
            extra + jnp.where(forward, 0.0, weighted),
            lift * sums,
        )
        finish(parts, rest[:-4], own_rows, core, chip, gain_stage, decay_stage)
        for copy in (
            pltpu.make_async_copy(
                gain_stage.at[pl.ds(early, 2)], grad_gain.at[pl.ds(early, 2)], end_sems.at[1]
            ),
            pltpu.make_async_copy(decay_stage, grad_decay, end_sems.at[2]),
        ):
            copy.start()
            copies.append(copy)
    for copy in copies:
        copy.wait()


def natural(pieces, core):
    return half_first(jnp.concatenate([*pieces[::2], *pieces[1::2]], axis=0), core)


def of_kind(counts, refs, number):
    return [
        ref[number * counts[at // 2] : (number + 1) * counts[at // 2], :]
        for at, ref in enumerate(refs)
    ]


def early_gains(counts, refs, core, grad_gain):
    levels = grad_gain.shape[0]
    groups = 2 * len(counts)
    for place_in in range(levels - 3):
        grad_gain[place_in] = natural([ref[place_in] for ref in refs[:groups]], core)
    first_rows = refs[2 * groups : 3 * groups]
    grad_gain[levels - 3] = natural(of_kind(counts, first_rows, 2), core)


def finish(counts, refs, own_rows, core, chip, grad_gain, grad_decay):
    levels, heads, tok = grad_gain.shape
    groups = 2 * len(counts)
    decay_rows, first_rows = refs[groups : 2 * groups], refs[2 * groups : 3 * groups]
    last_rows = refs[3 * groups : 4 * groups - 1]

    def last(number):
        return natural(of_kind(counts, last_rows, number) + [own_rows[number]], core)

    first, second = natural(of_kind(counts, first_rows, 3), core), last(2)
    grad_gain[levels - 2] = jnp.where(chip % 2 == 1, first, 0.0)
    grad_gain[levels - 1] = jnp.where(chip == 2, first, jnp.where(chip == 3, second, 0.0))
    own = natural([ref[...] for ref in decay_rows], core)
    own = own + natural(of_kind(counts, first_rows, 0), core) + last(0)
    later = natural(of_kind(counts, first_rows, 1), core) + last(1)
    upper = lax.broadcasted_iota(jnp.int32, (tok, tok), 0)
    lower = lax.broadcasted_iota(jnp.int32, (tok, tok), 1)
    from_here = (upper >= lower).astype(BF16)
    sums = jnp.concatenate([twice_rows(from_here), jnp.ones((2 * tok, tok), BF16)], axis=0)
    grad_decay[...] = mxu(
        jnp.concatenate([split_lanes(own), split_lanes(later)], axis=1), sums, NN
    )


def after(value, *others):
    return lax.optimization_barrier((value, *others))[0]


def sds(*shape, dtype=F32):
    return jax.ShapeDtypeStruct(shape, dtype)


FIRST_LIMIT = 24


def params(mebibytes=24):
    return pltpu.CompilerParams(vmem_limit_bytes=mebibytes * 1024 * 1024)


SCALAR = pl.BlockSpec(memory_space=pltpu.SMEM)
ANYWHERE = pl.BlockSpec(memory_space=pl.ANY)
IN_HBM = pl.BlockSpec(memory_space=pltpu.HBM)
RATE_FIRST = 16
RATE_SECOND = 0.001
RATE_LOCAL = ((.01,.01),(16,1))
RATE_USE = ((4,4),(4,4))
RATE_LAST = ((16,4),(4,4))
RATE_MERGE = (4,4)


def cost(microseconds, rate=16):
    return pl.CostEstimate(flops=int(microseconds * rate * 10**9), bytes_accessed=1, transcendentals=0)


def chunk_heads(half):
    return (half // 2, half - half // 2)


def line_device(queries, keys_in, value_input, level_gain, decay_log, out_grad):
    heads, tok = decay_log.shape
    dim = queries.shape[1] // heads
    half = heads // 2
    counts = chunk_heads(half)
    parts = range(len(counts))
    lows = [sum(counts[:part]) for part in parts]
    inner = tok.bit_length()
    place = lax.axis_index("ctx").astype(jnp.int32).reshape(1)
    tokens = (queries, keys_in, value_input, out_grad)
    inputs = (place, *tokens, level_gain, decay_log)
    core_swap = [(at, at ^ 1) for at in range(8)]
    side_swap = [(at, at ^ 2) for at in range(8)]
    middle_swap = [(0, 1), (1, 0), (2, 4), (4, 2), (3, 5), (5, 3), (6, 7), (7, 6)]

    def swap(block, route):
        return lax.ppermute(block, "ctx", route)

    def call(kernel, out_shape, operands, unread=(), spent=None, name=None, **options):
        return pl.pallas_call(
            kernel,
            out_shape=out_shape,
            in_specs=[SCALAR] + [pl.BlockSpec()] * (len(operands) - 1) + [ANYWHERE] * len(unread),
            compiler_params=params(),
            cost_estimate=spent,
            name=name,
            **options,
        )(*operands, *unread)

    found = pl.pallas_call(
        first_export_kernel,
        out_shape=tuple(
            pltpu.VMEM((count * dim + (0 if part else heads), dim), F32)
            for part, count in enumerate(counts)
        )
        + tuple(pltpu.VMEM(array.shape, array.dtype) for array in inputs[1:]),
        in_specs=[SCALAR] + [IN_HBM] * 6,
        scratch_shapes=[pltpu.VMEM((heads, tok), F32), pltpu.SemaphoreType.DMA((10,))],
        compiler_params=params(),
        cost_estimate=cost(2),
        name="first_exports",
    )(place, *(pltpu.with_memory_space_constraint(array, pltpu.HBM) for array in inputs[1:]))
    send1, kept = found[: len(counts)], found[len(counts) :]
    inputs = (place, *kept)
    got1 = [swap(block, core_swap) for block in send1]
    keep1, totals = call(
        own_export_kernel,
        (sds(half * dim, dim), sds(heads, tok)),
        inputs,
        (send1[0],),
        cost(0.8, RATE_FIRST),
        "own_exports",
    )

    def first_merge(part, *unread):
        return call(
            functools.partial(first_merge_kernel, lows[part], part == parts[-1]),
            sds(counts[part] * dim + (heads if part == parts[-1] else 0), dim),
            (place, totals, got1[0], keep1, got1[part]),
            unread,
            cost(0.2, RATE_FIRST),
            "first_merge",
        )

    first_sent = [first_merge(0)]
    first = [swap(first_sent[0], side_swap)]

    local_done = {}

    def local(part, mine, *unread):
        count = counts[part]
        local_done[part, mine] = call(
            functools.partial(local_kernel, lows[part], mine),
            (sds(tok, count * dim),) * 4 + (sds(inner, count, tok), sds(count, tok)),
            inputs,
            unread,
            cost(0.4 * count, RATE_LOCAL[part][not mine]),
            "local",
        )
        return local_done[part, mine][-1]

    done = first_sent[-1]
    *send2, keep2, bundle, factors = call(
        second_export_kernel,
        tuple(sds(count * dim, dim) for count in counts)
        + (sds(half * dim, dim), sds(4 * half * dim, dim), sds(3 * half, tok)),
        (*inputs, keep1, got1[0]),
        (done,),
        cost(1.6, RATE_SECOND),
        "second_exports",
    )
    got2 = [swap(block, core_swap) for block in send2]

    def second_merge(part, *unread):
        return pl.pallas_call(
            functools.partial(second_merge_kernel, lows[part]),
            out_shape=sds(counts[part] * dim, dim),
            in_specs=[pl.BlockSpec()] * 4 + [ANYWHERE] * len(unread),
            compiler_params=params(),
            cost_estimate=cost(0.3, RATE_MERGE[part]),
            name="second_merge",
        )(factors, keep2, got2[part], first[part], *unread)

    done = local(0, True, keep2)
    first_sent.append(first_merge(1, done))
    first.append(swap(first_sent[1], side_swap))
    done = local(0, False, done)
    sent = [second_merge(0, done, *got2[1:])]
    done = local(1, True, sent[0])
    done = local(1, False, done)
    sent.append(second_merge(1, done))
    front = swap(bundle, core_swap)
    second = [swap(block, middle_swap) for block in sent]
    third = [swap(second[0], side_swap)]
    second_over = [swap(second[0], core_swap)]
    done = second[0]

    used = {}

    def first_use(part, mine, *unread):
        count = counts[part]
        used[part, mine] = call(
            functools.partial(first_use_kernel, lows[part], mine),
            (sds(tok, count * dim),) * 4 + (sds(4 * count, tok),),
            (
                *inputs,
                got1[0],
                got1[part],
                (first if mine else first_over)[part],
                (second if mine else second_over)[part],
                got2[part],
                front,
                *local_done[part, mine][:4],
            ),
            unread,
            cost(0.3 * count, RATE_USE[part][not mine]),
            "first_use",
        )
        return used[part, mine][-1]

    results = ()
    last_rows, held = [], {}

    def last_use(part, mine, ending=False):
        nonlocal results
        count = counts[part]
        operands = (
            *inputs,
            got1[0],
            got1[part],
            first[-1],
            (second if mine else second_over)[part],
            (third if mine else third_over)[part],
            front,
            *used[part, mine][:4],
        )
        order = [(at, side) for at in parts for side in (True, False)]
        rows = ()
        if ending:
            rows = (
                *(local_done[key][4] for key in order),
                *(local_done[key][5] for key in order),
                *(used[key][4] for key in order),
                *last_rows,
            )
        if mine:
            *found, last = call(
                functools.partial(last_use_kernel, lows[part], mine, None),
                (sds(tok, count * dim, dtype=BF16),) * 4 + (sds(3 * count, tok),),
                operands,
                spent=cost(0.15 * count, RATE_LAST[part][0]),
                name="last_use",
            )
            held[part] = found
            last_rows.append(last)
            return
        operands = (*operands, *held[part])
        before = len(operands) + len(rows)
        tail = (sds(*level_gain.shape), sds(heads, tok)) if ending else (sds(3 * count, tok),)
        ending_scratch = [
            pltpu.VMEM(level_gain.shape, F32),
            pltpu.VMEM((heads, tok), F32),
            pltpu.SemaphoreType.DMA((3,)),
        ]
        found = pl.pallas_call(
            functools.partial(last_use_kernel, lows[part], mine, counts if ending else None),
            out_shape=(sds(tok, heads * dim, dtype=BF16),) * 4 + tail,
            in_specs=[SCALAR] + [pl.BlockSpec()] * (before - 1) + [ANYWHERE] * len(results),
            out_specs=(ANYWHERE,) * 4 + (ANYWHERE if ending else pl.BlockSpec(),) * len(tail),
            input_output_aliases={before + at: at for at in range(len(results))},
            scratch_shapes=[
                pltpu.VMEM((4, tok, count * dim), BF16),
                pltpu.SemaphoreType.DMA((4 * count + 4,)),
            ]
            + ending_scratch * ending,
            compiler_params=params(),
            cost_estimate=cost(0.25 * count, RATE_LAST[part][1]),
            name="last_use",
        )(*operands, *rows, *results)
        results = found[:4]
        last_rows.extend(found[4:])

    first_over = [swap(after(first[0], sent[0]), core_swap)]
    done = first_use(0, True, done, first_over[0])
    done = first_use(0, False, done)
    second[1] = after(second[1], done)
    third.append(swap(second[1], side_swap))
    second_over.append(swap(second[1], core_swap))
    first_over.append(swap(after(first[1], second[1]), core_swap))
    done = first_use(1, True, done)
    done = first_use(1, False, done)
    third_over = [swap(after(third[0], done), core_swap)]
    last_use(0, True)
    last_use(0, False)
    third_over.append(swap(after(third[1], done, last_rows[-1]), core_swap))
    last_use(1, True)
    last_use(1, False, ending=True)
    return (*results, *last_rows[-2:])


def solution(mesh):
    placed = (
        P(("seq", "ctx"), None),
        P(("seq", "ctx"), None),
        P(("seq", "ctx"), None),
        P(None, None, ("seq", "ctx")),
        P(None, ("seq", "ctx")),
        P(("seq", "ctx"), None),
    )
    return jax.shard_map(
        line_device if mesh.shape["ctx"] == 8 else per_device,
        mesh=mesh,
        in_specs=placed,
        out_specs=(
            P(("seq", "ctx"), None),
            P(("seq", "ctx"), None),
            P(("seq", "ctx"), None),
            P(("seq", "ctx"), None),
            P(None, None, ("seq", "ctx")),
            P(None, ("seq", "ctx")),
        ),
        check_vma=False,
    )
```

```python
import functools

import jax
import jax.numpy as jnp
from jax import lax
from jax.experimental import pallas as pl
from jax.experimental.pallas import tpu as pltpu
from jax.sharding import PartitionSpec as P

TOP_ACCURACY = lax.Precision.HIGHEST


def from_partner(block, axis, distance):
    count = lax.axis_size(axis)
    route = []
    for low in range(count):
        high = low | 1 << distance
        if high != low and high < count:
            route += [(low, high), (high, low)]
    return lax.ppermute(block, axis, route)


def passed_along(value, axis, steps):
    count = lax.axis_size(axis)
    first, last = (max(0, -steps), min(count, count - steps))
    return lax.ppermute(value, axis, [(source, source + steps) for source in range(first, last)])


def level_table(tok, lvl_in):
    places = jnp.arange(tok, dtype=jnp.int32)
    mixing = jnp.bitwise_xor(places[:, None], places[None, :])
    table = jnp.zeros((tok, tok), jnp.int32)
    for power in range(lvl_in):
        table = table + (mixing >= 2**power).astype(jnp.int32)
    return table


def block_front(keys_h, value_rows_head, decay):
    running = jnp.cumsum(decay, axis=1)
    total_sum = running[:, -1]
    scaled_result = keys_h * jnp.exp(total_sum[:, None] - running)[:, :, None]
    return (
        jnp.einsum("ybu,ybe->yue", scaled_result, value_rows_head, precision=TOP_ACCURACY),
        total_sum,
    )


def block_output(queries_h, keys_h, value_rows_head, gain, decay, buckets):
    tok = queries_h.shape[1]
    lvl_in = tok.bit_length() - 1
    running = jnp.cumsum(decay, axis=1)
    places = jnp.arange(tok, dtype=jnp.int32)
    causal = places[:, None] >= places[None, :]
    spread_gap = jnp.where(causal[None], running[:, :, None] - running[:, None, :], 0.0)
    fading = jnp.where(causal[None], jnp.exp(spread_gap), 0.0)
    table = level_table(tok, lvl_in)
    picks = (table[None] == jnp.arange(lvl_in + 1, dtype=jnp.int32)[:, None, None]).astype(
        jnp.float32
    )
    weighting = jnp.einsum("lij,lhi->hij", picks, gain[: lvl_in + 1], precision=TOP_ACCURACY)
    scores = jnp.einsum("hik,hjk->hij", queries_h, keys_h, precision=TOP_ACCURACY)
    result = jnp.einsum(
        "hij,hjv->hiv", scores * weighting * fading, value_rows_head, precision=TOP_ACCURACY
    )
    lifted = queries_h * jnp.exp(running)[:, :, None]
    reach = gain[lvl_in + 1 :][:, :, :, None] * lifted[None]
    return result + jnp.einsum("jhik,jhkv->hiv", reach, buckets, precision=TOP_ACCURACY)


def merge_step(own_total, own_state, offset, other_total, other_state, is_upper):
    bucket = jnp.where(is_upper, jnp.exp(offset)[:, None, None] * other_state, 0.0)
    low_state = jnp.where(is_upper, other_state, own_state)
    high_state = jnp.where(is_upper, own_state, other_state)
    high_total = jnp.where(is_upper, own_total, other_total)
    merged = jnp.exp(high_total)[:, None, None] * low_state + high_state
    new_offset = offset + jnp.where(is_upper, other_total, 0.0)
    return (own_total + other_total, merged, new_offset, bucket)


def partner_grads(
    own_total, own_state, offset, other_total, g_total, g_state, g_offset, g_bucket, is_upper
):
    factor = jnp.exp(jnp.where(is_upper, own_total, other_total))
    d_other_state = jnp.where(
        is_upper,
        factor[:, None, None] * g_state + jnp.exp(offset)[:, None, None] * g_bucket,
        g_state,
    )
    lower_term = factor * jnp.sum(g_state * own_state, axis=(1, 2))
    d_other_total = g_total + jnp.where(is_upper, g_offset, lower_term)
    return (d_other_total, d_other_state)


def own_grads(
    own_total, offset, other_total, other_state, g_total, g_state, g_offset, g_bucket, is_upper
):
    factor = jnp.exp(jnp.where(is_upper, own_total, other_total))
    d_own_state = jnp.where(is_upper, g_state, factor[:, None, None] * g_state)
    upper_total = factor * jnp.sum(g_state * other_state, axis=(1, 2))
    d_own_total = g_total + jnp.where(is_upper, upper_total, 0.0)
    upper_offset = jnp.exp(offset) * jnp.sum(g_bucket * other_state, axis=(1, 2))
    d_offset = g_offset + jnp.where(is_upper, upper_offset, 0.0)
    return (d_own_total, d_own_state, d_offset)


def to_heads(block, heads):
    tokens, width = block.shape
    return block.reshape(tokens, heads, width // heads).transpose(1, 0, 2).astype(jnp.float32)


def from_heads(block):
    heads, tokens, head_dim = block.shape
    return block.transpose(1, 0, 2).reshape(tokens, heads * head_dim)


def per_device(queries, keys_in, value_input, level_gain, decay_log, out_grad):
    heads = decay_log.shape[0]
    query_h = to_heads(queries, heads)
    key_h = to_heads(keys_in, heads)
    value_h = to_heads(value_input, heads)
    cotangent = to_heads(out_grad, heads)
    count = lax.axis_size("ctx")
    depth = count.bit_length() - 1
    position = lax.axis_index("ctx")
    (state, total_sum), front_back = jax.vjp(block_front, key_h, value_h, decay_log)
    own_total = total_sum
    own_state = state
    offset = jnp.zeros_like(total_sum)
    saved = []
    found = []
    top_other = state
    for bit in range(depth):
        other_total, other_state = from_partner((own_total, own_state), "ctx", bit)
        is_upper = jnp.right_shift(position, bit) % 2 == 1
        saved.append((own_total, own_state, offset, other_total))
        if bit == depth - 1:
            top_other = other_state
        own_total, own_state, offset, bucket = merge_step(
            own_total, own_state, offset, other_total, other_state, is_upper
        )
        found.append(bucket)
    buckets = jnp.stack(found)
    mixed, out_back = jax.vjp(block_output, query_h, key_h, value_h, level_gain, decay_log, buckets)
    grad_query, grad_key, grad_value, grad_gain, grad_decay, bucket_gradient = out_back(cotangent)
    grad_total = jnp.zeros_like(total_sum)
    grad_state = jnp.zeros_like(state)
    grad_offset = jnp.zeros_like(total_sum)
    for bit in reversed(range(depth)):
        is_upper = jnp.right_shift(position, bit) % 2 == 1
        level_total, level_state, level_offset, level_other_total = saved[bit]
        d_other_total, d_other_state = partner_grads(
            level_total,
            level_state,
            level_offset,
            level_other_total,
            grad_total,
            grad_state,
            grad_offset,
            bucket_gradient[bit],
            is_upper,
        )
        if bit == depth - 1:
            back_total, back_state = passed_along(
                (d_other_total, d_other_state), "ctx", -(count // 2)
            )
            partner_state = top_other
        else:
            back_total, back_state, partner_state = from_partner(
                (d_other_total, d_other_state, level_state), "ctx", bit
            )
        d_own_total, d_own_state, d_offset = own_grads(
            level_total,
            level_offset,
            level_other_total,
            partner_state,
            grad_total,
            grad_state,
            grad_offset,
            bucket_gradient[bit],
            is_upper,
        )
        grad_total = d_own_total + back_total
        grad_state = d_own_state + back_state
        grad_offset = d_offset
    key_more, value_more, decay_more = front_back((grad_state, grad_total))
    return (
        from_heads(mixed).astype(jnp.bfloat16),
        from_heads(grad_query).astype(jnp.bfloat16),
        from_heads(grad_key + key_more).astype(jnp.bfloat16),
        from_heads(grad_value + value_more).astype(jnp.bfloat16),
        grad_gain,
        grad_decay + decay_more,
    )


F32 = jnp.float32
BF16 = jnp.bfloat16
NT = (((1,), (1,)), ((), ()))
TN = (((0,), (0,)), ((), ()))
NN = (((1,), (0,)), ((), ()))
NEVER = -1e30


def mxu(left, right, dims):
    return lax.dot_general(left, right, dims, preferred_element_type=F32)


def halves(value):
    high = value.astype(BF16)
    low = (value - high.astype(F32)).astype(BF16)
    return high, low


def split_rows(value):
    return jnp.concatenate(halves(value), axis=0)


def split_lanes(value):
    return jnp.concatenate(halves(value), axis=1)


def twice_rows(value):
    return jnp.concatenate([value, value], axis=0)


def twice_lanes(value):
    return jnp.concatenate([value, value], axis=1)


def running_decay(decay):
    tok = decay.shape[1]
    earlier = lax.broadcasted_iota(jnp.int32, (tok, tok), 0)
    later = lax.broadcasted_iota(jnp.int32, (tok, tok), 1)
    upto = (earlier <= later).astype(BF16)
    high, _ = halves(decay)
    middle, low = halves(decay - high.astype(F32))
    return mxu(
        jnp.concatenate([high, middle, low], axis=1),
        jnp.concatenate([upto, upto, upto], axis=0),
        NN,
    )


def last_lane(running):
    return jnp.broadcast_to(running[:, running.shape[1] - 1 :], running.shape)


def columns(rows):
    count, tok = rows.shape
    if count < tok:
        rows = jnp.concatenate([rows, jnp.zeros((tok - count, tok), rows.dtype)], axis=0)
    return rows.T


def half_first(rows, core):
    half = rows.shape[0] // 2
    swapped = jnp.concatenate([rows[half:], rows[:half]], axis=0)
    return jnp.where(core == 0, rows, swapped)


def lane_block(ref, head, width):
    return ref[:, pl.ds(pl.multiple_of(head * width, width), width)]


def take_half(rows, core, low, count):
    half = rows.shape[0] // 2
    return jnp.where(core == 0, rows[low : low + count], rows[half + low : half + low + count])


def outer_products(left, right, weight_column):
    turned = left.T
    return mxu(twice_lanes(turned), split_rows(right.astype(F32) * weight_column), NN)


def first_export_half(state, core, weight, query, key, value, cotangent, outs, ready):
    heads, tok = weight.shape
    dim = query.shape[1] // heads
    half = heads // 2
    spread = columns(half_first(weight, core))
    targets = [(out, row) for out in outs for row in range(out.shape[0] // dim)]

    def products(left, right):
        for index in range(half):
            head = core * half + index
            out, row = targets[index]
            out[pl.ds(row * dim, dim), :] = outer_products(
                lane_block(left, head, dim),
                lane_block(right, head, dim),
                spread[:, index : index + 1],
            )

    @pl.when(state)
    def _():
        ready(key, value)
        products(key, value)

    @pl.when(jnp.logical_not(state))
    def _():
        ready(query, cotangent)
        products(query, cotangent)


def first_weights(position, gain, decay):
    chip = position // 2
    cross = gain.shape[0] - 3
    running = decay[...]
    total = last_lane(running)
    weight = jnp.where(
        chip % 2 == 0,
        jnp.exp(total - running),
        jnp.where(chip == 1, gain[cross + 1], gain[cross + 2]) * jnp.exp(running),
    )
    return weight, total


def first_export_kernel(
    place, query, key, value, cotangent, gain, decay, *rest
):
    sends, kept, raw, sems = rest[:-8], rest[-8:-2], rest[-2], rest[-1]
    position = place[0]
    core = position % 2
    heads, tok = decay.shape
    half = heads // 2
    wide = query.shape[1] // 2
    state = position // 2 % 2 == 0
    sources = (query, key, value, cotangent)
    names = ("query", "key", "value", "cotangent")
    moves = {}
    for number, (name, source, target) in enumerate(zip(names, sources, kept)):
        for side in range(2):
            lanes = pl.ds(pl.multiple_of((1 - core if side == 0 else core) * wide, wide), wide)
            moves[name, side] = pltpu.make_async_copy(
                source.at[:, lanes], target.at[:, lanes], sems.at[2 * number + side]
            )
    small = [
        pltpu.make_async_copy(source, target, sems.at[8 + number])
        for number, (source, target) in enumerate(zip((gain, decay), (kept[4], raw)))
    ]
    for move in small:
        move.start()

    def start(*order):
        for side in range(2):
            for name in order:
                moves[name, side].start()

    @pl.when(state)
    def _():
        start("key", "value")
        start("query", "cotangent")

    @pl.when(jnp.logical_not(state))
    def _():
        start("query", "cotangent")
        start("key", "value")

    for move in small:
        move.wait()
    kept[5][...] = running_decay(raw[...])
    weight, total = first_weights(position, *kept[4:])
    sends[0][pl.ds(sends[0].shape[0] - heads, heads), :] = total

    def ready(left, right):
        for name, target in zip(names, kept):
            if target is left or target is right:
                moves[name, 0].wait()

    first_export_half(state, 1 - core, weight, *kept[:4], sends, ready)

    @pl.when(state)
    def _():
        for name in ("query", "cotangent"):
            moves[name, 0].wait()

    @pl.when(jnp.logical_not(state))
    def _():
        for name in ("key", "value"):
            moves[name, 0].wait()

    for name in names:
        moves[name, 1].wait()


def own_export_kernel(place, query, key, value, cotangent, gain, decay, after, keep, totals):
    position = place[0]
    weight, total = first_weights(position, gain, decay)
    totals[...] = total
    first_export_half(
        position // 2 % 2 == 0,
        position % 2,
        weight,
        query,
        key,
        value,
        cotangent,
        [keep],
        lambda left, right: None,
    )


def second_core(position):
    return jnp.bitwise_xor(position % 2, (position // 2 == 3).astype(jnp.int32))


def second_export_kernel(
    place, query, key, value, cotangent, gain, decay, keep1, first_got, after, *outs
):
    *sends, keep, bundle, factors = outs
    position = place[0]
    core = second_core(position)
    chip = position // 2
    heads, tok = decay.shape
    dim = query.shape[1] // heads
    half = heads // 2
    cross = gain.shape[0] - 3
    running = decay[...]
    lift = jnp.exp(running)
    fall = jnp.exp(last_lane(running) - running)
    state2 = chip == 1
    state0 = position % 2 == 0
    weight2 = jnp.where(state2, fall, jnp.where(chip == 2, gain[cross + 2], gain[cross + 1]) * lift)
    weight2 = jnp.where(chip == 0, 0.0, weight2)
    weight0 = jnp.where(state0, fall, gain[cross] * lift)
    spread = columns(jnp.concatenate([half_first(weight2, 1 - core), weight0], axis=0))
    own_total = last_lane(running)
    other_total = first_got[pl.ds(first_got.shape[0] - heads, heads), :]
    inner = (chip == 1) | (chip == 2)
    merged = (
        *pair_factors(position, own_total, other_total, chip == 1),
        jnp.where(inner, jnp.exp(own_total + other_total), 0.0),
    )
    for kind, rows in enumerate(merged):
        factors[kind * half : (kind + 1) * half, :] = half_first(rows, core)[:half]
    bundle[pl.ds(heads * dim, half * dim), :] = keep1[...]
    place_of = [(part, row) for part, send in enumerate(sends) for row in range(send.shape[0] // dim)]
    for index in range(heads):
        mine = index >= half
        head = (core if mine else 1 - core) * half + index % half
        q, k, v, o = (lane_block(ref, head, dim) for ref in (query, key, value, cotangent))
        second = outer_products(
            jnp.where(state2, k, q), jnp.where(state2, v, o), spread[:, index : index + 1]
        )
        if mine:
            keep[pl.ds(index % half * dim, dim), :] = second
            bundle[pl.ds((heads + index) * dim, dim), :] = second
        else:
            part, row = place_of[index]
            sends[part][pl.ds(row * dim, dim), :] = second
    for head in range(heads):
        lanes = slice(head * dim, (head + 1) * dim)
        q, k, v, o = (ref[:, lanes] for ref in (query, key, value, cotangent))
        bundle[pl.ds(head * dim, dim), :] = outer_products(
            jnp.where(state0, k, q),
            jnp.where(state0, v, o),
            spread[:, heads + head : heads + head + 1],
        )


def pair_factors(position, own_total, other_total, is_state):
    even = position % 2 == 0
    scale_own = is_state == even
    return (
        jnp.where(scale_own, jnp.exp(other_total), 1.0),
        jnp.where(scale_own, 1.0, jnp.exp(own_total)),
    )


def first_merge_kernel(low, last, place, totals, first_got, keep, got, *rest):
    out = rest[-1]
    position = place[0]
    chip = position // 2
    heads, dim = totals.shape[0], keep.shape[1]
    own_total = totals[...]
    other_total = first_got[pl.ds(first_got.shape[0] - heads, heads), :]
    count = got.shape[0] // dim
    factors = pair_factors(position, own_total, other_total, chip % 2 == 0)
    own_factor, other_factor = (take_half(rows, position % 2, low, count) for rows in factors)
    for index in range(count):
        rows = pl.ds(index * dim, dim)
        one = slice(index, index + 1)
        out[rows, :] = (
            own_factor[one] * keep[pl.ds((low + index) * dim, dim), :]
            + other_factor[one] * got[rows, :]
        )
    if last:
        out[pl.ds(count * dim, heads), :] = own_total + other_total


def second_merge_kernel(low, factors, keep, got, first, *rest):
    out = rest[-1]
    dim = keep.shape[1]
    half = keep.shape[0] // dim
    for index in range(out.shape[0] // dim):
        rows = pl.ds(index * dim, dim)
        own, other, earlier = (
            factors[kind * half + low + index : kind * half + low + index + 1, :] for kind in range(3)
        )
        out[rows, :] = (
            own * keep[pl.ds((low + index) * dim, dim), :]
            + other * got[rows, :]
            + earlier * first[rows, :]
        )


def lane_sums(value):
    ones = jnp.ones((2 * value.shape[1], value.shape[1]), BF16)
    return mxu(split_lanes(value), ones, NN)


def row_sums(value):
    ones = jnp.ones((16, 2 * value.shape[1]), BF16)
    return mxu(ones, split_lanes(value), NT)[:1]


def apply_state(left, right, state, weight, summed=lane_sums):
    high, low = halves(state)
    first = mxu(twice_lanes(left), jnp.concatenate([high, low], axis=0), NN)
    second = mxu(twice_lanes(right), jnp.concatenate([high, low], axis=1), NT)
    sums = summed(first * right.astype(F32))
    return weight * first, weight * second, sums


def local_kernel(low, mine, place, query, key, value, cotangent, gain, decay, *rest):
    acc_out, acc_query, acc_key, acc_value, gain_rows, decay_rows = rest[-6:]
    core = place[0] % 2
    side = core if mine else 1 - core
    heads, tok = decay.shape
    count = decay_rows.shape[0]
    dim = query.shape[1] // heads
    inner_levels = tok.bit_length()
    running = take_half(decay[...], side, low, count)
    gains = [take_half(gain[place_in], side, low, count) for place_in in range(inner_levels)]
    spread = columns(running)
    source = lax.broadcasted_iota(jnp.int32, (tok, tok), 0)
    target = lax.broadcasted_iota(jnp.int32, (tok, tok), 1)
    mixing = jnp.bitwise_xor(source, target)
    level = jnp.zeros((tok, tok), jnp.int32)
    for power in range(inner_levels - 1):
        level = level + (mixing >= 2**power).astype(jnp.int32)
    causal = source <= target
    level = jnp.where(causal, level, -1)
    gathered = jnp.zeros((tok, tok), F32)
    for index in range(count):
        lanes = slice(index * dim, (index + 1) * dim)
        one = slice(index, index + 1)
        head = side * (heads // 2) + low + index
        q, k, v, o = (lane_block(ref, head, dim) for ref in (query, key, value, cotangent))
        scores = mxu(k, q, NT)
        pulls = mxu(v, o, NT)
        fading = jnp.exp(jnp.where(causal, running[one] - spread[:, one], NEVER))
        weighting = jnp.zeros((tok, tok), F32)
        for place_in in range(inner_levels):
            weighting = jnp.where(level == place_in, gains[place_in][one], weighting)
        weighting = weighting * fading
        mixing_part = scores * weighting
        score_grad = pulls * weighting
        product = scores * pulls * fading
        flow = jnp.zeros((1, tok), F32)
        for place_in in range(inner_levels):
            found = jnp.sum(jnp.where(level == place_in, product, 0.0), axis=0, keepdims=True)
            gain_rows[place_in, one, :] = found
            if place_in > 0:
                flow = flow + gains[place_in][one] * found
        decay_rows[one, :] = flow
        left = jnp.where(level > 0, mixing_part * pulls, 0.0)
        gathered = jnp.where(target == index, lane_sums(left), gathered)
        high, low_part = halves(mixing_part)
        acc_out[:, lanes] = mxu(jnp.concatenate([high, low_part], axis=0), twice_rows(v), TN)
        acc_value[:, lanes] = mxu(jnp.concatenate([high, low_part], axis=1), twice_rows(o), NN)
        high, low_part = halves(score_grad)
        acc_query[:, lanes] = mxu(jnp.concatenate([high, low_part], axis=0), twice_rows(k), TN)
        acc_key[:, lanes] = mxu(jnp.concatenate([high, low_part], axis=1), twice_rows(q), NN)
    decay_rows[...] = decay_rows[...] - gathered.T[:count]


def use_rows(rows_out, uses, gathered, extra):
    turned = gathered.T
    count = extra.shape[0]
    decay_row = jnp.zeros((count, turned.shape[1]), F32)
    flow_row = extra
    for number, (forward, weight, lift) in enumerate(uses):
        sums = turned[number * count : (number + 1) * count]
        weighted = weight * sums
        decay_row = decay_row + jnp.where(forward, weighted, -weighted)
        flow_row = flow_row + jnp.where(forward, 0.0, weighted)
        rows_out[(2 + number) * count : (3 + number) * count, :] = lift * sums
    rows_out[:count, :] = decay_row
    rows_out[count : 2 * count, :] = flow_row


def first_use_kernel(
    low,
    mine,
    place,
    query,
    key,
    value,
    cotangent,
    gain,
    decay,
    first_got,
    pair_got,
    first,
    second,
    second_got,
    front,
    acc_out,
    acc_query,
    acc_key,
    acc_value,
    *rest,
):
    out_mixed, out_query, out_key, out_value, rows_out = rest[-5:]
    position = place[0]
    core = position % 2
    side = core if mine else 1 - core
    chip = position // 2
    heads, tok = decay.shape
    half = heads // 2
    dim = query.shape[1] // heads
    count = acc_out.shape[1] // dim
    cross = gain.shape[0] - 3
    running = decay[...]
    total = last_lane(running)
    other = first_got[pl.ds(first_got.shape[0] - heads, heads), :]
    odd = core == 1
    forward = chip != 0
    offset = jnp.where(forward == odd, other, 0.0)
    lift0 = jnp.exp(running)
    lift = jnp.exp(running + offset)
    fall0 = jnp.exp(total - running)
    weight0 = jnp.where(odd, gain[cross] * lift0, fall0)
    weight = jnp.where(
        forward,
        jnp.where(chip == 2, gain[cross + 2], gain[cross + 1]) * lift,
        jnp.exp(total - running + offset),
    )
    pair_flow = jnp.where(forward != odd, jnp.exp(total), 0.0)
    chip_flow = jnp.where((chip == 1) | (chip == 2), jnp.exp(total + other), 0.0)
    lift0, lift, weight0, weight, pair_flow, chip_flow = (
        take_half(rows, side, low, count)
        for rows in (jnp.where(odd, lift0, 0.0), lift, weight0, weight, pair_flow, chip_flow)
    )
    spread = columns(jnp.concatenate([weight0, weight], axis=0))
    lane = lax.broadcasted_iota(jnp.int32, (tok, tok), 1)
    gathered = jnp.zeros((tok, tok), F32)
    flows = []
    for index in range(count):
        lanes = slice(index * dim, (index + 1) * dim)
        rows = pl.ds(index * dim, dim)
        one = slice(index, index + 1)
        head = side * half + low + index
        q, k, v, o = (lane_block(ref, head, dim) for ref in (query, key, value, cotangent))
        level0 = front[pl.ds(pl.multiple_of(head * dim, dim), dim), :]
        pair1 = pair_got[rows, :] if mine else front[pl.ds((heads + low + index) * dim, dim), :]
        pair2_kept = front[pl.ds((heads + half + low + index) * dim, dim), :]
        pair2 = jnp.where((chip == 3) == mine, pair2_kept, second_got[rows, :])
        state = jnp.where(chip == 2, second[rows, :], first[rows, :])
        partner = jnp.where(odd, level0, jnp.where(chip == 1, pair1, pair2))
        flows.append(
            pair_flow[one] * jnp.sum(state * partner, axis=0, keepdims=True)
            + chip_flow[one] * jnp.sum(first[rows, :] * second[rows, :], axis=0, keepdims=True)
        )
        left0, right0, sums = apply_state(
            jnp.where(odd, q, k), jnp.where(odd, o, v), level0, spread[:, one]
        )
        gathered = jnp.where(lane == index, sums, gathered)
        left, right, sums = apply_state(
            jnp.where(forward, q, k),
            jnp.where(forward, o, v),
            state,
            spread[:, count + index : count + index + 1],
        )
        gathered = jnp.where(lane == count + index, sums, gathered)
        out_mixed[:, lanes] = (
            acc_out[:, lanes] + jnp.where(odd, left0, 0.0) + jnp.where(forward, left, 0.0)
        )
        out_query[:, lanes] = (
            acc_query[:, lanes] + jnp.where(odd, right0, 0.0) + jnp.where(forward, right, 0.0)
        )
        out_value[:, lanes] = (
            acc_value[:, lanes] + jnp.where(odd, 0.0, left0) + jnp.where(forward, 0.0, left)
        )
        out_key[:, lanes] = (
            acc_key[:, lanes] + jnp.where(odd, 0.0, right0) + jnp.where(forward, 0.0, right)
        )
    use_rows(
        rows_out,
        ((odd, weight0, lift0), (forward, weight, lift)),
        gathered,
        jnp.concatenate(flows, axis=0),
    )


def last_use_kernel(
    low,
    mine,
    parts,
    place,
    query,
    key,
    value,
    cotangent,
    gain,
    decay,
    first_got,
    pair_got,
    chip_total,
    second,
    third,
    front,
    acc_out,
    acc_query,
    acc_key,
    acc_value,
    *rest,
):
    ending = parts is not None
    if ending:
        *rest, grad_gain, grad_decay, staged, sems, gain_stage, decay_stage, end_sems = rest
    elif mine:
        *rest, rows_out = rest
    else:
        *rest, rows_out, staged, sems = rest
    outs, before = rest[-4:], rest[:4]
    if not mine:
        rest = rest[4:]
    position = place[0]
    core = position % 2
    side = core if mine else 1 - core
    chip = position // 2
    heads, tok = decay.shape
    half = heads // 2
    dim = query.shape[1] // heads
    count = acc_out.shape[1] // dim
    cross = gain.shape[0] - 3
    running = decay[...]
    total = last_lane(running)
    other = first_got[pl.ds(first_got.shape[0] - heads, heads), :]
    chip_rows = chip_total[pl.ds(chip_total.shape[0] - heads, heads), :]
    odd = core == 1
    forward = chip == 3
    chip_offset = jnp.where((chip == 0) | (chip == 3), chip_rows, 0.0)
    offset = jnp.where(forward == odd, other, 0.0) + chip_offset
    lift = jnp.exp(running + offset)
    weight = jnp.where(forward, gain[cross + 2] * lift, jnp.exp(total - running + offset))
    pair_flow = jnp.where(forward != odd, jnp.exp(total + chip_offset), 0.0)
    lift, weight, pair_flow = (
        take_half(rows, side, low, count) for rows in (lift, weight, pair_flow)
    )
    spread = columns(weight)
    lane = lax.broadcasted_iota(jnp.int32, (tok, tok), 1)
    gathered = jnp.zeros((tok, tok), F32)
    flows, summed = [], []
    copies = []
    if not mine:
        wide = before[0].shape[1]
        start = pl.multiple_of(core * half * dim + low * dim, dim)
        for number in range(4):
            copy = pltpu.make_async_copy(
                before[number], outs[number].at[:, pl.ds(start, wide)], sems.at[4 * count + number]
            )
            copy.start()
            copies.append(copy)
    if ending:
        early = gain.shape[0] - 2
        copies.append(
            pltpu.make_async_copy(
                gain_stage.at[pl.ds(0, early)], grad_gain.at[pl.ds(0, early)], end_sems.at[0]
            )
        )
        early_gains(parts, rest[:-4], core, gain_stage)
        copies[-1].start()
    for index in range(count):
        lanes = slice(index * dim, (index + 1) * dim)
        rows = pl.ds(index * dim, dim)
        one = slice(index, index + 1)
        head = side * half + low + index
        q, k, v, o = (lane_block(ref, head, dim) for ref in (query, key, value, cotangent))
        state = jnp.where(chip == 1, second[rows, :], third[rows, :])
        level0 = front[pl.ds(pl.multiple_of(head * dim, dim), dim), :]
        if mine:
            pair1 = pair_got[rows, :]
        else:
            pair1 = front[pl.ds((heads + low + index) * dim, dim), :]
        partner = jnp.where(odd, level0, pair1)
        flows.append(pair_flow[one] * jnp.sum(state * partner, axis=0, keepdims=True))
        left, right, sums = apply_state(
            jnp.where(forward, q, k),
            jnp.where(forward, o, v),
            state,
            spread[:, one],
            row_sums if ending else lane_sums,
        )
        if ending:
            summed.append(sums)
        else:
            gathered = jnp.where(lane == index, sums, gathered)
        results = (
            acc_out[:, lanes] + jnp.where(forward, left, 0.0),
            acc_query[:, lanes] + jnp.where(forward, right, 0.0),
            acc_key[:, lanes] + jnp.where(forward, 0.0, right),
            acc_value[:, lanes] + jnp.where(forward, 0.0, left),
        )
        for number, result in enumerate(results):
            if mine:
                outs[number][:, lanes] = result.astype(BF16)
                continue
            staged[number, :, lanes] = result.astype(BF16)
            copy = pltpu.make_async_copy(
                staged.at[number, :, pl.ds(index * dim, dim)],
                outs[number].at[:, pl.ds(pl.multiple_of(head * dim, dim), dim)],
                sems.at[number * count + index],
            )
            copy.start()
            copies.append(copy)
    extra = jnp.concatenate(flows, axis=0)
    if not ending:
        use_rows(rows_out, ((forward, weight, lift),), gathered, extra)
    else:
        sums = jnp.concatenate(summed, axis=0)
        weighted = weight * sums
        own_rows = (
            jnp.where(forward, weighted, -weighted),
            extra + jnp.where(forward, 0.0, weighted),
            lift * sums,
        )
        finish(parts, rest[:-4], own_rows, core, chip, gain_stage, decay_stage)
        for copy in (
            pltpu.make_async_copy(
                gain_stage.at[pl.ds(early, 2)], grad_gain.at[pl.ds(early, 2)], end_sems.at[1]
            ),
            pltpu.make_async_copy(decay_stage, grad_decay, end_sems.at[2]),
        ):
            copy.start()
            copies.append(copy)
    for copy in copies:
        copy.wait()


def natural(pieces, core):
    return half_first(jnp.concatenate([*pieces[::2], *pieces[1::2]], axis=0), core)


def of_kind(counts, refs, number):
    return [
        ref[number * counts[at // 2] : (number + 1) * counts[at // 2], :]
        for at, ref in enumerate(refs)
    ]


def early_gains(counts, refs, core, grad_gain):
    levels = grad_gain.shape[0]
    groups = 2 * len(counts)
    for place_in in range(levels - 3):
        grad_gain[place_in] = natural([ref[place_in] for ref in refs[:groups]], core)
    first_rows = refs[2 * groups : 3 * groups]
    grad_gain[levels - 3] = natural(of_kind(counts, first_rows, 2), core)


def finish(counts, refs, own_rows, core, chip, grad_gain, grad_decay):
    levels, heads, tok = grad_gain.shape
    groups = 2 * len(counts)
    decay_rows, first_rows = refs[groups : 2 * groups], refs[2 * groups : 3 * groups]
    last_rows = refs[3 * groups : 4 * groups - 1]

    def last(number):
        return natural(of_kind(counts, last_rows, number) + [own_rows[number]], core)

    first, second = natural(of_kind(counts, first_rows, 3), core), last(2)
    grad_gain[levels - 2] = jnp.where(chip % 2 == 1, first, 0.0)
    grad_gain[levels - 1] = jnp.where(chip == 2, first, jnp.where(chip == 3, second, 0.0))
    own = natural([ref[...] for ref in decay_rows], core)
    own = own + natural(of_kind(counts, first_rows, 0), core) + last(0)
    later = natural(of_kind(counts, first_rows, 1), core) + last(1)
    upper = lax.broadcasted_iota(jnp.int32, (tok, tok), 0)
    lower = lax.broadcasted_iota(jnp.int32, (tok, tok), 1)
    from_here = (upper >= lower).astype(BF16)
    sums = jnp.concatenate([twice_rows(from_here), jnp.ones((2 * tok, tok), BF16)], axis=0)
    grad_decay[...] = mxu(
        jnp.concatenate([split_lanes(own), split_lanes(later)], axis=1), sums, NN
    )


def after(value, *others):
    return lax.optimization_barrier((value, *others))[0]


def sds(*shape, dtype=F32):
    return jax.ShapeDtypeStruct(shape, dtype)


FIRST_LIMIT = 24


def params(mebibytes=24):
    return pltpu.CompilerParams(vmem_limit_bytes=mebibytes * 1024 * 1024)


SCALAR = pl.BlockSpec(memory_space=pltpu.SMEM)
ANYWHERE = pl.BlockSpec(memory_space=pl.ANY)
IN_HBM = pl.BlockSpec(memory_space=pltpu.HBM)
RATE_FIRST = 16
RATE_SECOND = 0.001
RATE_LOCAL = ((.01,.01),(16,1))
RATE_USE = ((4,4),(4,4))
RATE_LAST = ((16,4),(4,4))
RATE_MERGE = (4,4)


def cost(microseconds, rate=16):
    return pl.CostEstimate(flops=int(microseconds * rate * 10**9), bytes_accessed=1, transcendentals=0)


def chunk_heads(half):
    return (half // 2, half - half // 2)


def line_device(queries, keys_in, value_input, level_gain, decay_log, out_grad):
    heads, tok = decay_log.shape
    dim = queries.shape[1] // heads
    half = heads // 2
    counts = chunk_heads(half)
    parts = range(len(counts))
    lows = [sum(counts[:part]) for part in parts]
    inner = tok.bit_length()
    place = lax.axis_index("ctx").astype(jnp.int32).reshape(1)
    tokens = (queries, keys_in, value_input, out_grad)
    inputs = (place, *tokens, level_gain, decay_log)
    core_swap = [(at, at ^ 1) for at in range(8)]
    side_swap = [(at, at ^ 2) for at in range(8)]
    middle_swap = [(0, 1), (1, 0), (2, 4), (4, 2), (3, 5), (5, 3), (6, 7), (7, 6)]

    def swap(block, route):
        return lax.ppermute(block, "ctx", route)

    def call(kernel, out_shape, operands, unread=(), spent=None, name=None, **options):
        return pl.pallas_call(
            kernel,
            out_shape=out_shape,
            in_specs=[SCALAR] + [pl.BlockSpec()] * (len(operands) - 1) + [ANYWHERE] * len(unread),
            compiler_params=params(),
            cost_estimate=spent,
            name=name,
            **options,
        )(*operands, *unread)

    found = pl.pallas_call(
        first_export_kernel,
        out_shape=tuple(
            pltpu.VMEM((count * dim + (0 if part else heads), dim), F32)
            for part, count in enumerate(counts)
        )
        + tuple(pltpu.VMEM(array.shape, array.dtype) for array in inputs[1:]),
        in_specs=[SCALAR] + [IN_HBM] * 6,
        scratch_shapes=[pltpu.VMEM((heads, tok), F32), pltpu.SemaphoreType.DMA((10,))],
        compiler_params=params(),
        cost_estimate=cost(2),
        name="first_exports",
    )(place, *(pltpu.with_memory_space_constraint(array, pltpu.HBM) for array in inputs[1:]))
    send1, kept = found[: len(counts)], found[len(counts) :]
    inputs = (place, *kept)
    got1 = [swap(block, core_swap) for block in send1]
    keep1, totals = call(
        own_export_kernel,
        (sds(half * dim, dim), sds(heads, tok)),
        inputs,
        (send1[0],),
        cost(0.8, RATE_FIRST),
        "own_exports",
    )

    def first_merge(part, *unread):
        return call(
            functools.partial(first_merge_kernel, lows[part], part == parts[-1]),
            sds(counts[part] * dim + (heads if part == parts[-1] else 0), dim),
            (place, totals, got1[0], keep1, got1[part]),
            unread,
            cost(0.2, RATE_FIRST),
            "first_merge",
        )

    first_sent = [first_merge(0)]
    first = [swap(first_sent[0], side_swap)]

    local_done = {}

    def local(part, mine, *unread):
        count = counts[part]
        local_done[part, mine] = call(
            functools.partial(local_kernel, lows[part], mine),
            (sds(tok, count * dim),) * 4 + (sds(inner, count, tok), sds(count, tok)),
            inputs,
            unread,
            cost(0.4 * count, RATE_LOCAL[part][not mine]),
            "local",
        )
        return local_done[part, mine][-1]

    done = first_sent[-1]
    *send2, keep2, bundle, factors = call(
        second_export_kernel,
        tuple(sds(count * dim, dim) for count in counts)
        + (sds(half * dim, dim), sds(4 * half * dim, dim), sds(3 * half, tok)),
        (*inputs, keep1, got1[0]),
        (done,),
        cost(1.6, RATE_SECOND),
        "second_exports",
    )
    got2 = [swap(block, core_swap) for block in send2]

    def second_merge(part, *unread):
        return pl.pallas_call(
            functools.partial(second_merge_kernel, lows[part]),
            out_shape=sds(counts[part] * dim, dim),
            in_specs=[pl.BlockSpec()] * 4 + [ANYWHERE] * len(unread),
            compiler_params=params(),
            cost_estimate=cost(0.3, RATE_MERGE[part]),
            name="second_merge",
        )(factors, keep2, got2[part], first[part], *unread)

    done = local(0, True, keep2)
    first_sent.append(first_merge(1, done))
    first.append(swap(first_sent[1], side_swap))
    done = local(0, False, done)
    sent = [second_merge(0, done, *got2[1:])]
    done = local(1, True, sent[0])
    done = local(1, False, done)
    sent.append(second_merge(1, done))
    front = swap(bundle, core_swap)
    second = [swap(block, middle_swap) for block in sent]
    third = [swap(second[0], side_swap)]
    done = second[0]

    used = {}

    def first_use(part, mine, *unread):
        count = counts[part]
        used[part, mine] = call(
            functools.partial(first_use_kernel, lows[part], mine),
            (sds(tok, count * dim),) * 4 + (sds(4 * count, tok),),
            (
                *inputs,
                got1[0],
                got1[part],
                (first if mine else first_over)[part],
                (second if mine else second_over)[part],
                got2[part],
                front,
                *local_done[part, mine][:4],
            ),
            unread,
            cost(0.3 * count, RATE_USE[part][not mine]),
            "first_use",
        )
        return used[part, mine][-1]

    results = ()
    last_rows, held = [], {}

    def last_use(part, mine, ending=False):
        nonlocal results
        count = counts[part]
        operands = (
            *inputs,
            got1[0],
            got1[part],
            first[-1],
            (second if mine else second_over)[part],
            (third if mine else third_over)[part],
            front,
            *used[part, mine][:4],
        )
        order = [(at, side) for at in parts for side in (True, False)]
        rows = ()
        if ending:
            rows = (
                *(local_done[key][4] for key in order),
                *(local_done[key][5] for key in order),
                *(used[key][4] for key in order),
                *last_rows,
            )
        if mine:
            *found, last = call(
                functools.partial(last_use_kernel, lows[part], mine, None),
                (sds(tok, count * dim, dtype=BF16),) * 4 + (sds(3 * count, tok),),
                operands,
                spent=cost(0.15 * count, RATE_LAST[part][0]),
                name="last_use",
            )
            held[part] = found
            last_rows.append(last)
            return
        operands = (*operands, *held[part])
        before = len(operands) + len(rows)
        tail = (sds(*level_gain.shape), sds(heads, tok)) if ending else (sds(3 * count, tok),)
        ending_scratch = [
            pltpu.VMEM(level_gain.shape, F32),
            pltpu.VMEM((heads, tok), F32),
            pltpu.SemaphoreType.DMA((3,)),
        ]
        found = pl.pallas_call(
            functools.partial(last_use_kernel, lows[part], mine, counts if ending else None),
            out_shape=(sds(tok, heads * dim, dtype=BF16),) * 4 + tail,
            in_specs=[SCALAR] + [pl.BlockSpec()] * (before - 1) + [ANYWHERE] * len(results),
            out_specs=(ANYWHERE,) * 4 + (ANYWHERE if ending else pl.BlockSpec(),) * len(tail),
            input_output_aliases={before + at: at for at in range(len(results))},
            scratch_shapes=[
                pltpu.VMEM((4, tok, count * dim), BF16),
                pltpu.SemaphoreType.DMA((4 * count + 4,)),
            ]
            + ending_scratch * ending,
            compiler_params=params(),
            cost_estimate=cost(0.25 * count, RATE_LAST[part][1]),
            name="last_use",
        )(*operands, *rows, *results)
        results = found[:4]
        last_rows.extend(found[4:])

    first_over = [swap(after(first[0], sent[0]), core_swap)]
    second_over = [swap(after(second[0], first_over[0]), core_swap)]
    done = first_use(0, True, done, first_over[0])
    done = first_use(0, False, done)
    second[1] = after(second[1], done)
    third.append(swap(second[1], side_swap))
    second_over.append(swap(second[1], core_swap))
    first_over.append(swap(after(first[1], second[1]), core_swap))
    done = first_use(1, True, done)
    done = first_use(1, False, done)
    third_over = [swap(after(third[0], done), core_swap)]
    last_use(0, True)
    last_use(0, False)
    third_over.append(swap(after(third[1], done, last_rows[-1]), core_swap))
    last_use(1, True)
    last_use(1, False, ending=True)
    return (*results, *last_rows[-2:])


def solution(mesh):
    placed = (
        P(("seq", "ctx"), None),
        P(("seq", "ctx"), None),
        P(("seq", "ctx"), None),
        P(None, None, ("seq", "ctx")),
        P(None, ("seq", "ctx")),
        P(("seq", "ctx"), None),
    )
    return jax.shard_map(
        line_device if mesh.shape["ctx"] == 8 else per_device,
        mesh=mesh,
        in_specs=placed,
        out_specs=(
            P(("seq", "ctx"), None),
            P(("seq", "ctx"), None),
            P(("seq", "ctx"), None),
            P(("seq", "ctx"), None),
            P(None, None, ("seq", "ctx")),
            P(None, ("seq", "ctx")),
        ),
        check_vma=False,
    )
```
